32 devices in a mesh: section: 4 (over z), tm: 4 (over y, x), batch: 2 (over core).
Axes of the slice: x: 2, y: 2, z: 4, core: 2. Of those that a mesh axis runs over, the one named last changes fastest.
Arguments:
- acts: bfloat16 [4, 4, 8, 6, 10240], P('section', 'batch', 'tm'), may hold values from -6 to 6
- cot: bfloat16 [4, 8, 6, 10240], P('batch', 'tm'), may hold values from -6 to 6
- spatial_weight: bfloat16 [4, 9, 64, 64], P('section'), may hold values from -0.25 to 0.25
- temporal_weight: bfloat16 [4, 3, 64, 64], P('section'), may hold values from -0.4375 to 0.4375
Outputs:
- grad_in: bfloat16 [4, 4, 8, 6, 10240], P('section', 'batch', 'tm')
- grad_spatial: float32 [4, 9, 64, 64], P('section')
- grad_temporal: float32 [4, 3, 64, 64], P('section')
The draws below stay inside these ranges and needn't reach their ends.
All inputs are finite; a program needn't handle non-finite values.
Results may differ from the reference program's by a relative error of at most 0.012.
Values may be sent and summed in bfloat16 or wider, within the bound.
A program may use at most 128 MiB of HBM per device.

```python
import jax
import jax.numpy as jnp

C = 64
W = 160
H = 6
TIME_DILATION = 2
SECTIONS = 4
SAMPLE_BINS = 8
SAMPLES = 4


def block_scale(own_key, extent, pieces, low, largest):
    gain = 1.0
    for dim, blocks in pieces:
        draws = jax.random.uniform(jax.random.fold_in(jax.random.fold_in(own_key, 6), dim), (blocks,), jnp.float32, low / len(pieces), largest / len(pieces))
        gain = gain * jnp.repeat(jnp.exp(draws), extent[dim] // blocks).reshape((-1,) + (1,) * (len(extent) - 1 - dim))
    return gain


def scatter_about(key, extent, deviation, most, split=(), held_as=jnp.bfloat16):
    array = jax.random.normal(key, extent, jnp.float32) * deviation
    if len(split) > 0:
        array = block_scale(key, extent, split, -0.22, 0.18) * array
    return jnp.clip(array, min=-most, max=most).astype(held_as)


def setup_inputs(seed: int = 0) -> dict:
    arg_keys = jax.random.split(jax.random.key(seed), 5)
    return {
        "acts": scatter_about(arg_keys[0], (SECTIONS, SAMPLES, SAMPLE_BINS, H, W * C), 1.0, 6.0, ((0, 4), (1, 2), (2, 4))),
        "cot": scatter_about(arg_keys[1], (SAMPLES, SAMPLE_BINS, H, W * C), 1.0, 6.0, ((0, 2), (1, 4))),
        "spatial_weight": scatter_about(arg_keys[2], (SECTIONS, 9, C, C), (9 * C) ** -0.5, 0.25, ((0, 4),)),
        "temporal_weight": scatter_about(arg_keys[3], (SECTIONS, 3, C, C), (3 * C) ** -0.5, 0.4375, ((0, 4),)),
    }


def split_pixels(a, chans):
    return a.reshape(a.shape[:-1] + (a.shape[-1] // chans, chans))


def spatial_fwd(x, ws):
    rows, width = x.shape[1], x.shape[2]
    chans = ws.shape[-1]
    padded = jnp.pad(x, ((0, 0), (1, 1), (chans, chans))).astype(jnp.float32)
    total = jnp.zeros(x.shape, jnp.float32)
    for i in range(3):
        for j in range(3):
            piece = split_pixels(padded[:, i:i + rows, j * chans:j * chans + width], chans)
            total = total + jnp.einsum("nrwc,cd->nrwd", piece, ws[3 * i + j].astype(jnp.float32)).reshape(x.shape)
    return total


def spatial_back(gz, x, ws):
    rows, width = x.shape[1], x.shape[2]
    chans = ws.shape[-1]
    xpad = jnp.pad(x, ((0, 0), (1, 1), (chans, chans))).astype(jnp.float32)
    gradient_padded = jnp.pad(gz, ((0, 0), (1, 1), (chans, chans))).astype(jnp.float32)
    gz_pix = split_pixels(gz.astype(jnp.float32), chans)
    total = jnp.zeros(x.shape, jnp.float32)
    grads = []
    for i in range(3):
        for j in range(3):
            gpiece = split_pixels(gradient_padded[:, 2 - i:2 - i + rows, (2 - j) * chans:(2 - j) * chans + width], chans)
            total = total + jnp.einsum("nrwd,cd->nrwc", gpiece, ws[3 * i + j].astype(jnp.float32)).reshape(x.shape)
            xpiece = split_pixels(xpad[:, i:i + rows, j * chans:j * chans + width], chans)
            grads.append(jnp.einsum("nrwc,nrwd->cd", xpiece, gz_pix))
    return total, jnp.stack(grads)


def reference(acts, cot, spatial_weight, temporal_weight):
    chans = spatial_weight.shape[-1]
    gradient_piece = cot
    outs_in, outs_sp, outs_tm = [], [], []
    for s in range(SECTIONS - 1, -1, -1):
        x = acts[s].reshape((SAMPLES * SAMPLE_BINS, H, W * C))
        z = spatial_fwd(x, spatial_weight[s])
        sig = jax.nn.sigmoid(z)
        h = (z * sig).astype(jnp.bfloat16).reshape(cot.shape)
        deriv = sig * (1.0 + z * (1.0 - sig))
        gradient_padded = jnp.pad(gradient_piece, ((0, 0), (TIME_DILATION, TIME_DILATION), (0, 0), (0, 0)))
        kernel_taps = [gradient_padded[:, 2 * TIME_DILATION:2 * TIME_DILATION + SAMPLE_BINS], gradient_piece, gradient_padded[:, 0:SAMPLE_BINS]]
        wt = temporal_weight[s].astype(jnp.float32)
        gh = jnp.zeros(cot.shape, jnp.float32)
        h_pix = split_pixels(h.astype(jnp.float32), chans)
        tgrads = []
        for k in range(3):
            tap = split_pixels(kernel_taps[k].astype(jnp.float32), chans)
            gh = gh + jnp.einsum("ntrwd,cd->ntrwc", tap, wt[k]).reshape(cot.shape)
            tgrads.append(jnp.einsum("ntrwc,ntrwd->cd", h_pix, tap))
        gh = gh.astype(jnp.bfloat16).reshape(x.shape)
        gz = (gh.astype(jnp.float32) * deriv).astype(jnp.bfloat16)
        back, sgrads = spatial_back(gz, x, spatial_weight[s])
        gradient_piece = (gradient_piece.astype(jnp.float32).reshape(x.shape) + back).astype(jnp.bfloat16).reshape(cot.shape)
        outs_in.append(gradient_piece)
        outs_sp.append(sgrads)
        outs_tm.append(jnp.stack(tgrads))
    return (jnp.stack(outs_in[::-1]), jnp.stack(outs_sp[::-1]), jnp.stack(outs_tm[::-1]))
```

```python
import functools

import jax
import jax.numpy as jnp
from jax import lax
from jax.experimental import pallas as pl
from jax.experimental.pallas import tpu as pltpu
from jax.sharding import PartitionSpec as P

DILATION = 2
ROWS = 8
LANES = 128
HALO = 3
MESH = pl.DeviceIdType.MESH


def neighbours(x):
    none = jnp.zeros_like(x[:, :1])
    after = jnp.concatenate([x[:, 1:], none], axis=1)
    before = jnp.concatenate([none, x[:, :-1]], axis=1)
    lane = lax.broadcasted_iota(jnp.int32, x.shape, 3)
    return jnp.where(lane < LANES // 2, after, before)


def flat(x):
    return x.reshape(-1, x.shape[-1])


def mm(a, b, dims):
    return lax.dot_general(a, b, (dims, ((), ())), preferred_element_type=jnp.float32)


def taps_of(d, dt, chans):
    def block(a, r, i, b):
        at = i * LANES + b * chans
        return a[r * chans : (r + 1) * chans, at : at + chans]

    taps = []
    for i in range(3):
        taps.append(block(d, 0, i, 1) + block(d, 3, i, 0))
        taps.append(block(d, 0, i, 0) + block(d, 1, i, 1))
        taps.append(block(d, 1, i, 0) + block(d, 2, i, 1))
    for k in range(3):
        taps.append(block(dt, 0, k, 0) + block(dt, 1, k, 1))
    return taps


def set_weights(ws_ref, wt_ref, fwd, back, time):
    chans = ws_ref.shape[-1]
    zero = jnp.zeros((chans, chans), jnp.bfloat16)
    for i in range(3):
        a, b, c = [ws_ref[3 * i + j] for j in range(3)]
        at = slice(i * LANES, (i + 1) * LANES)
        rows = [[b, a], [c, b], [zero, c], [a, zero]]
        fwd[:, at] = jnp.concatenate([jnp.concatenate(v, axis=1) for v in rows], axis=0)
        at = slice(i * 2 * LANES, (i + 1) * 2 * LANES)
        rows = [[b, a, zero, c], [c, b, a, zero]]
        back[:, at] = jnp.concatenate([jnp.concatenate(v, axis=1) for v in rows], axis=0)
        at = slice(i * LANES, (i + 1) * LANES)
        rows = [[wt_ref[i], zero], [zero, wt_ref[i]]]
        time[:, at] = jnp.concatenate([jnp.concatenate(v, axis=1) for v in rows], axis=0)


def pack(frames, stage, c, tiles, line, flatten, skip):
    tm, size = stage.shape[0], stage.shape[2]
    rows, count = frames.shape[1], frames.shape[2]
    local = stage.shape[1] // frames.shape[0]
    pairs = count // local
    flatten[...] = frames[c // local].astype(jnp.float32).reshape(flatten.shape)
    for r in range(rows):
        at = r * count + c % local
        line[pl.ds(HALO * rows + r, pairs, stride=rows), :] = flatten[pl.ds(at, pairs, stride=local), :]
    for m in range(tm):
        at = (tiles * m + skip) * rows
        stage[m, c] = line[at : at + size, :].astype(jnp.bfloat16)


def spread(packed, loose, wide, rows, first, count):
    loose[...] = packed.astype(jnp.float32)
    for n in range(loose.shape[0]):
        for p in range(count):
            wide[n, first + p, 0:rows, :] = loose[n, rows * p : rows * (p + 1), :]


def kernel(
    sections, batches, tiles, acts, cot, ws_ref, wt_ref, out, spatial, temporal,
    x_stage, g_stage, x_buf, g_buf, r_buf, o_buf, home, fwd, back, time, acc, acc_t, ds,
    w_send, w_recv, w_piece, w_full,
    line, flatten, x_loose, g_loose, o_loose, x_wide, g_wide,
    x_sem, g_sem, z_sem, o_sem, w_sem, f_sem,
):
    tm = x_stage.shape[0]
    micro, frame_rows, count, _ = acts.shape
    chains = x_stage.shape[1]
    local = chains // micro
    width = count // local * LANES
    chans = ws_ref.shape[-1]
    pairs = x_wide.shape[1]
    tile_rows = o_buf.shape[2]
    group = tm * batches
    section, me, core = [lax.axis_index(a) for a in ("section", "tm", "batch")]
    rank = me * batches + core

    def member(e):
        other = lax.rem(rank + e, group)
        return other, (section, other // batches, lax.rem(other, batches))

    def peer(d):
        other = lax.rem(me + d, tm)
        return other, (section, other, core)

    barrier = pltpu.get_barrier_semaphore()
    for e in range(1, group):
        pl.semaphore_signal(barrier, inc=1, device_id=member(e)[1], device_id_type=MESH)

    @pl.when(section > 0)
    def _():
        pl.semaphore_signal(barrier, inc=1, device_id=(section - 1, me, core), device_id_type=MESH)

    @pl.when(section < sections - 1)
    def _():
        pl.semaphore_signal(barrier, inc=1, device_id=(section + 1, me, core), device_id_type=MESH)

    def copy(src, dst, sems, at, device):
        return pltpu.make_async_remote_copy(
            src_ref=src, dst_ref=dst, send_sem=sems.at[(0,) + at], recv_sem=sems.at[(1,) + at],
            device_id=device, device_id_type=MESH,
        )

    def x_copy(c, d):
        other, device = peer(d)
        return copy(x_stage.at[other, c], x_buf.at[c, me], x_sem, (c, d - 1), device)

    def g_copy(c, d):
        other, device = peer(d)
        return copy(g_stage.at[other, c], g_buf.at[c, me], g_sem, (c, d - 1), device)

    def z_copy(c):
        return copy(r_buf.at[c], g_buf.at[c], z_sem, (c,), (lax.max(section - 1, 0), me, core))

    def o_copy(c, d):
        other, device = peer(d)
        return copy(o_buf.at[c, other], home.at[c, me], o_sem, (c, d - 1), device)

    def w_copy(e):
        other, device = member(e)
        return copy(w_send.at[other], w_recv.at[rank], w_sem, (e - 1,), device)

    def f_copy(e):
        return copy(w_piece, w_full.at[rank], f_sem, (e - 1,), member(e)[1])

    line[...] = jnp.zeros_like(line)
    x_wide[...] = jnp.zeros_like(x_wide)
    g_wide[...] = jnp.zeros_like(g_wide)
    g_loose[...] = jnp.zeros_like(g_loose)
    pack(acts, x_stage, 0, tiles, line, flatten, 0)

    @pl.when(section == sections - 1)
    def _():
        pack(cot, g_stage, 0, tiles, line, flatten, 1)

    more = (section > 0).astype(jnp.int32) + (section < sections - 1).astype(jnp.int32)
    pl.semaphore_wait(barrier, group - 1 + more)

    def send(c):
        if c > 0:
            pack(acts, x_stage, c, tiles, line, flatten, 0)

            @pl.when(section == sections - 1)
            def _():
                pack(cot, g_stage, c, tiles, line, flatten, 1)

        for d in range(1, tm):
            x_copy(c, d).start()
        x_buf[c, me] = x_stage[me, c]

        @pl.when(section == sections - 1)
        def _():
            for d in range(1, tm):
                g_copy(c, d).start()
            g_buf[c, me] = g_stage[me, c]

    for c in range(chains):
        send(c)
    set_weights(ws_ref, wt_ref, fwd, back, time)
    acc[...] = jnp.zeros_like(acc)
    acc_t[...] = jnp.zeros_like(acc_t)

    shape = (tm, pairs, ROWS, LANES)
    blank = jnp.zeros((1, pairs, ROWS, LANES), jnp.float32)
    centre = slice(HALO, HALO + tiles)

    def turn(c, carry):
        for d in range(1, tm):
            x_copy(c, d).wait_recv()
        spread(x_buf[c], x_loose, x_wide, frame_rows, 0, pairs)
        x = x_wide[...]
        xx = jnp.concatenate([x, neighbours(x)], axis=3)
        y = mm(flat(xx).astype(jnp.bfloat16), fwd[...], ((1,), (0,)))
        part = [y[:, LANES * i : LANES * (i + 1)].reshape(-1, ROWS, LANES) for i in range(3)]
        z = part[1] + pltpu.roll(part[0], 1, 1) + pltpu.roll(part[2], ROWS - 1, 1)
        z = z.reshape(shape)
        sig = jax.nn.sigmoid(z)
        h = z * sig
        slope = sig * (1.0 + z * (1.0 - sig))

        @pl.when(section == sections - 1)
        def _():
            for d in range(1, tm):
                g_copy(c, d).wait_recv()

        @pl.when(section < sections - 1)
        def _():
            z_copy(c).wait_recv()

        spread(g_buf[c], g_loose, g_wide, frame_rows, 1, pairs - 2)
        g = g_wide[...]
        g3 = jnp.concatenate(
            [
                jnp.concatenate([g[1:], blank], axis=0),
                g,
                jnp.concatenate([blank, g[:-1]], axis=0),
            ],
            axis=3,
        )
        gh = mm(flat(g3).astype(jnp.bfloat16), time[...], ((1,), (1,))).astype(jnp.bfloat16)
        gz = (gh.astype(jnp.float32).reshape(shape) * slope).astype(jnp.bfloat16)
        gz = gz.astype(jnp.float32)
        flat_gz = gz.reshape(-1, ROWS, LANES)
        gg = [
            pltpu.roll(flat_gz, ROWS - 1, 1).reshape(shape),
            gz,
            pltpu.roll(flat_gz, 1, 1).reshape(shape),
        ]
        sides = []
        for v in gg:
            sides += [v, neighbours(v)]
        sides = jnp.concatenate(sides, axis=3).astype(jnp.bfloat16)
        inner = mm(flat(sides), back[...], ((1,), (1,))).reshape(shape)
        place = me * tiles - HALO + lax.broadcasted_iota(jnp.int32, shape, 1)
        row = lax.broadcasted_iota(jnp.int32, shape, 2)
        inside = (place >= 0) & (place < width // LANES) & (row < frame_rows)
        result = jnp.where(inside, g + inner, 0.0)
        for n in range(tm):
            for p in range(pairs - 2):
                at = frame_rows * p
                g_loose[n, at : at + frame_rows, :] = result[n, p + 1, 0:frame_rows]
        r_buf[c] = g_loose[...].astype(jnp.bfloat16)

        @pl.when(section > 0)
        def _():
            z_copy(c).start()

        at = (HALO - 1) * frame_rows
        o_buf[c] = g_loose[:, at : at + tile_rows, :].astype(jnp.bfloat16)
        for d in range(1, tm):
            o_copy(c, d).start()
        home[c, me] = o_buf[c, me]
        hc = flat(h[:, centre]).astype(jnp.bfloat16)
        acc_t[...] += mm(hc, flat(g3[:, centre]).astype(jnp.bfloat16), ((0,), (0,)))
        gc = jnp.concatenate([v[:, centre] for v in gg], axis=3).astype(jnp.bfloat16)
        acc[...] += mm(flat(xx[:, centre]).astype(jnp.bfloat16), flat(gc), ((0,), (0,)))
        return carry

    lax.fori_loop(0, chains, turn, 0)

    taps = taps_of(acc[...], acc_t[...], chans)
    for k in range(6):
        ds[k * chans : (k + 1) * chans, :] = jnp.concatenate([taps[2 * k], taps[2 * k + 1]], axis=1)
    rows = w_send.shape[1]
    for k in range(group):
        w_send[k] = ds[k * rows : (k + 1) * rows, :].astype(jnp.bfloat16)
    for e in range(1, group):
        w_copy(e).start()
    w_recv[rank] = w_send[rank]

    def unpack(c):
        for d in range(1, tm):
            o_copy(c, d).wait_recv()
        o_loose[...] = home[c].astype(jnp.float32)
        for m in range(tm):
            for r in range(frame_rows):
                at = r * count + m * tiles * local + c % local
                flatten[pl.ds(at, tiles, stride=local), :] = o_loose[m, pl.ds(r, tiles, stride=frame_rows), :]
        if c % local == local - 1:
            out[c // local] = flatten[...].astype(jnp.bfloat16).reshape(frame_rows, count, LANES)

    for c in range(chains - 1):
        unpack(c)
    for e in range(1, group):
        w_copy(e).wait_recv()
    w_piece[...] = jnp.sum(w_recv[...].astype(jnp.float32), axis=0)
    for e in range(1, group):
        f_copy(e).start()
    w_full[rank] = w_piece[...]
    unpack(chains - 1)

    for e in range(1, group):
        f_copy(e).wait_recv()
    for k in range(group):
        ds[k * rows : (k + 1) * rows, :] = w_full[k]
    for t in range(12):
        both = ds[(t // 2) * chans : (t // 2 + 1) * chans, :]
        half = both[:, (t % 2) * chans : (t % 2 + 1) * chans]
        if t < 9:
            spatial[t] = half
        else:
            temporal[t - 9] = half

    def finish(c, carry):
        for d in range(1, tm):
            x_copy(c, d).wait_send()
            o_copy(c, d).wait_send()

        @pl.when(section == sections - 1)
        def _():
            for d in range(1, tm):
                g_copy(c, d).wait_send()

        @pl.when(section > 0)
        def _():
            z_copy(c).wait_send()

        return carry

    lax.fori_loop(0, chains, finish, 0)
    for e in range(1, group):
        w_copy(e).wait_send()
        f_copy(e).wait_send()


def tiled(a):
    micro, local, rows, width = a.shape
    a = a.reshape(micro, local, rows, width // LANES, LANES)
    return a.transpose(0, 2, 3, 1, 4).reshape(micro, rows, width // LANES * local, LANES)


def untiled(a, local):
    micro, rows, count, _ = a.shape
    a = a.reshape(micro, rows, count // local, local, LANES)
    return a.transpose(0, 3, 1, 2, 4).reshape(micro, local, rows, count // local * LANES)


def body(acts, cot, spatial_weight, temporal_weight):
    sections, tm, batches = [lax.axis_size(a) for a in ("section", "tm", "batch")]
    micro, local, rows, width = cot.shape
    chans = spatial_weight.shape[-1]
    chains = micro * local
    group = tm * batches
    tiles = width // LANES // tm
    pairs = tiles + 2 * HALO
    pairs += pairs % 2
    x_rows, g_rows, tile_rows = [-(-n * rows // 16) * 16 for n in (pairs, pairs - 2, tiles)]
    piece = 6 * chans // group
    bf16, f32 = jnp.bfloat16, jnp.float32
    vmem, dma = pltpu.VMEM, pltpu.SemaphoreType.DMA
    grad, spatial, temporal = pl.pallas_call(
        functools.partial(kernel, sections, batches, tiles),
        out_shape=[
            jax.ShapeDtypeStruct((micro, rows, width // LANES * local, LANES), bf16),
            jax.ShapeDtypeStruct((9, chans, chans), f32),
            jax.ShapeDtypeStruct((3, chans, chans), f32),
        ],
        in_specs=[pl.BlockSpec(memory_space=vmem)] * 4,
        out_specs=[pl.BlockSpec(memory_space=vmem)] * 3,
        scratch_shapes=[
            vmem((tm, chains, x_rows, LANES), bf16),
            vmem((tm, chains, g_rows, LANES), bf16),
            vmem((chains, tm, x_rows, LANES), bf16),
            vmem((chains, tm, g_rows, LANES), bf16),
            vmem((chains, tm, g_rows, LANES), bf16),
            vmem((chains, tm, tile_rows, LANES), bf16),
            vmem((chains, tm, tile_rows, LANES), bf16),
            vmem((2 * LANES, 3 * LANES), bf16),
            vmem((LANES, 6 * LANES), bf16),
            vmem((LANES, 3 * LANES), bf16),
            vmem((2 * LANES, 3 * LANES), f32),
            vmem((LANES, 3 * LANES), f32),
            vmem((6 * chans, LANES), f32),
            vmem((group, piece, LANES), bf16),
            vmem((group, piece, LANES), bf16),
            vmem((piece, LANES), f32),
            vmem((group, piece, LANES), f32),
            vmem(((width // LANES + HALO + pairs) * rows + 16, LANES), f32),
            vmem((rows * width // LANES * local, LANES), f32),
            vmem((tm, x_rows, LANES), f32),
            vmem((tm, g_rows, LANES), f32),
            vmem((tm, tile_rows, LANES), f32),
            vmem((tm, pairs, ROWS, LANES), f32),
            vmem((tm, pairs, ROWS, LANES), f32),
            dma((2, chains, tm - 1)),
            dma((2, chains, tm - 1)),
            dma((2, chains)),
            dma((2, chains, tm - 1)),
            dma((2, group - 1)),
            dma((2, group - 1)),
        ],
        compiler_params=pltpu.CompilerParams(
            collective_id=0, has_side_effects=True, vmem_limit_bytes=56 * 2**20
        ),
    )(tiled(acts[0]), tiled(cot), spatial_weight[0], temporal_weight[0])
    return untiled(grad, local)[None], spatial[None], temporal[None]


def solution(mesh):
    in_specs = (
        P("section", "batch", "tm", None, None),
        P("batch", "tm", None, None),
        P("section", None, None, None),
        P("section", None, None, None),
    )
    out_specs = (
        P("section", "batch", "tm", None, None),
        P("section", None, None, None),
        P("section", None, None, None),
    )
    return jax.shard_map(body, mesh=mesh, in_specs=in_specs, out_specs=out_specs, check_vma=False)
```

```python
import functools

import jax
import jax.numpy as jnp
from jax import lax
from jax.experimental import pallas as pl
from jax.experimental.pallas import tpu as pltpu
from jax.sharding import PartitionSpec as P

DILATION = 2
ROWS = 8
LANES = 128
HALO = 3
MESH = pl.DeviceIdType.MESH


def neighbours(x):
    none = jnp.zeros_like(x[:, :1])
    after = jnp.concatenate([x[:, 1:], none], axis=1)
    before = jnp.concatenate([none, x[:, :-1]], axis=1)
    lane = lax.broadcasted_iota(jnp.int32, x.shape, 3)
    return jnp.where(lane < LANES // 2, after, before)


def flat(x):
    return x.reshape(-1, x.shape[-1])


def mm(a, b, dims):
    return lax.dot_general(a, b, (dims, ((), ())), preferred_element_type=jnp.float32)


def taps_of(d, dt, chans):
    def block(a, r, i, b):
        at = i * LANES + b * chans
        return a[r * chans : (r + 1) * chans, at : at + chans]

    taps = []
    for i in range(3):
        taps.append(block(d, 0, i, 1) + block(d, 3, i, 0))
        taps.append(block(d, 0, i, 0) + block(d, 1, i, 1))
        taps.append(block(d, 1, i, 0) + block(d, 2, i, 1))
    for k in range(3):
        taps.append(block(dt, 0, k, 0) + block(dt, 1, k, 1))
    return taps


def set_weights(ws_ref, wt_ref, fwd, back, time):
    chans = ws_ref.shape[-1]
    zero = jnp.zeros((chans, chans), jnp.bfloat16)
    for i in range(3):
        a, b, c = [ws_ref[3 * i + j] for j in range(3)]
        at = slice(i * LANES, (i + 1) * LANES)
        rows = [[b, a], [c, b], [zero, c], [a, zero]]
        fwd[:, at] = jnp.concatenate([jnp.concatenate(v, axis=1) for v in rows], axis=0)
        at = slice(i * 2 * LANES, (i + 1) * 2 * LANES)
        rows = [[b, a, zero, c], [c, b, a, zero]]
        back[:, at] = jnp.concatenate([jnp.concatenate(v, axis=1) for v in rows], axis=0)
        at = slice(i * LANES, (i + 1) * LANES)
        rows = [[wt_ref[i], zero], [zero, wt_ref[i]]]
        time[:, at] = jnp.concatenate([jnp.concatenate(v, axis=1) for v in rows], axis=0)


def pack(frames, stage, c, tiles, line, flatten, skip):
    tm, size = stage.shape[0], stage.shape[2]
    rows, count = frames.shape[1], frames.shape[2]
    local = stage.shape[1] // frames.shape[0]
    pairs = count // local
    flatten[...] = frames[c // local].astype(jnp.float32).reshape(flatten.shape)
    for r in range(rows):
        at = r * count + c % local
        line[pl.ds(HALO * rows + r, pairs, stride=rows), :] = flatten[pl.ds(at, pairs, stride=local), :]
    for m in range(tm):
        at = (tiles * m + skip) * rows
        stage[m, c] = line[at : at + size, :].astype(jnp.bfloat16)


def spread(packed, loose, wide, rows, first, count):
    loose[...] = packed.astype(jnp.float32)
    for n in range(loose.shape[0]):
        for p in range(count):
            wide[n, first + p, 0:rows, :] = loose[n, rows * p : rows * (p + 1), :]


def tile_kernel(
    sections, batches, tiles, acts, cot, ws_ref, wt_ref, out, spatial, temporal,
    x_stage, g_stage, x_buf, g_buf, r_buf, o_buf, home, fwd, back, time, acc, acc_t, ds,
    w_send, w_recv, w_piece, w_full,
    line, flatten, x_loose, g_loose, o_loose, x_wide, g_wide,
    x_sem, g_sem, z_sem, o_sem, w_sem, f_sem,
):
    tm = x_stage.shape[0]
    micro, frame_rows, count, _ = acts.shape
    chains = x_stage.shape[1]
    local = chains // micro
    width = count // local * LANES
    chans = ws_ref.shape[-1]
    pairs = x_wide.shape[1]
    tile_rows = o_buf.shape[2]
    group = tm * batches
    section, me, core = [lax.axis_index(a) for a in ("section", "tm", "batch")]
    rank = me * batches + core

    def member(e):
        other = lax.rem(rank + e, group)
        return other, (section, other // batches, lax.rem(other, batches))

    def peer(d):
        other = lax.rem(me + d, tm)
        return other, (section, other, core)

    barrier = pltpu.get_barrier_semaphore()
    for e in range(1, group):
        pl.semaphore_signal(barrier, inc=1, device_id=member(e)[1], device_id_type=MESH)

    @pl.when(section > 0)
    def _():
        pl.semaphore_signal(barrier, inc=1, device_id=(section - 1, me, core), device_id_type=MESH)

    @pl.when(section < sections - 1)
    def _():
        pl.semaphore_signal(barrier, inc=1, device_id=(section + 1, me, core), device_id_type=MESH)

    def copy(src, dst, sems, at, device):
        return pltpu.make_async_remote_copy(
            src_ref=src, dst_ref=dst, send_sem=sems.at[(0,) + at], recv_sem=sems.at[(1,) + at],
            device_id=device, device_id_type=MESH,
        )

    def x_copy(c, d):
        other, device = peer(d)
        return copy(x_stage.at[other, c], x_buf.at[c, me], x_sem, (c, d - 1), device)

    def g_copy(c, d):
        other, device = peer(d)
        return copy(g_stage.at[other, c], g_buf.at[c, me], g_sem, (c, d - 1), device)

    def z_copy(c):
        return copy(r_buf.at[c], g_buf.at[c], z_sem, (c,), (lax.max(section - 1, 0), me, core))

    def o_copy(c, d):
        other, device = peer(d)
        return copy(o_buf.at[c, other], home.at[c, me], o_sem, (c, d - 1), device)

    def w_copy(e):
        other, device = member(e)
        return copy(w_send.at[other], w_recv.at[rank], w_sem, (e - 1,), device)

    def f_copy(e):
        return copy(w_piece, w_full.at[rank], f_sem, (e - 1,), member(e)[1])

    line[...] = jnp.zeros_like(line)
    x_wide[...] = jnp.zeros_like(x_wide)
    g_wide[...] = jnp.zeros_like(g_wide)
    g_loose[...] = jnp.zeros_like(g_loose)
    pack(acts, x_stage, 0, tiles, line, flatten, 0)

    @pl.when(section == sections - 1)
    def _():
        pack(cot, g_stage, 0, tiles, line, flatten, 1)

    more = (section > 0).astype(jnp.int32) + (section < sections - 1).astype(jnp.int32)
    pl.semaphore_wait(barrier, group - 1 + more)

    def send(c):
        if c > 0:
            pack(acts, x_stage, c, tiles, line, flatten, 0)

            @pl.when(section == sections - 1)
            def _():
                pack(cot, g_stage, c, tiles, line, flatten, 1)

        for d in range(1, tm):
            x_copy(c, d).start()
        x_buf[c, me] = x_stage[me, c]

        @pl.when(section == sections - 1)
        def _():
            for d in range(1, tm):
                g_copy(c, d).start()
            g_buf[c, me] = g_stage[me, c]

    for c in range(chains):
        send(c)
    set_weights(ws_ref, wt_ref, fwd, back, time)
    acc[...] = jnp.zeros_like(acc)
    acc_t[...] = jnp.zeros_like(acc_t)

    shape = (tm, pairs, ROWS, LANES)
    blank = jnp.zeros((1, pairs, ROWS, LANES), jnp.float32)
    centre = slice(HALO, HALO + tiles)

    def turn(c, carry):
        for d in range(1, tm):
            x_copy(c, d).wait_recv()
        spread(x_buf[c], x_loose, x_wide, frame_rows, 0, pairs)
        x = x_wide[...]
        xx = jnp.concatenate([x, neighbours(x)], axis=3)
        y = mm(flat(xx).astype(jnp.bfloat16), fwd[...], ((1,), (0,)))
        part = [y[:, LANES * i : LANES * (i + 1)].reshape(-1, ROWS, LANES) for i in range(3)]
        z = part[1] + pltpu.roll(part[0], 1, 1) + pltpu.roll(part[2], ROWS - 1, 1)
        z = z.reshape(shape)
        sig = jax.nn.sigmoid(z)
        h = z * sig
        slope = sig * (1.0 + z * (1.0 - sig))

        @pl.when(section == sections - 1)
        def _():
            for d in range(1, tm):
                g_copy(c, d).wait_recv()

        @pl.when(section < sections - 1)
        def _():
            z_copy(c).wait_recv()

        spread(g_buf[c], g_loose, g_wide, frame_rows, 1, pairs - 2)
        g = g_wide[...]
        g3 = jnp.concatenate(
            [
                jnp.concatenate([g[1:], blank], axis=0),
                g,
                jnp.concatenate([blank, g[:-1]], axis=0),
            ],
            axis=3,
        )
        gh = mm(flat(g3).astype(jnp.bfloat16), time[...], ((1,), (1,))).astype(jnp.bfloat16)
        gz = (gh.astype(jnp.float32).reshape(shape) * slope).astype(jnp.bfloat16)
        gz = gz.astype(jnp.float32)
        flat_gz = gz.reshape(-1, ROWS, LANES)
        gg = [
            pltpu.roll(flat_gz, ROWS - 1, 1).reshape(shape),
            gz,
            pltpu.roll(flat_gz, 1, 1).reshape(shape),
        ]
        sides = []
        for v in gg:
            sides += [v, neighbours(v)]
        sides = jnp.concatenate(sides, axis=3).astype(jnp.bfloat16)
        inner = mm(flat(sides), back[...], ((1,), (1,))).reshape(shape)
        place = me * tiles - HALO + lax.broadcasted_iota(jnp.int32, shape, 1)
        row = lax.broadcasted_iota(jnp.int32, shape, 2)
        inside = (place >= 0) & (place < width // LANES) & (row < frame_rows)
        result = jnp.where(inside, g + inner, 0.0)
        for n in range(tm):
            for p in range(pairs - 2):
                at = frame_rows * p
                g_loose[n, at : at + frame_rows, :] = result[n, p + 1, 0:frame_rows]
        r_buf[c] = g_loose[...].astype(jnp.bfloat16)

        @pl.when(section > 0)
        def _():
            z_copy(c).start()

        at = (HALO - 1) * frame_rows
        o_buf[c] = g_loose[:, at : at + tile_rows, :].astype(jnp.bfloat16)
        for d in range(1, tm):
            o_copy(c, d).start()
        home[c, me] = o_buf[c, me]
        hc = flat(h[:, centre]).astype(jnp.bfloat16)
        acc_t[...] += mm(hc, flat(g3[:, centre]).astype(jnp.bfloat16), ((0,), (0,)))
        gc = jnp.concatenate([v[:, centre] for v in gg], axis=3).astype(jnp.bfloat16)
        acc[...] += mm(flat(xx[:, centre]).astype(jnp.bfloat16), flat(gc), ((0,), (0,)))
        return carry

    lax.fori_loop(0, chains, turn, 0)

    taps = taps_of(acc[...], acc_t[...], chans)
    for k in range(6):
        ds[k * chans : (k + 1) * chans, :] = jnp.concatenate([taps[2 * k], taps[2 * k + 1]], axis=1)
    rows = w_send.shape[1]
    for k in range(group):
        w_send[k] = ds[k * rows : (k + 1) * rows, :].astype(jnp.bfloat16)
    for e in range(1, group):
        w_copy(e).start()
    w_recv[rank] = w_send[rank]

    def unpack(c):
        for d in range(1, tm):
            o_copy(c, d).wait_recv()
        o_loose[...] = home[c].astype(jnp.float32)
        for m in range(tm):
            for r in range(frame_rows):
                at = r * count + m * tiles * local + c % local
                flatten[pl.ds(at, tiles, stride=local), :] = o_loose[m, pl.ds(r, tiles, stride=frame_rows), :]
        if c % local == local - 1:
            out[c // local] = flatten[...].astype(jnp.bfloat16).reshape(frame_rows, count, LANES)

    for c in range(chains - 1):
        unpack(c)
    for e in range(1, group):
        w_copy(e).wait_recv()
    w_piece[...] = jnp.sum(w_recv[...].astype(jnp.float32), axis=0)
    for e in range(1, group):
        f_copy(e).start()
    w_full[rank] = w_piece[...]
    unpack(chains - 1)

    for e in range(1, group):
        f_copy(e).wait_recv()
    for k in range(group):
        ds[k * rows : (k + 1) * rows, :] = w_full[k]
    for t in range(12):
        both = ds[(t // 2) * chans : (t // 2 + 1) * chans, :]
        half = both[:, (t % 2) * chans : (t % 2 + 1) * chans]
        if t < 9:
            spatial[t] = half
        else:
            temporal[t - 9] = half

    def finish(c, carry):
        for d in range(1, tm):
            x_copy(c, d).wait_send()
            o_copy(c, d).wait_send()

        @pl.when(section == sections - 1)
        def _():
            for d in range(1, tm):
                g_copy(c, d).wait_send()

        @pl.when(section > 0)
        def _():
            z_copy(c).wait_send()

        return carry

    lax.fori_loop(0, chains, finish, 0)
    for e in range(1, group):
        w_copy(e).wait_send()
        f_copy(e).wait_send()


def tiled(a):
    micro, local, rows, width = a.shape
    a = a.reshape(micro, local, rows, width // LANES, LANES)
    return a.transpose(0, 2, 3, 1, 4).reshape(micro, rows, width // LANES * local, LANES)


def untiled(a, local):
    micro, rows, count, _ = a.shape
    a = a.reshape(micro, rows, count // local, local, LANES)
    return a.transpose(0, 3, 1, 2, 4).reshape(micro, local, rows, count // local * LANES)


def tile_plan(acts, cot, spatial_weight, temporal_weight):
    sections, tm, batches = [lax.axis_size(a) for a in ("section", "tm", "batch")]
    micro, local, rows, width = cot.shape
    chans = spatial_weight.shape[-1]
    chains = micro * local
    group = tm * batches
    tiles = width // LANES // tm
    pairs = tiles + 2 * HALO
    pairs += pairs % 2
    x_rows, g_rows, tile_rows = [-(-n * rows // 16) * 16 for n in (pairs, pairs - 2, tiles)]
    piece = 6 * chans // group
    bf16, f32 = jnp.bfloat16, jnp.float32
    vmem, dma = pltpu.VMEM, pltpu.SemaphoreType.DMA
    grad, spatial, temporal = pl.pallas_call(
        functools.partial(tile_kernel, sections, batches, tiles),
        out_shape=[
            jax.ShapeDtypeStruct((micro, rows, width // LANES * local, LANES), bf16),
            jax.ShapeDtypeStruct((9, chans, chans), f32),
            jax.ShapeDtypeStruct((3, chans, chans), f32),
        ],
        in_specs=[pl.BlockSpec(memory_space=vmem)] * 4,
        out_specs=[pl.BlockSpec(memory_space=vmem)] * 3,
        scratch_shapes=[
            vmem((tm, chains, x_rows, LANES), bf16),
            vmem((tm, chains, g_rows, LANES), bf16),
            vmem((chains, tm, x_rows, LANES), bf16),
            vmem((chains, tm, g_rows, LANES), bf16),
            vmem((chains, tm, g_rows, LANES), bf16),
            vmem((chains, tm, tile_rows, LANES), bf16),
            vmem((chains, tm, tile_rows, LANES), bf16),
            vmem((2 * LANES, 3 * LANES), bf16),
            vmem((LANES, 6 * LANES), bf16),
            vmem((LANES, 3 * LANES), bf16),
            vmem((2 * LANES, 3 * LANES), f32),
            vmem((LANES, 3 * LANES), f32),
            vmem((6 * chans, LANES), f32),
            vmem((group, piece, LANES), bf16),
            vmem((group, piece, LANES), bf16),
            vmem((piece, LANES), f32),
            vmem((group, piece, LANES), f32),
            vmem(((width // LANES + HALO + pairs) * rows + 16, LANES), f32),
            vmem((rows * width // LANES * local, LANES), f32),
            vmem((tm, x_rows, LANES), f32),
            vmem((tm, g_rows, LANES), f32),
            vmem((tm, tile_rows, LANES), f32),
            vmem((tm, pairs, ROWS, LANES), f32),
            vmem((tm, pairs, ROWS, LANES), f32),
            dma((2, chains, tm - 1)),
            dma((2, chains, tm - 1)),
            dma((2, chains)),
            dma((2, chains, tm - 1)),
            dma((2, group - 1)),
            dma((2, group - 1)),
        ],
        compiler_params=pltpu.CompilerParams(
            collective_id=0, has_side_effects=True, vmem_limit_bytes=56 * 2**20
        ),
    )(tiled(acts[0]), tiled(cot), spatial_weight[0], temporal_weight[0])
    return grad, spatial, temporal

STEP = 6
TILE = 8


def row_before(v):
    sub = lax.broadcasted_iota(jnp.int32, v[:, :1].shape, 2)
    first = jnp.where(sub >= ROWS // 2, pltpu.roll(v[:, -1:], ROWS // 2, 2), 0.0)
    return jnp.concatenate([first, v[:, :-1]], axis=1)


def row_after(v):
    sub = lax.broadcasted_iota(jnp.int32, v[:, :1].shape, 2)
    last = jnp.where(sub < ROWS // 2, pltpu.roll(v[:, :1], ROWS // 2, 2), 0.0)
    return jnp.concatenate([v[:, 1:], last], axis=1)


def beside(v):
    count = v.shape[0] - 2
    lane = lax.broadcasted_iota(jnp.int32, (count,) + v.shape[1:], 3)
    return jnp.where(lane < LANES // 2, v[2:], v[:-2])


def lanes(parts):
    return jnp.concatenate([flat(v).astype(jnp.bfloat16) for v in parts], axis=1)


def wide_weights(ws_ref, wt_ref, fwd, back, time):
    chans = ws_ref.shape[-1]
    zero = jnp.zeros((chans, chans), jnp.bfloat16)

    def grid(rows):
        return jnp.concatenate([jnp.concatenate(v, axis=1) for v in rows], axis=0)

    for i in range(3):
        a, b, c = [ws_ref[3 * i + j] for j in range(3)]
        at = slice(i * LANES, (i + 1) * LANES)
        fwd[:, at] = grid([[b, a], [c, b], [zero, c], [a, zero]])
        back[at, :] = grid([[b, a, zero, c], [c, b, a, zero]])
        time[:, at] = grid([[wt_ref[i], zero], [zero, wt_ref[i]]])


def chain_kernel(
    sections, batches, acts_hbm, cot_hbm, ws_hbm, wt_hbm, out, spatial, temporal,
    acts, cot, ws, wt, x_stage, g_stage, x_in, g_in, xw, gw, res, g_buf, r_buf, o_stage, o_in,
    loose, fwd, back, time, acc, acc_t, ds, w_send, w_recv, w_piece, w_full,
    l_sem, x_sem, g_sem, z_sem, o_sem, w_sem, f_sem,
):
    micro, rows, count, _ = acts.shape
    tiles, tm = x_in.shape[:2]
    local = tm // micro
    steps = g_buf.shape[0]
    chans = ws.shape[-1]
    pair = rows * tm
    size = STEP * pair
    group = tm * batches
    section, me, core = [lax.axis_index(a) for a in ("section", "tm", "batch")]
    last = section == sections - 1
    lag = sections - 1 - section
    rank = me * batches + core

    def member(e):
        other = lax.rem(rank + e, group)
        return other, (section, other // batches, lax.rem(other, batches))

    def peer(d):
        other = lax.rem(me + d, tm)
        return other, (section, other, core)

    barrier = pltpu.get_barrier_semaphore()
    for e in range(1, group):
        pl.semaphore_signal(barrier, inc=1, device_id=member(e)[1], device_id_type=MESH)

    @pl.when(section > 0)
    def _():
        pl.semaphore_signal(barrier, inc=1, device_id=(section - 1, me, core), device_id_type=MESH)

    @pl.when(section < sections - 1)
    def _():
        pl.semaphore_signal(barrier, inc=1, device_id=(section + 1, me, core), device_id_type=MESH)

    loads = [
        pltpu.make_async_copy(a, b, l_sem.at[i])
        for i, (a, b) in enumerate([(acts_hbm, acts), (cot_hbm, cot), (ws_hbm, ws), (wt_hbm, wt)])
    ]
    loads[0].start()

    @pl.when(last)
    def _():
        loads[1].start()

    loads[2].start()
    loads[3].start()

    def copy(src, dst, sems, at, device):
        return pltpu.make_async_remote_copy(
            src_ref=src, dst_ref=dst, send_sem=sems.at[(0,) + at], recv_sem=sems.at[(1,) + at],
            device_id=device, device_id_type=MESH,
        )

    def x_copy(j, d):
        other, device = peer(d)
        return copy(x_stage.at[j, other], x_in.at[j, me], x_sem, (j, d - 1), device)

    def g_copy(j, d):
        other, device = peer(d)
        return copy(g_stage.at[j, other], g_in.at[j, me], g_sem, (j, d - 1), device)

    def z_copy(k):
        return copy(r_buf.at[k], g_buf.at[k], z_sem, (k,), (lax.max(section - 1, 0), me, core))

    def o_copy(j, d):
        other, device = peer(d)
        return copy(o_stage.at[j, other], o_in.at[j, me], o_sem, (j, d - 1), device)

    def w_copy(e):
        other, device = member(e)
        return copy(w_send.at[other], w_recv.at[rank], w_sem, (e - 1,), device)

    def f_copy(e):
        return copy(w_piece, w_full.at[rank], f_sem, (e - 1,), member(e)[1])

    def sub_of(r):
        return r % (rows // 2) * ROWS + r // (rows // 2) * tm

    span = TILE * local

    def pack(frames, stage):
        def tile(j, carry):
            at = pl.ds(pl.multiple_of(span * j, span), span)
            for n in range(micro):
                for r in range(rows):
                    loose[(n * rows + r) * span : (n * rows + r + 1) * span, :] = frames[n, r, at, :].astype(jnp.float32)
            for n in range(micro):
                for t in range(local):
                    cut = [loose[pl.ds((n * rows + r) * span + t, TILE, stride=local), :] for r in range(rows)]
                    stage[j, n * local + t] = jnp.concatenate(cut, axis=0).astype(jnp.bfloat16)
            return carry

        lax.fori_loop(0, tiles, tile, 0)

    xw[...] = jnp.zeros_like(xw)
    gw[...] = jnp.zeros_like(gw)
    acc[...] = jnp.zeros_like(acc)
    acc_t[...] = jnp.zeros_like(acc_t)

    @pl.when(last)
    def _():
        loads[1].wait()
        pack(cot, g_stage)

    loads[0].wait()
    pack(acts, x_stage)
    more = (section > 0).astype(jnp.int32) + (section < sections - 1).astype(jnp.int32)
    pl.semaphore_wait(barrier, group - 1 + more)

    def send(j, carry):
        for d in range(1, tm):
            x_copy(j, d).start()
        x_in[j, me] = x_stage[j, me]

        @pl.when(last)
        def _():
            for d in range(1, tm):
                g_copy(j, d).start()
            g_in[j, me] = g_stage[j, me]

        return carry

    lax.fori_loop(0, tiles, send, 0)
    loads[2].wait()
    loads[3].wait()
    wide_weights(ws, wt, fwd, back, time)

    def spread(tile, wide, base):
        for m in range(tm):
            v = tile[m].astype(jnp.float32)
            for r in range(rows):
                at = base + (sub_of(r) + m)
                wide[pl.ds(at, TILE, stride=pair), :] = v[TILE * r : TILE * (r + 1)]

    def land(j, carry):
        for d in range(1, tm):
            x_copy(j, d).wait_recv()
        spread(x_in[j], xw, (j * TILE + 1 + lag) * pair)

        @pl.when(last)
        def _():
            for d in range(1, tm):
                g_copy(j, d).wait_recv()
            spread(g_in[j], gw, (j * TILE + 1) * pair)

        return carry

    def wanted(k):
        return jnp.where(k < 0, 0, lax.min((STEP * (k + 1) + TILE) // TILE, tiles))

    def ready(k):
        return lax.max((STEP * (k + 1) + TILE - sections) // TILE - 1, 0)

    shape = (STEP, rows // 2, ROWS, LANES)
    sub = lax.broadcasted_iota(jnp.int32, shape, 2)
    bin_at = sub % tm

    def window(ref, first, many):
        at = pl.multiple_of(first * pair, ROWS)
        return ref[pl.ds(at, many * pair), :].reshape((many,) + shape[1:])

    def give(j, carry):
        base = (j * TILE + sections) * pair
        for m in range(tm):
            cut = [res[pl.ds(base + (sub_of(r) + m), TILE, stride=pair), :] for r in range(rows)]
            o_stage[j, m] = jnp.concatenate(cut, axis=0).astype(jnp.bfloat16)
        for d in range(1, tm):
            o_copy(j, d).start()
        o_in[j, me] = o_stage[j, me]
        return carry

    def turn(k, tail):
        lax.fori_loop(wanted(k - 1), wanted(k), land, 0)
        x = window(xw, STEP * k, STEP + 2)
        xx = lanes([x[1:-1], beside(x)])
        y = mm(xx, fwd[...], ((1,), (0,)))
        part = [y[:, LANES * i : LANES * (i + 1)].reshape(shape) for i in range(3)]
        z = part[1] + row_before(part[0]) + row_after(part[2])
        sig = jax.nn.sigmoid(z)
        h = z * sig
        slope = sig * (1.0 + z * (1.0 - sig))

        @pl.when(section < sections - 1)
        def _():
            z_copy(k).wait_recv()
            at = pl.multiple_of((STEP * k + 1) * pair, ROWS)
            gw[pl.ds(at, size), :] = g_buf[k].astype(jnp.float32)

        held = window(gw, STEP * k, STEP + 1)
        g = held[1:]
        after = jnp.where(bin_at < tm - 1, pltpu.roll(g, ROWS - 1, 2), 0.0)
        before = jnp.where(bin_at > 0, pltpu.roll(g, 1, 2), 0.0)
        g3 = lanes([after, g, before])
        gh = mm(g3, time[...], ((1,), (1,))).astype(jnp.bfloat16)
        gz = (gh.astype(jnp.float32).reshape(shape) * slope).astype(jnp.bfloat16)
        gz = gz.astype(jnp.float32)
        sent = jnp.concatenate([tail, gz], axis=0)
        y = mm(lanes([sent[1:-1], beside(sent)]), back[...], ((1,), (1,)))
        part = [y[:, LANES * i : LANES * (i + 1)].reshape(shape) for i in range(3)]
        inner = part[1] + row_after(part[0]) + row_before(part[2])
        first = STEP * k - lag - 1
        place = first + lax.broadcasted_iota(jnp.int32, shape, 0)
        inside = (place >= 0) & (place < TILE * tiles)
        result = flat(jnp.where(inside, held[:-1] + inner, 0.0))
        r_buf[k] = result.astype(jnp.bfloat16)

        @pl.when(section > 0)
        def _():
            z_copy(k).start()

        res[pl.ds(pl.multiple_of((first + sections) * pair, ROWS), size), :] = result

        lax.fori_loop(ready(k - 1), ready(k), give, 0)
        acc_t[...] += mm(flat(h).astype(jnp.bfloat16), g3, ((0,), (0,)))
        acc[...] += mm(xx, lanes([row_after(gz), gz, row_before(gz)]), ((0,), (0,)))
        return gz[-2:]

    lax.fori_loop(0, steps, turn, jnp.zeros((2,) + shape[1:], jnp.float32))

    taps = taps_of(acc[...], acc_t[...], chans)
    for k in range(6):
        ds[k * chans : (k + 1) * chans, :] = jnp.concatenate([taps[2 * k], taps[2 * k + 1]], axis=1)
    share = w_send.shape[1]
    for k in range(group):
        w_send[k] = ds[k * share : (k + 1) * share, :].astype(jnp.bfloat16)
    for e in range(1, group):
        w_copy(e).start()
    w_recv[rank] = w_send[rank]

    def unpack(j, carry):
        for d in range(1, tm):
            o_copy(j, d).wait_recv()
        for c in range(tm):
            v = o_in[j, c].astype(jnp.float32)
            for r in range(rows):
                at = (c // local * rows + r) * span + c % local
                loose[pl.ds(at, TILE, stride=local), :] = v[TILE * r : TILE * (r + 1)]
        at = pl.ds(pl.multiple_of(span * j, span), span)
        for n in range(micro):
            for r in range(rows):
                v = loose[(n * rows + r) * span : (n * rows + r + 1) * span, :]
                out[n, r, at, :] = v.astype(jnp.bfloat16)
        return carry

    lax.fori_loop(0, tiles - 2, unpack, 0)
    for e in range(1, group):
        w_copy(e).wait_recv()
    w_piece[...] = jnp.sum(w_recv[...].astype(jnp.float32), axis=0)
    for e in range(1, group):
        f_copy(e).start()
    w_full[rank] = w_piece[...]
    lax.fori_loop(tiles - 2, tiles, unpack, 0)

    for e in range(1, group):
        f_copy(e).wait_recv()
    for k in range(group):
        ds[k * share : (k + 1) * share, :] = w_full[k]
    for t in range(12):
        both = ds[(t // 2) * chans : (t // 2 + 1) * chans, :]
        half = both[:, (t % 2) * chans : (t % 2 + 1) * chans]
        if t < 9:
            spatial[t] = half
        else:
            temporal[t - 9] = half

    def finish(j, carry):
        for d in range(1, tm):
            x_copy(j, d).wait_send()
            o_copy(j, d).wait_send()

        @pl.when(last)
        def _():
            for d in range(1, tm):
                g_copy(j, d).wait_send()

        return carry

    lax.fori_loop(0, tiles, finish, 0)

    @pl.when(section > 0)
    def _():
        def sent(k, carry):
            z_copy(k).wait_send()
            return carry

        lax.fori_loop(0, steps, sent, 0)

    for e in range(1, group):
        w_copy(e).wait_send()
        f_copy(e).wait_send()


def chain_plan(acts, cot, spatial_weight, temporal_weight):
    sections, tm, batches = [lax.axis_size(a) for a in ("section", "tm", "batch")]
    micro, local, rows, width = cot.shape
    chans = spatial_weight.shape[-1]
    group = tm * batches
    count = width // LANES
    tiles = count // TILE
    steps = -(-(count + sections) // STEP)
    pair = rows * tm
    piece = 6 * chans // group
    bf16, f32 = jnp.bfloat16, jnp.float32
    vmem, dma = pltpu.VMEM, pltpu.SemaphoreType.DMA
    return pl.pallas_call(
        functools.partial(chain_kernel, sections, batches),
        out_shape=[
            jax.ShapeDtypeStruct((micro, rows, count * local, LANES), bf16),
            jax.ShapeDtypeStruct((9, chans, chans), f32),
            jax.ShapeDtypeStruct((3, chans, chans), f32),
        ],
        in_specs=[pl.BlockSpec(memory_space=pl.ANY)] * 4,
        out_specs=[pl.BlockSpec(memory_space=vmem)] * 3,
        scratch_shapes=[
            vmem((micro, rows, count * local, LANES), bf16),
            vmem((micro, rows, count * local, LANES), bf16),
            vmem((9, chans, chans), bf16),
            vmem((3, chans, chans), bf16),
        ]
        + [vmem((tiles, tm, TILE * rows, LANES), bf16)] * 4
        + [
            vmem(((max(steps * STEP, count + sections) + 2) * pair, LANES), f32),
            vmem(((steps * STEP + 1) * pair, LANES), f32),
            vmem(((steps * STEP + sections) * pair, LANES), f32),
            vmem((steps, STEP * pair, LANES), bf16),
            vmem((steps, STEP * pair, LANES), bf16),
            vmem((tiles, tm, TILE * rows, LANES), bf16),
            vmem((tiles, tm, TILE * rows, LANES), bf16),
            vmem((micro * rows * TILE * local, LANES), f32),
            vmem((2 * LANES, 3 * LANES), bf16),
            vmem((3 * LANES, 2 * LANES), bf16),
            vmem((LANES, 3 * LANES), bf16),
            vmem((2 * LANES, 3 * LANES), f32),
            vmem((LANES, 3 * LANES), f32),
            vmem((6 * chans, LANES), f32),
            vmem((group, piece, LANES), bf16),
            vmem((group, piece, LANES), bf16),
            vmem((piece, LANES), f32),
            vmem((group, piece, LANES), f32),
            dma((4,)),
            dma((2, tiles, tm - 1)),
            dma((2, tiles, tm - 1)),
            dma((2, steps)),
            dma((2, tiles, tm - 1)),
            dma((2, group - 1)),
            dma((2, group - 1)),
        ],
        compiler_params=pltpu.CompilerParams(
            collective_id=0, has_side_effects=True, vmem_limit_bytes=56 * 2**20
        ),
    )(tiled(acts[0]), tiled(cot), spatial_weight[0], temporal_weight[0])


def hand_over(*refs):
    half = len(refs) // 2
    for a, b in zip(refs[:half], refs[half:]):
        b[...] = a[...]


def settle(arrays):
    spec = [pl.BlockSpec(memory_space=pltpu.VMEM)] * len(arrays)
    shapes = [jax.ShapeDtypeStruct(a.shape, a.dtype) for a in arrays]
    return pl.pallas_call(hand_over, out_shape=shapes, in_specs=spec, out_specs=spec)(*arrays)


def body(acts, cot, spatial_weight, temporal_weight):
    tm, (micro, local, rows, width) = lax.axis_size("tm"), cot.shape
    one_chain_each = tm == micro * local and 2 * tm == ROWS
    whole = rows % 2 == 0 and width % (TILE * LANES) == 0 and TILE * local % 16 == 0 and TILE * rows % 16 == 0
    plan = chain_plan if one_chain_each and whole and local == DILATION else tile_plan
    grad, spatial, temporal = settle(plan(acts, cot, spatial_weight, temporal_weight))
    return untiled(grad, local)[None], spatial[None], temporal[None]


def solution(mesh):
    in_specs = (
        P("section", "batch", "tm", None, None),
        P("batch", "tm", None, None),
        P("section", None, None, None),
        P("section", None, None, None),
    )
    out_specs = (
        P("section", "batch", "tm", None, None),
        P("section", None, None, None),
        P("section", None, None, None),
    )
    return jax.shard_map(body, mesh=mesh, in_specs=in_specs, out_specs=out_specs, check_vma=False)
```

```python
import functools

import jax
import jax.numpy as jnp
from jax import lax
from jax.experimental import pallas as pl
from jax.experimental.pallas import tpu as pltpu
from jax.sharding import PartitionSpec as P

DILATION = 2
ROWS = 8
LANES = 128
HALO = 3
MESH = pl.DeviceIdType.MESH


def neighbours(x):
    none = jnp.zeros_like(x[:, :1])
    after = jnp.concatenate([x[:, 1:], none], axis=1)
    before = jnp.concatenate([none, x[:, :-1]], axis=1)
    lane = lax.broadcasted_iota(jnp.int32, x.shape, 3)
    return jnp.where(lane < LANES // 2, after, before)


def flat(x):
    return x.reshape(-1, x.shape[-1])


def mm(a, b, dims):
    return lax.dot_general(a, b, (dims, ((), ())), preferred_element_type=jnp.float32)


def taps_of(d, dt, chans):
    def block(a, r, i, b):
        at = i * LANES + b * chans
        return a[r * chans : (r + 1) * chans, at : at + chans]

    taps = []
    for i in range(3):
        taps.append(block(d, 0, i, 1) + block(d, 3, i, 0))
        taps.append(block(d, 0, i, 0) + block(d, 1, i, 1))
        taps.append(block(d, 1, i, 0) + block(d, 2, i, 1))
    for k in range(3):
        taps.append(block(dt, 0, k, 0) + block(dt, 1, k, 1))
    return taps


def set_weights(ws_ref, wt_ref, fwd, back, time):
    chans = ws_ref.shape[-1]
    zero = jnp.zeros((chans, chans), jnp.bfloat16)
    for i in range(3):
        a, b, c = [ws_ref[3 * i + j] for j in range(3)]
        at = slice(i * LANES, (i + 1) * LANES)
        rows = [[b, a], [c, b], [zero, c], [a, zero]]
        fwd[:, at] = jnp.concatenate([jnp.concatenate(v, axis=1) for v in rows], axis=0)
        at = slice(i * 2 * LANES, (i + 1) * 2 * LANES)
        rows = [[b, a, zero, c], [c, b, a, zero]]
        back[:, at] = jnp.concatenate([jnp.concatenate(v, axis=1) for v in rows], axis=0)
        at = slice(i * LANES, (i + 1) * LANES)
        rows = [[wt_ref[i], zero], [zero, wt_ref[i]]]
        time[:, at] = jnp.concatenate([jnp.concatenate(v, axis=1) for v in rows], axis=0)


def pack(frames, stage, c, tiles, line, flatten, skip):
    tm, size = stage.shape[0], stage.shape[2]
    rows, count = frames.shape[1], frames.shape[2]
    local = stage.shape[1] // frames.shape[0]
    pairs = count // local
    flatten[...] = frames[c // local].astype(jnp.float32).reshape(flatten.shape)
    for r in range(rows):
        at = r * count + c % local
        line[pl.ds(HALO * rows + r, pairs, stride=rows), :] = flatten[pl.ds(at, pairs, stride=local), :]
    for m in range(tm):
        at = (tiles * m + skip) * rows
        stage[m, c] = line[at : at + size, :].astype(jnp.bfloat16)


def spread(packed, loose, wide, rows, first, count):
    loose[...] = packed.astype(jnp.float32)
    for n in range(loose.shape[0]):
        for p in range(count):
            wide[n, first + p, 0:rows, :] = loose[n, rows * p : rows * (p + 1), :]


def tile_kernel(
    sections, batches, tiles, acts, cot, ws_ref, wt_ref, out, spatial, temporal,
    x_stage, g_stage, x_buf, g_buf, r_buf, o_buf, home, fwd, back, time, acc, acc_t, ds,
    w_send, w_recv, w_piece, w_full,
    line, flatten, x_loose, g_loose, o_loose, x_wide, g_wide,
    x_sem, g_sem, z_sem, o_sem, w_sem, f_sem,
):
    tm = x_stage.shape[0]
    micro, frame_rows, count, _ = acts.shape
    chains = x_stage.shape[1]
    local = chains // micro
    width = count // local * LANES
    chans = ws_ref.shape[-1]
    pairs = x_wide.shape[1]
    tile_rows = o_buf.shape[2]
    group = tm * batches
    section, me, core = [lax.axis_index(a) for a in ("section", "tm", "batch")]
    rank = me * batches + core

    def member(e):
        other = lax.rem(rank + e, group)
        return other, (section, other // batches, lax.rem(other, batches))

    def peer(d):
        other = lax.rem(me + d, tm)
        return other, (section, other, core)

    barrier = pltpu.get_barrier_semaphore()
    for e in range(1, group):
        pl.semaphore_signal(barrier, inc=1, device_id=member(e)[1], device_id_type=MESH)

    @pl.when(section > 0)
    def _():
        pl.semaphore_signal(barrier, inc=1, device_id=(section - 1, me, core), device_id_type=MESH)

    @pl.when(section < sections - 1)
    def _():
        pl.semaphore_signal(barrier, inc=1, device_id=(section + 1, me, core), device_id_type=MESH)

    def copy(src, dst, sems, at, device):
        return pltpu.make_async_remote_copy(
            src_ref=src, dst_ref=dst, send_sem=sems.at[(0,) + at], recv_sem=sems.at[(1,) + at],
            device_id=device, device_id_type=MESH,
        )

    def x_copy(c, d):
        other, device = peer(d)
        return copy(x_stage.at[other, c], x_buf.at[c, me], x_sem, (c, d - 1), device)

    def g_copy(c, d):
        other, device = peer(d)
        return copy(g_stage.at[other, c], g_buf.at[c, me], g_sem, (c, d - 1), device)

    def z_copy(c):
        return copy(r_buf.at[c], g_buf.at[c], z_sem, (c,), (lax.max(section - 1, 0), me, core))

    def o_copy(c, d):
        other, device = peer(d)
        return copy(o_buf.at[c, other], home.at[c, me], o_sem, (c, d - 1), device)

    def w_copy(e):
        other, device = member(e)
        return copy(w_send.at[other], w_recv.at[rank], w_sem, (e - 1,), device)

    def f_copy(e):
        return copy(w_piece, w_full.at[rank], f_sem, (e - 1,), member(e)[1])

    line[...] = jnp.zeros_like(line)
    x_wide[...] = jnp.zeros_like(x_wide)
    g_wide[...] = jnp.zeros_like(g_wide)
    g_loose[...] = jnp.zeros_like(g_loose)
    pack(acts, x_stage, 0, tiles, line, flatten, 0)

    @pl.when(section == sections - 1)
    def _():
        pack(cot, g_stage, 0, tiles, line, flatten, 1)

    more = (section > 0).astype(jnp.int32) + (section < sections - 1).astype(jnp.int32)
    pl.semaphore_wait(barrier, group - 1 + more)

    def send(c):
        if c > 0:
            pack(acts, x_stage, c, tiles, line, flatten, 0)

            @pl.when(section == sections - 1)
            def _():
                pack(cot, g_stage, c, tiles, line, flatten, 1)

        for d in range(1, tm):
            x_copy(c, d).start()
        x_buf[c, me] = x_stage[me, c]

        @pl.when(section == sections - 1)
        def _():
            for d in range(1, tm):
                g_copy(c, d).start()
            g_buf[c, me] = g_stage[me, c]

    for c in range(chains):
        send(c)
    set_weights(ws_ref, wt_ref, fwd, back, time)
    acc[...] = jnp.zeros_like(acc)
    acc_t[...] = jnp.zeros_like(acc_t)

    shape = (tm, pairs, ROWS, LANES)
    blank = jnp.zeros((1, pairs, ROWS, LANES), jnp.float32)
    centre = slice(HALO, HALO + tiles)

    def turn(c, carry):
        for d in range(1, tm):
            x_copy(c, d).wait_recv()
        spread(x_buf[c], x_loose, x_wide, frame_rows, 0, pairs)
        x = x_wide[...]
        xx = jnp.concatenate([x, neighbours(x)], axis=3)
        y = mm(flat(xx).astype(jnp.bfloat16), fwd[...], ((1,), (0,)))
        part = [y[:, LANES * i : LANES * (i + 1)].reshape(-1, ROWS, LANES) for i in range(3)]
        z = part[1] + pltpu.roll(part[0], 1, 1) + pltpu.roll(part[2], ROWS - 1, 1)
        z = z.reshape(shape)
        sig = jax.nn.sigmoid(z)
        h = z * sig
        slope = sig * (1.0 + z * (1.0 - sig))

        @pl.when(section == sections - 1)
        def _():
            for d in range(1, tm):
                g_copy(c, d).wait_recv()

        @pl.when(section < sections - 1)
        def _():
            z_copy(c).wait_recv()

        spread(g_buf[c], g_loose, g_wide, frame_rows, 1, pairs - 2)
        g = g_wide[...]
        g3 = jnp.concatenate(
            [
                jnp.concatenate([g[1:], blank], axis=0),
                g,
                jnp.concatenate([blank, g[:-1]], axis=0),
            ],
            axis=3,
        )
        gh = mm(flat(g3).astype(jnp.bfloat16), time[...], ((1,), (1,))).astype(jnp.bfloat16)
        gz = (gh.astype(jnp.float32).reshape(shape) * slope).astype(jnp.bfloat16)
        gz = gz.astype(jnp.float32)
        flat_gz = gz.reshape(-1, ROWS, LANES)
        gg = [
            pltpu.roll(flat_gz, ROWS - 1, 1).reshape(shape),
            gz,
            pltpu.roll(flat_gz, 1, 1).reshape(shape),
        ]
        sides = []
        for v in gg:
            sides += [v, neighbours(v)]
        sides = jnp.concatenate(sides, axis=3).astype(jnp.bfloat16)
        inner = mm(flat(sides), back[...], ((1,), (1,))).reshape(shape)
        place = me * tiles - HALO + lax.broadcasted_iota(jnp.int32, shape, 1)
        row = lax.broadcasted_iota(jnp.int32, shape, 2)
        inside = (place >= 0) & (place < width // LANES) & (row < frame_rows)
        result = jnp.where(inside, g + inner, 0.0)
        for n in range(tm):
            for p in range(pairs - 2):
                at = frame_rows * p
                g_loose[n, at : at + frame_rows, :] = result[n, p + 1, 0:frame_rows]
        r_buf[c] = g_loose[...].astype(jnp.bfloat16)

        @pl.when(section > 0)
        def _():
            z_copy(c).start()

        at = (HALO - 1) * frame_rows
        o_buf[c] = g_loose[:, at : at + tile_rows, :].astype(jnp.bfloat16)
        for d in range(1, tm):
            o_copy(c, d).start()
        home[c, me] = o_buf[c, me]
        hc = flat(h[:, centre]).astype(jnp.bfloat16)
        acc_t[...] += mm(hc, flat(g3[:, centre]).astype(jnp.bfloat16), ((0,), (0,)))
        gc = jnp.concatenate([v[:, centre] for v in gg], axis=3).astype(jnp.bfloat16)
        acc[...] += mm(flat(xx[:, centre]).astype(jnp.bfloat16), flat(gc), ((0,), (0,)))
        return carry

    lax.fori_loop(0, chains, turn, 0)

    taps = taps_of(acc[...], acc_t[...], chans)
    for k in range(6):
        ds[k * chans : (k + 1) * chans, :] = jnp.concatenate([taps[2 * k], taps[2 * k + 1]], axis=1)
    rows = w_send.shape[1]
    for k in range(group):
        w_send[k] = ds[k * rows : (k + 1) * rows, :].astype(jnp.bfloat16)
    for e in range(1, group):
        w_copy(e).start()
    w_recv[rank] = w_send[rank]

    def unpack(c):
        for d in range(1, tm):
            o_copy(c, d).wait_recv()
        o_loose[...] = home[c].astype(jnp.float32)
        for m in range(tm):
            for r in range(frame_rows):
                at = r * count + m * tiles * local + c % local
                flatten[pl.ds(at, tiles, stride=local), :] = o_loose[m, pl.ds(r, tiles, stride=frame_rows), :]
        if c % local == local - 1:
            out[c // local] = flatten[...].astype(jnp.bfloat16).reshape(frame_rows, count, LANES)

    for c in range(chains - 1):
        unpack(c)
    for e in range(1, group):
        w_copy(e).wait_recv()
    w_piece[...] = jnp.sum(w_recv[...].astype(jnp.float32), axis=0)
    for e in range(1, group):
        f_copy(e).start()
    w_full[rank] = w_piece[...]
    unpack(chains - 1)

    for e in range(1, group):
        f_copy(e).wait_recv()
    for k in range(group):
        ds[k * rows : (k + 1) * rows, :] = w_full[k]
    for t in range(12):
        both = ds[(t // 2) * chans : (t // 2 + 1) * chans, :]
        half = both[:, (t % 2) * chans : (t % 2 + 1) * chans]
        if t < 9:
            spatial[t] = half
        else:
            temporal[t - 9] = half

    def finish(c, carry):
        for d in range(1, tm):
            x_copy(c, d).wait_send()
            o_copy(c, d).wait_send()

        @pl.when(section == sections - 1)
        def _():
            for d in range(1, tm):
                g_copy(c, d).wait_send()

        @pl.when(section > 0)
        def _():
            z_copy(c).wait_send()

        return carry

    lax.fori_loop(0, chains, finish, 0)
    for e in range(1, group):
        w_copy(e).wait_send()
        f_copy(e).wait_send()


def tiled(a):
    micro, local, rows, width = a.shape
    a = a.reshape(micro, local, rows, width // LANES, LANES)
    return a.transpose(0, 2, 3, 1, 4).reshape(micro, rows, width // LANES * local, LANES)


def untiled(a, local):
    micro, rows, count, _ = a.shape
    a = a.reshape(micro, rows, count // local, local, LANES)
    return a.transpose(0, 3, 1, 2, 4).reshape(micro, local, rows, count // local * LANES)


def tile_plan(acts, cot, spatial_weight, temporal_weight):
    sections, tm, batches = [lax.axis_size(a) for a in ("section", "tm", "batch")]
    micro, local, rows, width = cot.shape
    chans = spatial_weight.shape[-1]
    chains = micro * local
    group = tm * batches
    tiles = width // LANES // tm
    pairs = tiles + 2 * HALO
    pairs += pairs % 2
    x_rows, g_rows, tile_rows = [-(-n * rows // 16) * 16 for n in (pairs, pairs - 2, tiles)]
    piece = 6 * chans // group
    bf16, f32 = jnp.bfloat16, jnp.float32
    vmem, dma = pltpu.VMEM, pltpu.SemaphoreType.DMA
    grad, spatial, temporal = pl.pallas_call(
        functools.partial(tile_kernel, sections, batches, tiles),
        out_shape=[
            jax.ShapeDtypeStruct((micro, rows, width // LANES * local, LANES), bf16),
            jax.ShapeDtypeStruct((9, chans, chans), f32),
            jax.ShapeDtypeStruct((3, chans, chans), f32),
        ],
        in_specs=[pl.BlockSpec(memory_space=vmem)] * 4,
        out_specs=[pl.BlockSpec(memory_space=vmem)] * 3,
        scratch_shapes=[
            vmem((tm, chains, x_rows, LANES), bf16),
            vmem((tm, chains, g_rows, LANES), bf16),
            vmem((chains, tm, x_rows, LANES), bf16),
            vmem((chains, tm, g_rows, LANES), bf16),
            vmem((chains, tm, g_rows, LANES), bf16),
            vmem((chains, tm, tile_rows, LANES), bf16),
            vmem((chains, tm, tile_rows, LANES), bf16),
            vmem((2 * LANES, 3 * LANES), bf16),
            vmem((LANES, 6 * LANES), bf16),
            vmem((LANES, 3 * LANES), bf16),
            vmem((2 * LANES, 3 * LANES), f32),
            vmem((LANES, 3 * LANES), f32),
            vmem((6 * chans, LANES), f32),
            vmem((group, piece, LANES), bf16),
            vmem((group, piece, LANES), bf16),
            vmem((piece, LANES), f32),
            vmem((group, piece, LANES), f32),
            vmem(((width // LANES + HALO + pairs) * rows + 16, LANES), f32),
            vmem((rows * width // LANES * local, LANES), f32),
            vmem((tm, x_rows, LANES), f32),
            vmem((tm, g_rows, LANES), f32),
            vmem((tm, tile_rows, LANES), f32),
            vmem((tm, pairs, ROWS, LANES), f32),
            vmem((tm, pairs, ROWS, LANES), f32),
            dma((2, chains, tm - 1)),
            dma((2, chains, tm - 1)),
            dma((2, chains)),
            dma((2, chains, tm - 1)),
            dma((2, group - 1)),
            dma((2, group - 1)),
        ],
        compiler_params=pltpu.CompilerParams(
            collective_id=0, has_side_effects=True, vmem_limit_bytes=56 * 2**20
        ),
    )(tiled(acts[0]), tiled(cot), spatial_weight[0], temporal_weight[0])
    return grad, spatial, temporal

STEP = 6
TILE = 8


def row_before(v):
    sub = lax.broadcasted_iota(jnp.int32, v[:, :1].shape, 2)
    first = jnp.where(sub >= ROWS // 2, pltpu.roll(v[:, -1:], ROWS // 2, 2), 0.0)
    return jnp.concatenate([first, v[:, :-1]], axis=1)


def row_after(v):
    sub = lax.broadcasted_iota(jnp.int32, v[:, :1].shape, 2)
    last = jnp.where(sub < ROWS // 2, pltpu.roll(v[:, :1], ROWS // 2, 2), 0.0)
    return jnp.concatenate([v[:, 1:], last], axis=1)


def beside(v):
    count = v.shape[0] - 2
    lane = lax.broadcasted_iota(jnp.int32, (count,) + v.shape[1:], 3)
    return jnp.where(lane < LANES // 2, v[2:], v[:-2])


def lanes(parts):
    return jnp.concatenate([flat(v).astype(jnp.bfloat16) for v in parts], axis=1)


def wide_weights(ws_ref, wt_ref, fwd, back, time):
    chans = ws_ref.shape[-1]
    zero = jnp.zeros((chans, chans), jnp.bfloat16)

    def grid(rows):
        return jnp.concatenate([jnp.concatenate(v, axis=1) for v in rows], axis=0)

    for i in range(3):
        a, b, c = [ws_ref[3 * i + j] for j in range(3)]
        at = slice(i * LANES, (i + 1) * LANES)
        fwd[:, at] = grid([[b, a], [c, b], [zero, c], [a, zero]])
        back[at, :] = grid([[b, a, zero, c], [c, b, a, zero]])
        time[:, at] = grid([[wt_ref[i], zero], [zero, wt_ref[i]]])


def chain_kernel(
    sections, batches, acts_hbm, cot_hbm, ws_hbm, wt_hbm, out, spatial, temporal,
    acts, cot, ws, wt, x_stage, g_stage, x_in, g_in, xw, gw, res, xs, hs, slopes, gs, ggs, g_buf, r_buf, o_stage, o_in,
    loose, fwd, back, time, acc, acc_t, ds, w_send, w_recv, w_piece, w_full,
    l_sem, x_sem, g_sem, z_sem, o_sem, w_sem, f_sem,
):
    micro, rows, count, _ = acts.shape
    tiles, tm = x_in.shape[:2]
    local = tm // micro
    steps = g_buf.shape[0]
    chans = ws.shape[-1]
    pair = rows * tm
    size = STEP * pair
    group = tm * batches
    section, me, core = [lax.axis_index(a) for a in ("section", "tm", "batch")]
    last = section == sections - 1
    lag = sections - 1 - section
    rank = me * batches + core

    def member(e):
        other = lax.rem(rank + e, group)
        return other, (section, other // batches, lax.rem(other, batches))

    def peer(d):
        other = lax.rem(me + d, tm)
        return other, (section, other, core)

    barrier = pltpu.get_barrier_semaphore()
    for e in range(1, group):
        pl.semaphore_signal(barrier, inc=1, device_id=member(e)[1], device_id_type=MESH)

    @pl.when(section > 0)
    def _():
        pl.semaphore_signal(barrier, inc=1, device_id=(section - 1, me, core), device_id_type=MESH)

    @pl.when(section < sections - 1)
    def _():
        pl.semaphore_signal(barrier, inc=1, device_id=(section + 1, me, core), device_id_type=MESH)

    loads = [
        pltpu.make_async_copy(a, b, l_sem.at[i])
        for i, (a, b) in enumerate([(acts_hbm, acts), (cot_hbm, cot), (ws_hbm, ws), (wt_hbm, wt)])
    ]
    loads[0].start()

    @pl.when(last)
    def _():
        loads[1].start()

    loads[2].start()
    loads[3].start()

    def copy(src, dst, sems, at, device):
        return pltpu.make_async_remote_copy(
            src_ref=src, dst_ref=dst, send_sem=sems.at[(0,) + at], recv_sem=sems.at[(1,) + at],
            device_id=device, device_id_type=MESH,
        )

    def x_copy(j, d):
        other, device = peer(d)
        return copy(x_stage.at[j, other], x_in.at[j, me], x_sem, (j, d - 1), device)

    def g_copy(j, d):
        other, device = peer(d)
        return copy(g_stage.at[j, other], g_in.at[j, me], g_sem, (j, d - 1), device)

    def z_copy(k):
        return copy(r_buf.at[k], g_buf.at[k], z_sem, (k,), (lax.max(section - 1, 0), me, core))

    def o_copy(j, d):
        other, device = peer(d)
        return copy(o_stage.at[j, other], o_in.at[j, me], o_sem, (j, d - 1), device)

    def w_copy(e):
        other, device = member(e)
        return copy(w_send.at[other], w_recv.at[rank], w_sem, (e - 1,), device)

    def f_copy(e):
        return copy(w_piece, w_full.at[rank], f_sem, (e - 1,), member(e)[1])

    def sub_of(r):
        return r % (rows // 2) * ROWS + r // (rows // 2) * tm

    span = TILE * local

    def pack(frames, stage):
        def tile(j, carry):
            at = pl.ds(pl.multiple_of(span * j, span), span)
            for n in range(micro):
                for r in range(rows):
                    loose[(n * rows + r) * span : (n * rows + r + 1) * span, :] = frames[n, r, at, :].astype(jnp.float32)
            for n in range(micro):
                for t in range(local):
                    cut = [loose[pl.ds((n * rows + r) * span + t, TILE, stride=local), :] for r in range(rows)]
                    stage[j, n * local + t] = jnp.concatenate(cut, axis=0).astype(jnp.bfloat16)
            return carry

        lax.fori_loop(0, tiles, tile, 0)

    xw[...] = jnp.zeros_like(xw)
    gw[...] = jnp.zeros_like(gw)
    acc[...] = jnp.zeros_like(acc)
    acc_t[...] = jnp.zeros_like(acc_t)

    @pl.when(last)
    def _():
        loads[1].wait()
        pack(cot, g_stage)

    loads[0].wait()
    pack(acts, x_stage)
    more = (section > 0).astype(jnp.int32) + (section < sections - 1).astype(jnp.int32)
    pl.semaphore_wait(barrier, group - 1 + more)

    def send(j, carry):
        for d in range(1, tm):
            x_copy(j, d).start()
        x_in[j, me] = x_stage[j, me]

        @pl.when(last)
        def _():
            for d in range(1, tm):
                g_copy(j, d).start()
            g_in[j, me] = g_stage[j, me]

        return carry

    lax.fori_loop(0, tiles, send, 0)
    loads[2].wait()
    loads[3].wait()
    wide_weights(ws, wt, fwd, back, time)

    def spread(tile, wide, base):
        for m in range(tm):
            v = tile[m].astype(jnp.float32)
            for r in range(rows):
                at = base + (sub_of(r) + m)
                wide[pl.ds(at, TILE, stride=pair), :] = v[TILE * r : TILE * (r + 1)]

    def land(j, carry):
        for d in range(1, tm):
            x_copy(j, d).wait_recv()
        spread(x_in[j], xw, (j * TILE + 1 + lag) * pair)

        @pl.when(last)
        def _():
            for d in range(1, tm):
                g_copy(j, d).wait_recv()
            spread(g_in[j], gw, (j * TILE + 1) * pair)

        return carry

    def wanted(k):
        return jnp.where(k < 0, 0, lax.min((STEP * (k + 1) + TILE) // TILE, tiles))

    def ready(k):
        return lax.max((STEP * (k + 1) + TILE - sections) // TILE - 1, 0)

    shape = (STEP, rows // 2, ROWS, LANES)
    sub = lax.broadcasted_iota(jnp.int32, shape, 2)
    bin_at = sub % tm

    def window(ref, first, many):
        at = pl.multiple_of(first * pair, ROWS)
        return ref[pl.ds(at, many * pair), :].reshape((many,) + shape[1:])

    def give(j, carry):
        third = rows // 2 * TILE
        for m in range(tm):
            at = [pl.multiple_of((j + 1) * TILE * pair + (a * tm + m) * third, TILE) for a in range(2)]
            cut = [res[pl.ds(i, third), :] for i in at]
            o_stage[j, m] = jnp.concatenate(cut, axis=0).astype(jnp.bfloat16)
        for d in range(1, tm):
            o_copy(j, d).start()
        o_in[j, me] = o_stage[j, me]
        return carry

    def ahead(k, carry):
        lax.fori_loop(wanted(k - 1), wanted(k), land, 0)
        x = window(xw, STEP * k, STEP + 2)
        xx = lanes([x[1:-1], beside(x)])
        y = mm(xx, fwd[...], ((1,), (0,)))
        part = [y[:, LANES * i : LANES * (i + 1)].reshape(shape) for i in range(3)]
        z = part[1] + row_before(part[0]) + row_after(part[2])
        sig = jax.nn.sigmoid(z)
        h = z * sig
        xs[k] = xx
        hs[k] = flat(h).astype(jnp.bfloat16)
        slopes[k] = flat(sig * (1.0 + z * (1.0 - sig)))
        return carry

    def grads(k, carry):
        acc_t[...] += mm(hs[k], gs[k], ((0,), (0,)))
        acc[...] += mm(xs[k], ggs[k], ((0,), (0,)))
        return carry

    def turn(k, tail):
        @pl.when(last)
        def _():
            ahead(k, 0)

        @pl.when(section < sections - 1)
        def _():
            z_copy(k).wait_recv()
            at = pl.multiple_of((STEP * k + 1) * pair, ROWS)
            gw[pl.ds(at, size), :] = g_buf[k].astype(jnp.float32)

        held = window(gw, STEP * k, STEP + 1)
        g = held[1:]
        after = jnp.where(bin_at < tm - 1, pltpu.roll(g, ROWS - 1, 2), 0.0)
        before = jnp.where(bin_at > 0, pltpu.roll(g, 1, 2), 0.0)
        g3 = lanes([after, g, before])
        gh = mm(g3, time[...], ((1,), (1,))).astype(jnp.bfloat16)
        gz = (gh.astype(jnp.float32) * slopes[k]).reshape(shape).astype(jnp.bfloat16)
        gz = gz.astype(jnp.float32)
        sent = jnp.concatenate([tail, gz], axis=0)
        y = mm(lanes([sent[1:-1], beside(sent)]), back[...], ((1,), (1,)))
        part = [y[:, LANES * i : LANES * (i + 1)].reshape(shape) for i in range(3)]
        inner = part[1] + row_after(part[0]) + row_before(part[2])
        first = STEP * k - lag - 1
        place = first + lax.broadcasted_iota(jnp.int32, shape, 0)
        inside = (place >= 0) & (place < TILE * tiles)
        result = jnp.where(inside, held[:-1] + inner, 0.0)
        r_buf[k] = flat(result).astype(jnp.bfloat16)

        @pl.when(section > 0)
        def _():
            z_copy(k).start()

        for i in range(STEP):
            q = first + TILE + i
            at = q // TILE * (TILE * pair) + q % TILE
            for b in range(rows // 2):
                res[pl.ds(at + b * TILE, ROWS, stride=rows // 2 * TILE), :] = result[i, b]

        lax.fori_loop(ready(k - 1), ready(k), give, 0)
        gs[k] = g3
        ggs[k] = lanes([row_after(gz), gz, row_before(gz)])

        @pl.when(section < sections - 1)
        def _():
            grads(k, 0)

        return gz[-2:]

    @pl.when(section < sections - 1)
    def _():
        lax.fori_loop(0, steps, ahead, 0)

    lax.fori_loop(0, steps, turn, jnp.zeros((2,) + shape[1:], jnp.float32))

    @pl.when(last)
    def _():
        lax.fori_loop(0, steps, grads, 0)

    taps = taps_of(acc[...], acc_t[...], chans)
    for k in range(6):
        ds[k * chans : (k + 1) * chans, :] = jnp.concatenate([taps[2 * k], taps[2 * k + 1]], axis=1)
    share = w_send.shape[1]
    for k in range(group):
        w_send[k] = ds[k * share : (k + 1) * share, :].astype(jnp.bfloat16)
    for e in range(1, group):
        w_copy(e).start()
    w_recv[rank] = w_send[rank]

    def unpack(j, carry):
        for d in range(1, tm):
            o_copy(j, d).wait_recv()
        for c in range(tm):
            v = o_in[j, c].astype(jnp.float32)
            for r in range(rows):
                at = (c // local * rows + r) * span + c % local
                loose[pl.ds(at, TILE, stride=local), :] = v[TILE * r : TILE * (r + 1)]
        at = pl.ds(pl.multiple_of(span * j, span), span)
        for n in range(micro):
            for r in range(rows):
                v = loose[(n * rows + r) * span : (n * rows + r + 1) * span, :]
                out[n, r, at, :] = v.astype(jnp.bfloat16)
        return carry

    lax.fori_loop(0, tiles - 2, unpack, 0)
    for e in range(1, group):
        w_copy(e).wait_recv()
    w_piece[...] = jnp.sum(w_recv[...].astype(jnp.float32), axis=0).astype(jnp.bfloat16)
    for e in range(1, group):
        f_copy(e).start()
    w_full[rank] = w_piece[...]
    lax.fori_loop(tiles - 2, tiles, unpack, 0)

    def finish(j, carry):
        for d in range(1, tm):
            x_copy(j, d).wait_send()
            o_copy(j, d).wait_send()

        @pl.when(last)
        def _():
            for d in range(1, tm):
                g_copy(j, d).wait_send()

        return carry

    lax.fori_loop(0, tiles, finish, 0)

    @pl.when(section > 0)
    def _():
        def sent(k, carry):
            z_copy(k).wait_send()
            return carry

        lax.fori_loop(0, steps, sent, 0)

    for e in range(1, group):
        w_copy(e).wait_send()
    for e in range(1, group):
        f_copy(e).wait_recv()
    for k in range(group):
        ds[k * share : (k + 1) * share, :] = w_full[k].astype(jnp.float32)
    for t in range(12):
        both = ds[(t // 2) * chans : (t // 2 + 1) * chans, :]
        half = both[:, (t % 2) * chans : (t % 2 + 1) * chans]
        if t < 9:
            spatial[t] = half
        else:
            temporal[t - 9] = half
    for e in range(1, group):
        f_copy(e).wait_send()


def chain_plan(acts, cot, spatial_weight, temporal_weight):
    sections, tm, batches = [lax.axis_size(a) for a in ("section", "tm", "batch")]
    micro, local, rows, width = cot.shape
    chans = spatial_weight.shape[-1]
    group = tm * batches
    count = width // LANES
    tiles = count // TILE
    steps = -(-(count + sections) // STEP)
    pair = rows * tm
    piece = 6 * chans // group
    bf16, f32 = jnp.bfloat16, jnp.float32
    vmem, dma = pltpu.VMEM, pltpu.SemaphoreType.DMA
    return pl.pallas_call(
        functools.partial(chain_kernel, sections, batches),
        out_shape=[
            vmem((micro, rows, count * local, LANES), bf16),
            vmem((9, chans, chans), f32),
            vmem((3, chans, chans), f32),
        ],
        in_specs=[pl.BlockSpec(memory_space=pl.ANY)] * 4,
        out_specs=[pl.BlockSpec(memory_space=vmem)] * 3,
        scratch_shapes=[
            vmem((micro, rows, count * local, LANES), bf16),
            vmem((micro, rows, count * local, LANES), bf16),
            vmem((9, chans, chans), bf16),
            vmem((3, chans, chans), bf16),
        ]
        + [vmem((tiles, tm, TILE * rows, LANES), bf16)] * 4
        + [
            vmem(((max(steps * STEP, count + sections) + 2) * pair, LANES), f32),
            vmem(((steps * STEP + 1) * pair, LANES), f32),
            vmem(((tiles + 2) * TILE * pair, LANES), f32),
            vmem((steps, STEP * pair, 2 * LANES), bf16),
            vmem((steps, STEP * pair, LANES), bf16),
            vmem((steps, STEP * pair, LANES), f32),
            vmem((steps, STEP * pair, 3 * LANES), bf16),
            vmem((steps, STEP * pair, 3 * LANES), bf16),
            vmem((steps, STEP * pair, LANES), bf16),
            vmem((steps, STEP * pair, LANES), bf16),
            vmem((tiles, tm, TILE * rows, LANES), bf16),
            vmem((tiles, tm, TILE * rows, LANES), bf16),
            vmem((micro * rows * TILE * local, LANES), f32),
            vmem((2 * LANES, 3 * LANES), bf16),
            vmem((3 * LANES, 2 * LANES), bf16),
            vmem((LANES, 3 * LANES), bf16),
            vmem((2 * LANES, 3 * LANES), f32),
            vmem((LANES, 3 * LANES), f32),
            vmem((6 * chans, LANES), f32),
            vmem((group, piece, LANES), bf16),
            vmem((group, piece, LANES), bf16),
            vmem((piece, LANES), bf16),
            vmem((group, piece, LANES), bf16),
            dma((4,)),
            dma((2, tiles, tm - 1)),
            dma((2, tiles, tm - 1)),
            dma((2, steps)),
            dma((2, tiles, tm - 1)),
            dma((2, group - 1)),
            dma((2, group - 1)),
        ],
        compiler_params=pltpu.CompilerParams(
            collective_id=0, has_side_effects=True, vmem_limit_bytes=56 * 2**20
        ),
    )(tiled(acts[0]), tiled(cot), spatial_weight[0], temporal_weight[0])


def hand_over(*refs):
    count = len(refs) // 2
    copies = [pltpu.make_async_copy(refs[i], refs[count + i], refs[-1].at[i]) for i in range(count)]
    for c in copies:
        c.start()
    for c in copies:
        c.wait()


def settle(arrays):
    count = len(arrays)
    return pl.pallas_call(
        hand_over,
        out_shape=[jax.ShapeDtypeStruct(a.shape, a.dtype) for a in arrays],
        in_specs=[pl.BlockSpec(memory_space=pltpu.VMEM)] * count,
        out_specs=[pl.BlockSpec(memory_space=pl.ANY)] * count,
        scratch_shapes=[pltpu.SemaphoreType.DMA((count,))],
    )(*[pltpu.with_memory_space_constraint(a, pltpu.VMEM) for a in arrays])


def body(acts, cot, spatial_weight, temporal_weight):
    tm, (micro, local, rows, width) = lax.axis_size("tm"), cot.shape
    one_chain_each = tm == micro * local and 2 * tm == ROWS
    whole = rows % 2 == 0 and width % (TILE * LANES) == 0 and TILE * local % 16 == 0 and TILE * rows % 16 == 0
    plan = chain_plan if one_chain_each and whole and local == DILATION else tile_plan
    grad, spatial, temporal = settle(plan(acts, cot, spatial_weight, temporal_weight))
    return untiled(grad, local)[None], spatial[None], temporal[None]


def solution(mesh):
    in_specs = (
        P("section", "batch", "tm", None, None),
        P("batch", "tm", None, None),
        P("section", None, None, None),
        P("section", None, None, None),
    )
    out_specs = (
        P("section", "batch", "tm", None, None),
        P("section", None, None, None),
        P("section", None, None, None),
    )
    return jax.shard_map(body, mesh=mesh, in_specs=in_specs, out_specs=out_specs, check_vma=False)
```

```python
import functools

import jax
import jax.numpy as jnp
from jax import lax
from jax.experimental import pallas as pl
from jax.experimental.pallas import tpu as pltpu
from jax.sharding import PartitionSpec as P

DILATION = 2
ROWS = 8
LANES = 128
HALO = 3
MESH = pl.DeviceIdType.MESH


def neighbours(x):
    none = jnp.zeros_like(x[:, :1])
    after = jnp.concatenate([x[:, 1:], none], axis=1)
    before = jnp.concatenate([none, x[:, :-1]], axis=1)
    lane = lax.broadcasted_iota(jnp.int32, x.shape, 3)
    return jnp.where(lane < LANES // 2, after, before)


def flat(x):
    return x.reshape(-1, x.shape[-1])


def mm(a, b, dims):
    return lax.dot_general(a, b, (dims, ((), ())), preferred_element_type=jnp.float32)


def taps_of(d, dt, chans):
    def block(a, r, i, b):
        at = i * LANES + b * chans
        return a[r * chans : (r + 1) * chans, at : at + chans]

    taps = []
    for i in range(3):
        taps.append(block(d, 0, i, 1) + block(d, 3, i, 0))
        taps.append(block(d, 0, i, 0) + block(d, 1, i, 1))
        taps.append(block(d, 1, i, 0) + block(d, 2, i, 1))
    for k in range(3):
        taps.append(block(dt, 0, k, 0) + block(dt, 1, k, 1))
    return taps


def set_weights(ws_ref, wt_ref, fwd, back, time):
    chans = ws_ref.shape[-1]
    zero = jnp.zeros((chans, chans), jnp.bfloat16)
    for i in range(3):
        a, b, c = [ws_ref[3 * i + j] for j in range(3)]
        at = slice(i * LANES, (i + 1) * LANES)
        rows = [[b, a], [c, b], [zero, c], [a, zero]]
        fwd[:, at] = jnp.concatenate([jnp.concatenate(v, axis=1) for v in rows], axis=0)
        at = slice(i * 2 * LANES, (i + 1) * 2 * LANES)
        rows = [[b, a, zero, c], [c, b, a, zero]]
        back[:, at] = jnp.concatenate([jnp.concatenate(v, axis=1) for v in rows], axis=0)
        at = slice(i * LANES, (i + 1) * LANES)
        rows = [[wt_ref[i], zero], [zero, wt_ref[i]]]
        time[:, at] = jnp.concatenate([jnp.concatenate(v, axis=1) for v in rows], axis=0)


def pack(frames, stage, c, tiles, line, flatten, skip):
    tm, size = stage.shape[0], stage.shape[2]
    rows, count = frames.shape[1], frames.shape[2]
    local = stage.shape[1] // frames.shape[0]
    pairs = count // local
    flatten[...] = frames[c // local].astype(jnp.float32).reshape(flatten.shape)
    for r in range(rows):
        at = r * count + c % local
        line[pl.ds(HALO * rows + r, pairs, stride=rows), :] = flatten[pl.ds(at, pairs, stride=local), :]
    for m in range(tm):
        at = (tiles * m + skip) * rows
        stage[m, c] = line[at : at + size, :].astype(jnp.bfloat16)


def spread(packed, loose, wide, rows, first, count):
    loose[...] = packed.astype(jnp.float32)
    for n in range(loose.shape[0]):
        for p in range(count):
            wide[n, first + p, 0:rows, :] = loose[n, rows * p : rows * (p + 1), :]


def tile_kernel(
    sections, batches, tiles, acts, cot, ws_ref, wt_ref, out, spatial, temporal,
    x_stage, g_stage, x_buf, g_buf, r_buf, o_buf, home, fwd, back, time, acc, acc_t, ds,
    w_send, w_recv, w_piece, w_full,
    line, flatten, x_loose, g_loose, o_loose, x_wide, g_wide,
    x_sem, g_sem, z_sem, o_sem, w_sem, f_sem,
):
    tm = x_stage.shape[0]
    micro, frame_rows, count, _ = acts.shape
    chains = x_stage.shape[1]
    local = chains // micro
    width = count // local * LANES
    chans = ws_ref.shape[-1]
    pairs = x_wide.shape[1]
    tile_rows = o_buf.shape[2]
    group = tm * batches
    section, me, core = [lax.axis_index(a) for a in ("section", "tm", "batch")]
    rank = me * batches + core

    def member(e):
        other = lax.rem(rank + e, group)
        return other, (section, other // batches, lax.rem(other, batches))

    def peer(d):
        other = lax.rem(me + d, tm)
        return other, (section, other, core)

    barrier = pltpu.get_barrier_semaphore()
    for e in range(1, group):
        pl.semaphore_signal(barrier, inc=1, device_id=member(e)[1], device_id_type=MESH)

    @pl.when(section > 0)
    def _():
        pl.semaphore_signal(barrier, inc=1, device_id=(section - 1, me, core), device_id_type=MESH)

    @pl.when(section < sections - 1)
    def _():
        pl.semaphore_signal(barrier, inc=1, device_id=(section + 1, me, core), device_id_type=MESH)

    def copy(src, dst, sems, at, device):
        return pltpu.make_async_remote_copy(
            src_ref=src, dst_ref=dst, send_sem=sems.at[(0,) + at], recv_sem=sems.at[(1,) + at],
            device_id=device, device_id_type=MESH,
        )

    def x_copy(c, d):
        other, device = peer(d)
        return copy(x_stage.at[other, c], x_buf.at[c, me], x_sem, (c, d - 1), device)

    def g_copy(c, d):
        other, device = peer(d)
        return copy(g_stage.at[other, c], g_buf.at[c, me], g_sem, (c, d - 1), device)

    def z_copy(c):
        return copy(r_buf.at[c], g_buf.at[c], z_sem, (c,), (lax.max(section - 1, 0), me, core))

    def o_copy(c, d):
        other, device = peer(d)
        return copy(o_buf.at[c, other], home.at[c, me], o_sem, (c, d - 1), device)

    def w_copy(e):
        other, device = member(e)
        return copy(w_send.at[other], w_recv.at[rank], w_sem, (e - 1,), device)

    def f_copy(e):
        return copy(w_piece, w_full.at[rank], f_sem, (e - 1,), member(e)[1])

    line[...] = jnp.zeros_like(line)
    x_wide[...] = jnp.zeros_like(x_wide)
    g_wide[...] = jnp.zeros_like(g_wide)
    g_loose[...] = jnp.zeros_like(g_loose)
    pack(acts, x_stage, 0, tiles, line, flatten, 0)

    @pl.when(section == sections - 1)
    def _():
        pack(cot, g_stage, 0, tiles, line, flatten, 1)

    more = (section > 0).astype(jnp.int32) + (section < sections - 1).astype(jnp.int32)
    pl.semaphore_wait(barrier, group - 1 + more)

    def send(c):
        if c > 0:
            pack(acts, x_stage, c, tiles, line, flatten, 0)

            @pl.when(section == sections - 1)
            def _():
                pack(cot, g_stage, c, tiles, line, flatten, 1)

        for d in range(1, tm):
            x_copy(c, d).start()
        x_buf[c, me] = x_stage[me, c]

        @pl.when(section == sections - 1)
        def _():
            for d in range(1, tm):
                g_copy(c, d).start()
            g_buf[c, me] = g_stage[me, c]

    for c in range(chains):
        send(c)
    set_weights(ws_ref, wt_ref, fwd, back, time)
    acc[...] = jnp.zeros_like(acc)
    acc_t[...] = jnp.zeros_like(acc_t)

    shape = (tm, pairs, ROWS, LANES)
    blank = jnp.zeros((1, pairs, ROWS, LANES), jnp.float32)
    centre = slice(HALO, HALO + tiles)

    def turn(c, carry):
        for d in range(1, tm):
            x_copy(c, d).wait_recv()
        spread(x_buf[c], x_loose, x_wide, frame_rows, 0, pairs)
        x = x_wide[...]
        xx = jnp.concatenate([x, neighbours(x)], axis=3)
        y = mm(flat(xx).astype(jnp.bfloat16), fwd[...], ((1,), (0,)))
        part = [y[:, LANES * i : LANES * (i + 1)].reshape(-1, ROWS, LANES) for i in range(3)]
        z = part[1] + pltpu.roll(part[0], 1, 1) + pltpu.roll(part[2], ROWS - 1, 1)
        z = z.reshape(shape)
        sig = jax.nn.sigmoid(z)
        h = z * sig
        slope = sig * (1.0 + z * (1.0 - sig))

        @pl.when(section == sections - 1)
        def _():
            for d in range(1, tm):
                g_copy(c, d).wait_recv()

        @pl.when(section < sections - 1)
        def _():
            z_copy(c).wait_recv()

        spread(g_buf[c], g_loose, g_wide, frame_rows, 1, pairs - 2)
        g = g_wide[...]
        g3 = jnp.concatenate(
            [
                jnp.concatenate([g[1:], blank], axis=0),
                g,
                jnp.concatenate([blank, g[:-1]], axis=0),
            ],
            axis=3,
        )
        gh = mm(flat(g3).astype(jnp.bfloat16), time[...], ((1,), (1,))).astype(jnp.bfloat16)
        gz = (gh.astype(jnp.float32).reshape(shape) * slope).astype(jnp.bfloat16)
        gz = gz.astype(jnp.float32)
        flat_gz = gz.reshape(-1, ROWS, LANES)
        gg = [
            pltpu.roll(flat_gz, ROWS - 1, 1).reshape(shape),
            gz,
            pltpu.roll(flat_gz, 1, 1).reshape(shape),
        ]
        sides = []
        for v in gg:
            sides += [v, neighbours(v)]
        sides = jnp.concatenate(sides, axis=3).astype(jnp.bfloat16)
        inner = mm(flat(sides), back[...], ((1,), (1,))).reshape(shape)
        place = me * tiles - HALO + lax.broadcasted_iota(jnp.int32, shape, 1)
        row = lax.broadcasted_iota(jnp.int32, shape, 2)
        inside = (place >= 0) & (place < width // LANES) & (row < frame_rows)
        result = jnp.where(inside, g + inner, 0.0)
        for n in range(tm):
            for p in range(pairs - 2):
                at = frame_rows * p
                g_loose[n, at : at + frame_rows, :] = result[n, p + 1, 0:frame_rows]
        r_buf[c] = g_loose[...].astype(jnp.bfloat16)

        @pl.when(section > 0)
        def _():
            z_copy(c).start()

        at = (HALO - 1) * frame_rows
        o_buf[c] = g_loose[:, at : at + tile_rows, :].astype(jnp.bfloat16)
        for d in range(1, tm):
            o_copy(c, d).start()
        home[c, me] = o_buf[c, me]
        hc = flat(h[:, centre]).astype(jnp.bfloat16)
        acc_t[...] += mm(hc, flat(g3[:, centre]).astype(jnp.bfloat16), ((0,), (0,)))
        gc = jnp.concatenate([v[:, centre] for v in gg], axis=3).astype(jnp.bfloat16)
        acc[...] += mm(flat(xx[:, centre]).astype(jnp.bfloat16), flat(gc), ((0,), (0,)))
        return carry

    lax.fori_loop(0, chains, turn, 0)

    taps = taps_of(acc[...], acc_t[...], chans)
    for k in range(6):
        ds[k * chans : (k + 1) * chans, :] = jnp.concatenate([taps[2 * k], taps[2 * k + 1]], axis=1)
    rows = w_send.shape[1]
    for k in range(group):
        w_send[k] = ds[k * rows : (k + 1) * rows, :].astype(jnp.bfloat16)
    for e in range(1, group):
        w_copy(e).start()
    w_recv[rank] = w_send[rank]

    def unpack(c):
        for d in range(1, tm):
            o_copy(c, d).wait_recv()
        o_loose[...] = home[c].astype(jnp.float32)
        for m in range(tm):
            for r in range(frame_rows):
                at = r * count + m * tiles * local + c % local
                flatten[pl.ds(at, tiles, stride=local), :] = o_loose[m, pl.ds(r, tiles, stride=frame_rows), :]
        if c % local == local - 1:
            out[c // local] = flatten[...].astype(jnp.bfloat16).reshape(frame_rows, count, LANES)

    for c in range(chains - 1):
        unpack(c)
    for e in range(1, group):
        w_copy(e).wait_recv()
    w_piece[...] = jnp.sum(w_recv[...].astype(jnp.float32), axis=0)
    for e in range(1, group):
        f_copy(e).start()
    w_full[rank] = w_piece[...]
    unpack(chains - 1)

    for e in range(1, group):
        f_copy(e).wait_recv()
    for k in range(group):
        ds[k * rows : (k + 1) * rows, :] = w_full[k]
    for t in range(12):
        both = ds[(t // 2) * chans : (t // 2 + 1) * chans, :]
        half = both[:, (t % 2) * chans : (t % 2 + 1) * chans]
        if t < 9:
            spatial[t] = half
        else:
            temporal[t - 9] = half

    def finish(c, carry):
        for d in range(1, tm):
            x_copy(c, d).wait_send()
            o_copy(c, d).wait_send()

        @pl.when(section == sections - 1)
        def _():
            for d in range(1, tm):
                g_copy(c, d).wait_send()

        @pl.when(section > 0)
        def _():
            z_copy(c).wait_send()

        return carry

    lax.fori_loop(0, chains, finish, 0)
    for e in range(1, group):
        w_copy(e).wait_send()
        f_copy(e).wait_send()


def tiled(a):
    micro, local, rows, width = a.shape
    a = a.reshape(micro, local, rows, width // LANES, LANES)
    return a.transpose(0, 2, 3, 1, 4).reshape(micro, rows, width // LANES * local, LANES)


def untiled(a, local):
    micro, rows, count, _ = a.shape
    a = a.reshape(micro, rows, count // local, local, LANES)
    return a.transpose(0, 3, 1, 2, 4).reshape(micro, local, rows, count // local * LANES)


def tile_plan(acts, cot, spatial_weight, temporal_weight):
    sections, tm, batches = [lax.axis_size(a) for a in ("section", "tm", "batch")]
    micro, local, rows, width = cot.shape
    chans = spatial_weight.shape[-1]
    chains = micro * local
    group = tm * batches
    tiles = width // LANES // tm
    pairs = tiles + 2 * HALO
    pairs += pairs % 2
    x_rows, g_rows, tile_rows = [-(-n * rows // 16) * 16 for n in (pairs, pairs - 2, tiles)]
    piece = 6 * chans // group
    bf16, f32 = jnp.bfloat16, jnp.float32
    vmem, dma = pltpu.VMEM, pltpu.SemaphoreType.DMA
    grad, spatial, temporal = pl.pallas_call(
        functools.partial(tile_kernel, sections, batches, tiles),
        out_shape=[
            jax.ShapeDtypeStruct((micro, rows, width // LANES * local, LANES), bf16),
            jax.ShapeDtypeStruct((9, chans, chans), f32),
            jax.ShapeDtypeStruct((3, chans, chans), f32),
        ],
        in_specs=[pl.BlockSpec(memory_space=vmem)] * 4,
        out_specs=[pl.BlockSpec(memory_space=vmem)] * 3,
        scratch_shapes=[
            vmem((tm, chains, x_rows, LANES), bf16),
            vmem((tm, chains, g_rows, LANES), bf16),
            vmem((chains, tm, x_rows, LANES), bf16),
            vmem((chains, tm, g_rows, LANES), bf16),
            vmem((chains, tm, g_rows, LANES), bf16),
            vmem((chains, tm, tile_rows, LANES), bf16),
            vmem((chains, tm, tile_rows, LANES), bf16),
            vmem((2 * LANES, 3 * LANES), bf16),
            vmem((LANES, 6 * LANES), bf16),
            vmem((LANES, 3 * LANES), bf16),
            vmem((2 * LANES, 3 * LANES), f32),
            vmem((LANES, 3 * LANES), f32),
            vmem((6 * chans, LANES), f32),
            vmem((group, piece, LANES), bf16),
            vmem((group, piece, LANES), bf16),
            vmem((piece, LANES), f32),
            vmem((group, piece, LANES), f32),
            vmem(((width // LANES + HALO + pairs) * rows + 16, LANES), f32),
            vmem((rows * width // LANES * local, LANES), f32),
            vmem((tm, x_rows, LANES), f32),
            vmem((tm, g_rows, LANES), f32),
            vmem((tm, tile_rows, LANES), f32),
            vmem((tm, pairs, ROWS, LANES), f32),
            vmem((tm, pairs, ROWS, LANES), f32),
            dma((2, chains, tm - 1)),
            dma((2, chains, tm - 1)),
            dma((2, chains)),
            dma((2, chains, tm - 1)),
            dma((2, group - 1)),
            dma((2, group - 1)),
        ],
        compiler_params=pltpu.CompilerParams(
            collective_id=0, has_side_effects=True, vmem_limit_bytes=56 * 2**20
        ),
    )(tiled(acts[0]), tiled(cot), spatial_weight[0], temporal_weight[0])
    return grad, spatial, temporal

STEP = 6
TILE = 8
EARLY = 4


def row_before(v):
    sub = lax.broadcasted_iota(jnp.int32, v[:, :1].shape, 2)
    first = jnp.where(sub >= ROWS // 2, pltpu.roll(v[:, -1:], ROWS // 2, 2), 0.0)
    return jnp.concatenate([first, v[:, :-1]], axis=1)


def row_after(v):
    sub = lax.broadcasted_iota(jnp.int32, v[:, :1].shape, 2)
    last = jnp.where(sub < ROWS // 2, pltpu.roll(v[:, :1], ROWS // 2, 2), 0.0)
    return jnp.concatenate([v[:, 1:], last], axis=1)


def beside(v):
    count = v.shape[0] - 2
    lane = lax.broadcasted_iota(jnp.int32, (count,) + v.shape[1:], 3)
    return jnp.where(lane < LANES // 2, v[2:], v[:-2])


def lanes(parts):
    return jnp.concatenate([flat(v).astype(jnp.bfloat16) for v in parts], axis=1)


def wide_weights(ws_ref, wt_ref, fwd, back, time):
    chans = ws_ref.shape[-1]
    zero = jnp.zeros((chans, chans), jnp.bfloat16)

    def grid(rows):
        return jnp.concatenate([jnp.concatenate(v, axis=1) for v in rows], axis=0)

    for i in range(3):
        a, b, c = [ws_ref[3 * i + j] for j in range(3)]
        at = slice(i * LANES, (i + 1) * LANES)
        fwd[:, at] = grid([[b, a], [c, b], [zero, c], [a, zero]])
        back[at, :] = grid([[b, a, zero, c], [c, b, a, zero]])
        time[:, at] = grid([[wt_ref[i], zero], [zero, wt_ref[i]]])


def folded(d, dt, chans):
    low = lax.broadcasted_iota(jnp.int32, (chans, LANES), 1) < chans

    def both(ref, i, a, b):
        at = slice(i * LANES, (i + 1) * LANES)
        v = jnp.where(low, ref[a * chans : (a + 1) * chans, at], ref[b * chans : (b + 1) * chans, at])
        return v + pltpu.roll(v, chans, 1)

    taps = [both(d, i, *rows) for i in range(3) for rows in ((3, 0), (0, 1), (1, 2))]
    return taps + [both(dt, k, 0, 1) for k in range(3)]


def chain_kernel(
    sections, batches, acts_hbm, cot_hbm, ws_hbm, wt_hbm, out, spatial, temporal,
    acts, cot, ws, wt, x_stage, g_stage, x_in, g_in, xw, gw, res, xs, hs, slopes, gs, ggs, g_buf, r_buf, o_stage, o_in,
    loose, fwd, back, time, acc, acc_t, ds, w_send, w_recv, w_piece, w_full,
    l_sem, x_sem, g_sem, z_sem, o_sem, w_sem, f_sem,
):
    micro, rows, count, _ = acts.shape
    tiles, tm = x_in.shape[:2]
    local = tm // micro
    steps = g_buf.shape[0]
    chans = ws.shape[-1]
    pair = rows * tm
    size = STEP * pair
    group = tm * batches
    section, me, core = [lax.axis_index(a) for a in ("section", "tm", "batch")]
    last = section == sections - 1
    busy = section >= sections - 2
    early = jnp.where(last, 1, jnp.where(busy, min(EARLY, steps), steps))
    lag = sections - 1 - section
    rank = me * batches + core

    def member(e):
        other = lax.rem(rank + e, group)
        return other, (section, other // batches, lax.rem(other, batches))

    def peer(d):
        other = lax.rem(me + d, tm)
        return other, (section, other, core)

    barrier = pltpu.get_barrier_semaphore()
    for e in range(1, group):
        pl.semaphore_signal(barrier, inc=1, device_id=member(e)[1], device_id_type=MESH)

    @pl.when(section > 0)
    def _():
        pl.semaphore_signal(barrier, inc=1, device_id=(section - 1, me, core), device_id_type=MESH)

    @pl.when(section < sections - 1)
    def _():
        pl.semaphore_signal(barrier, inc=1, device_id=(section + 1, me, core), device_id_type=MESH)

    loads = [
        pltpu.make_async_copy(a, b, l_sem.at[i])
        for i, (a, b) in enumerate([(acts_hbm, acts), (cot_hbm, cot), (ws_hbm, ws), (wt_hbm, wt)])
    ]
    loads[0].start()

    @pl.when(last)
    def _():
        loads[1].start()

    loads[2].start()
    loads[3].start()

    def copy(src, dst, sems, at, device):
        return pltpu.make_async_remote_copy(
            src_ref=src, dst_ref=dst, send_sem=sems.at[(0,) + at], recv_sem=sems.at[(1,) + at],
            device_id=device, device_id_type=MESH,
        )

    def x_copy(j, d):
        other, device = peer(d)
        return copy(x_stage.at[j, other], x_in.at[j, me], x_sem, (j, d - 1), device)

    def g_copy(j, d):
        other = peer(d)[0]
        return copy(g_stage.at[j, other], g_in.at[j, me], g_sem, (j, d - 1), (section, other, core))

    def z_copy(k):
        return copy(r_buf.at[k], g_buf.at[k], z_sem, (k,), (lax.max(section - 1, 0), me, core))

    def o_copy(j, d):
        other, device = peer(d)
        return copy(o_stage.at[j, other], o_in.at[j, me], o_sem, (j, d - 1), device)

    def w_copy(e):
        other, device = member(e)
        return copy(w_send.at[other], w_recv.at[rank], w_sem, (e - 1,), device)

    def f_copy(e):
        return copy(w_piece, w_full.at[rank], f_sem, (e - 1,), member(e)[1])

    def sub_of(r):
        return r % (rows // 2) * ROWS + r // (rows // 2) * tm

    span = TILE * local

    def pack(frames, stage, j):
        at = pl.ds(pl.multiple_of(span * j, span), span)
        for n in range(micro):
            for r in range(rows):
                loose[(n * rows + r) * span : (n * rows + r + 1) * span, :] = frames[n, r, at, :].astype(jnp.float32)
        for n in range(micro):
            for t in range(local):
                cut = [loose[pl.ds((n * rows + r) * span + t, TILE, stride=local), :] for r in range(rows)]
                stage[j, n * local + t] = jnp.concatenate(cut, axis=0).astype(jnp.bfloat16)

    def send(j, carry):
        @pl.when(last)
        def _():
            pack(cot, g_stage, j)
            for d in range(1, tm):
                g_copy(j, d).start()
            g_in[j, me] = g_stage[j, me]

        pack(acts, x_stage, j)
        for d in range(1, tm):
            x_copy(j, d).start()
        x_in[j, me] = x_stage[j, me]
        return carry

    more = (section > 0).astype(jnp.int32) + (section < sections - 1).astype(jnp.int32)
    pl.semaphore_wait(barrier, group - 1 + more)

    @pl.when(last)
    def _():
        loads[1].wait()

    loads[0].wait()
    lax.fori_loop(0, tiles, send, 0)
    xw[...] = jnp.zeros_like(xw)
    gw[...] = jnp.zeros_like(gw)
    acc[...] = jnp.zeros_like(acc)
    acc_t[...] = jnp.zeros_like(acc_t)
    loads[2].wait()
    loads[3].wait()
    wide_weights(ws, wt, fwd, back, time)

    def spread(tile, wide, base):
        for m in range(tm):
            v = tile[m].astype(jnp.float32)
            for r in range(rows):
                at = base + (sub_of(r) + m)
                wide[pl.ds(at, TILE, stride=pair), :] = v[TILE * r : TILE * (r + 1)]

    def land(j, carry):
        for d in range(1, tm):
            x_copy(j, d).wait_recv()
        spread(x_in[j], xw, (j * TILE + 1 + lag) * pair)

        @pl.when(last)
        def _():
            for d in range(1, tm):
                g_copy(j, d).wait_recv()
            spread(g_in[j], gw, (j * TILE + 1) * pair)

        return carry

    def wanted(k):
        return jnp.where(k < 0, 0, lax.min((STEP * (k + 1) + TILE) // TILE, tiles))

    def ready(k):
        return lax.max((STEP * (k + 1) + TILE - sections) // TILE - 1, 0)

    shape = (STEP, rows // 2, ROWS, LANES)
    sub = lax.broadcasted_iota(jnp.int32, shape, 2)
    bin_at = sub % tm

    def window(ref, first, many):
        at = pl.multiple_of(first * pair, ROWS)
        return ref[pl.ds(at, many * pair), :].reshape((many,) + shape[1:])

    def give(j, carry):
        third = rows // 2 * TILE
        for m in range(tm):
            at = [pl.multiple_of((j + 1) * TILE * pair + (a * tm + m) * third, TILE) for a in range(2)]
            cut = [res[pl.ds(i, third), :] for i in at]
            o_stage[j, m] = jnp.concatenate(cut, axis=0).astype(jnp.bfloat16)
        for d in range(1, tm):
            o_copy(j, d).start()
        o_in[j, me] = o_stage[j, me]
        return carry

    def ahead(k, carry):
        lax.fori_loop(wanted(k - 1), wanted(k), land, 0)
        x = window(xw, STEP * k, STEP + 2)
        xx = lanes([x[1:-1], beside(x)])
        y = mm(xx, fwd[...], ((1,), (0,)))
        part = [y[:, LANES * i : LANES * (i + 1)].reshape(shape) for i in range(3)]
        z = part[1] + row_before(part[0]) + row_after(part[2])
        sig = jax.nn.sigmoid(z)
        h = z * sig
        xs[k] = xx
        hs[k] = flat(h).astype(jnp.bfloat16)
        slopes[k] = flat(sig * (1.0 + z * (1.0 - sig)))
        return carry

    def grads(i, carry):
        two = pl.ds(2 * i, 2)
        acc_t[...] += mm(flat(hs[two]), flat(gs[two]), ((0,), (0,)))
        acc[...] += mm(flat(xs[two]), flat(ggs[two]), ((0,), (0,)))
        return carry

    def turn(k, tail):
        @pl.when(section < sections - 1)
        def _():
            z_copy(k).wait_recv()
            at = pl.multiple_of((STEP * k + 1) * pair, ROWS)
            gw[pl.ds(at, size), :] = g_buf[k].astype(jnp.float32)

        held = window(gw, STEP * k, STEP + 1)
        g = held[1:]
        after = jnp.where(bin_at < tm - 1, pltpu.roll(g, ROWS - 1, 2), 0.0)
        before = jnp.where(bin_at > 0, pltpu.roll(g, 1, 2), 0.0)
        g3 = lanes([after, g, before])
        gh = mm(g3, time[...], ((1,), (1,))).astype(jnp.bfloat16)
        gz = (gh.astype(jnp.float32) * slopes[k]).reshape(shape).astype(jnp.bfloat16)
        gz = gz.astype(jnp.float32)
        sent = jnp.concatenate([tail, gz], axis=0)
        y = mm(lanes([sent[1:-1], beside(sent)]), back[...], ((1,), (1,)))
        part = [y[:, LANES * i : LANES * (i + 1)].reshape(shape) for i in range(3)]
        inner = part[1] + row_after(part[0]) + row_before(part[2])
        first = STEP * k - lag - 1
        place = first + lax.broadcasted_iota(jnp.int32, shape, 0)
        inside = (place >= 0) & (place < TILE * tiles)
        result = jnp.where(inside, held[:-1] + inner, 0.0)
        r_buf[k] = flat(result).astype(jnp.bfloat16)

        @pl.when(section > 0)
        def _():
            z_copy(k).start()

        for i in range(STEP):
            q = first + TILE + i
            at = q // TILE * (TILE * pair) + q % TILE
            for b in range(rows // 2):
                res[pl.ds(at + b * TILE, ROWS, stride=rows // 2 * TILE), :] = result[i, b]

        lax.fori_loop(ready(k - 1), ready(k), give, 0)
        gs[k] = g3
        ggs[k] = lanes([row_after(gz), gz, row_before(gz)])

        @pl.when(busy & (k + early < steps))
        def _():
            ahead(k + early, 0)

        @pl.when(~busy & (k % 2 == 1))
        def _():
            grads(k // 2, 0)

        return gz[-2:]

    lax.fori_loop(0, early, ahead, 0)
    lax.fori_loop(0, steps, turn, jnp.zeros((2,) + shape[1:], jnp.float32))

    @pl.when(busy)
    def _():
        lax.fori_loop(0, steps // 2, grads, 0)

    taps = folded(acc, acc_t, chans)
    low = lax.broadcasted_iota(jnp.int32, taps[0].shape, 1) < chans
    for k in range(6):
        ds[k * chans : (k + 1) * chans, :] = jnp.where(low, taps[2 * k], taps[2 * k + 1])
    share = w_send.shape[1]
    for k in range(group):
        w_send[k] = ds[k * share : (k + 1) * share, :].astype(jnp.bfloat16)
    for e in range(1, group):
        w_copy(e).start()
    w_recv[rank] = w_send[rank]

    def unpack(j, carry):
        for d in range(1, tm):
            o_copy(j, d).wait_recv()
        for c in range(tm):
            v = o_in[j, c].astype(jnp.float32)
            for r in range(rows):
                at = (c // local * rows + r) * span + c % local
                loose[pl.ds(at, TILE, stride=local), :] = v[TILE * r : TILE * (r + 1)]
        at = pl.ds(pl.multiple_of(span * j, span), span)
        for n in range(micro):
            for r in range(rows):
                v = loose[(n * rows + r) * span : (n * rows + r + 1) * span, :]
                out[n, r, at, :] = v.astype(jnp.bfloat16)
        return carry

    lax.fori_loop(0, tiles - 2, unpack, 0)
    for e in range(1, group):
        w_copy(e).wait_recv()
    w_piece[...] = jnp.sum(w_recv[...].astype(jnp.float32), axis=0).astype(jnp.bfloat16)
    for e in range(1, group):
        f_copy(e).start()
    w_full[rank] = w_piece[...]
    lax.fori_loop(tiles - 2, tiles, unpack, 0)

    def finish(j, carry):
        for d in range(1, tm):
            x_copy(j, d).wait_send()
            o_copy(j, d).wait_send()

        @pl.when(last)
        def _():
            for d in range(1, tm):
                g_copy(j, d).wait_send()

        return carry

    lax.fori_loop(0, tiles, finish, 0)

    @pl.when(section > 0)
    def _():
        def sent(k, carry):
            z_copy(k).wait_send()
            return carry

        lax.fori_loop(0, steps, sent, 0)

    for e in range(1, group):
        w_copy(e).wait_send()
    for e in range(1, group):
        f_copy(e).wait_recv()
    for k in range(group):
        ds[k * share : (k + 1) * share, :] = w_full[k].astype(jnp.float32)
    for t in range(12):
        half = ds[(t // 2) * chans : (t // 2 + 1) * chans, (t % 2) * chans : (t % 2 + 1) * chans]
        if t < 9:
            spatial[t] = half
        else:
            temporal[t - 9] = half
    for e in range(1, group):
        f_copy(e).wait_send()


def chain_plan(acts, cot, spatial_weight, temporal_weight):
    sections, tm, batches = [lax.axis_size(a) for a in ("section", "tm", "batch")]
    micro, local, rows, width = cot.shape
    chans = spatial_weight.shape[-1]
    group = tm * batches
    count = width // LANES
    tiles = count // TILE
    steps = -(-(count + sections) // (2 * STEP)) * 2
    pair = rows * tm
    piece = 6 * chans // group
    bf16, f32 = jnp.bfloat16, jnp.float32
    vmem, dma = pltpu.VMEM, pltpu.SemaphoreType.DMA
    return pl.pallas_call(
        functools.partial(chain_kernel, sections, batches),
        out_shape=[
            vmem((micro, rows, count * local, LANES), bf16),
            vmem((9, chans, chans), f32),
            vmem((3, chans, chans), f32),
        ],
        in_specs=[pl.BlockSpec(memory_space=pl.ANY)] * 4,
        out_specs=[pl.BlockSpec(memory_space=vmem)] * 3,
        scratch_shapes=[
            vmem((micro, rows, count * local, LANES), bf16),
            vmem((micro, rows, count * local, LANES), bf16),
            vmem((9, chans, chans), bf16),
            vmem((3, chans, chans), bf16),
        ]
        + [vmem((tiles, tm, TILE * rows, LANES), bf16)] * 4
        + [
            vmem(((max(steps * STEP, count + sections) + 2) * pair, LANES), f32),
            vmem(((steps * STEP + 1) * pair, LANES), f32),
            vmem(((tiles + 2) * TILE * pair, LANES), f32),
            vmem((steps, STEP * pair, 2 * LANES), bf16),
            vmem((steps, STEP * pair, LANES), bf16),
            vmem((steps, STEP * pair, LANES), f32),
            vmem((steps, STEP * pair, 3 * LANES), bf16),
            vmem((steps, STEP * pair, 3 * LANES), bf16),
            vmem((steps, STEP * pair, LANES), bf16),
            vmem((steps, STEP * pair, LANES), bf16),
            vmem((tiles, tm, TILE * rows, LANES), bf16),
            vmem((tiles, tm, TILE * rows, LANES), bf16),
            vmem((micro * rows * TILE * local, LANES), f32),
            vmem((2 * LANES, 3 * LANES), bf16),
            vmem((3 * LANES, 2 * LANES), bf16),
            vmem((LANES, 3 * LANES), bf16),
            vmem((2 * LANES, 3 * LANES), f32),
            vmem((LANES, 3 * LANES), f32),
            vmem((6 * chans, LANES), f32),
            vmem((group, piece, LANES), bf16),
            vmem((group, piece, LANES), bf16),
            vmem((piece, LANES), bf16),
            vmem((group, piece, LANES), bf16),
            dma((4,)),
            dma((2, tiles, tm - 1)),
            dma((2, tiles, tm - 1)),
            dma((2, steps)),
            dma((2, tiles, tm - 1)),
            dma((2, group - 1)),
            dma((2, group - 1)),
        ],
        compiler_params=pltpu.CompilerParams(
            collective_id=0, has_side_effects=True, vmem_limit_bytes=56 * 2**20
        ),
    )(tiled(acts[0]), tiled(cot), spatial_weight[0], temporal_weight[0])


def hand_over(*refs):
    count = len(refs) // 2
    pieces = [(refs[0].at[n], refs[count].at[n]) for n in range(refs[0].shape[0])]
    pieces += [(refs[i], refs[count + i]) for i in range(1, count)]
    copies = [pltpu.make_async_copy(a, b, refs[-1].at[i]) for i, (a, b) in enumerate(pieces)]
    for c in copies:
        c.start()
    for c in copies:
        c.wait()


def settle(arrays):
    count = len(arrays)
    return pl.pallas_call(
        hand_over,
        out_shape=[jax.ShapeDtypeStruct(a.shape, a.dtype) for a in arrays],
        in_specs=[pl.BlockSpec(memory_space=pltpu.VMEM)] * count,
        out_specs=[pl.BlockSpec(memory_space=pl.ANY)] * count,
        scratch_shapes=[pltpu.SemaphoreType.DMA((arrays[0].shape[0] + count - 1,))],
    )(*[pltpu.with_memory_space_constraint(a, pltpu.VMEM) for a in arrays])


def body(acts, cot, spatial_weight, temporal_weight):
    tm, (micro, local, rows, width) = lax.axis_size("tm"), cot.shape
    one_chain_each = tm == micro * local and 2 * tm == ROWS
    whole = rows % 2 == 0 and width % (TILE * LANES) == 0 and TILE * local % 16 == 0 and TILE * rows % 16 == 0
    plan = chain_plan if one_chain_each and whole and local == DILATION else tile_plan
    grad, spatial, temporal = settle(plan(acts, cot, spatial_weight, temporal_weight))
    return untiled(grad, local)[None], spatial[None], temporal[None]


def solution(mesh):
    in_specs = (
        P("section", "batch", "tm", None, None),
        P("batch", "tm", None, None),
        P("section", None, None, None),
        P("section", None, None, None),
    )
    out_specs = (
        P("section", "batch", "tm", None, None),
        P("section", None, None, None),
        P("section", None, None, None),
    )
    return jax.shard_map(body, mesh=mesh, in_specs=in_specs, out_specs=out_specs, check_vma=False)
```

```python
import functools

import jax
import jax.numpy as jnp
from jax import lax
from jax.experimental import pallas as pl
from jax.experimental.pallas import tpu as pltpu
from jax.sharding import PartitionSpec as P

DILATION = 2
ROWS = 8
LANES = 128
HALO = 3
MESH = pl.DeviceIdType.MESH


def neighbours(x):
    none = jnp.zeros_like(x[:, :1])
    after = jnp.concatenate([x[:, 1:], none], axis=1)
    before = jnp.concatenate([none, x[:, :-1]], axis=1)
    lane = lax.broadcasted_iota(jnp.int32, x.shape, 3)
    return jnp.where(lane < LANES // 2, after, before)


def flat(x):
    return x.reshape(-1, x.shape[-1])


def mm(a, b, dims):
    return lax.dot_general(a, b, (dims, ((), ())), preferred_element_type=jnp.float32)


def taps_of(d, dt, chans):
    def block(a, r, i, b):
        at = i * LANES + b * chans
        return a[r * chans : (r + 1) * chans, at : at + chans]

    taps = []
    for i in range(3):
        taps.append(block(d, 0, i, 1) + block(d, 3, i, 0))
        taps.append(block(d, 0, i, 0) + block(d, 1, i, 1))
        taps.append(block(d, 1, i, 0) + block(d, 2, i, 1))
    for k in range(3):
        taps.append(block(dt, 0, k, 0) + block(dt, 1, k, 1))
    return taps


def set_weights(ws_ref, wt_ref, fwd, back, time):
    chans = ws_ref.shape[-1]
    zero = jnp.zeros((chans, chans), jnp.bfloat16)
    for i in range(3):
        a, b, c = [ws_ref[3 * i + j] for j in range(3)]
        at = slice(i * LANES, (i + 1) * LANES)
        rows = [[b, a], [c, b], [zero, c], [a, zero]]
        fwd[:, at] = jnp.concatenate([jnp.concatenate(v, axis=1) for v in rows], axis=0)
        at = slice(i * 2 * LANES, (i + 1) * 2 * LANES)
        rows = [[b, a, zero, c], [c, b, a, zero]]
        back[:, at] = jnp.concatenate([jnp.concatenate(v, axis=1) for v in rows], axis=0)
        at = slice(i * LANES, (i + 1) * LANES)
        rows = [[wt_ref[i], zero], [zero, wt_ref[i]]]
        time[:, at] = jnp.concatenate([jnp.concatenate(v, axis=1) for v in rows], axis=0)


def pack(frames, stage, c, tiles, line, flatten, skip):
    tm, size = stage.shape[0], stage.shape[2]
    rows, count = frames.shape[1], frames.shape[2]
    local = stage.shape[1] // frames.shape[0]
    pairs = count // local
    flatten[...] = frames[c // local].astype(jnp.float32).reshape(flatten.shape)
    for r in range(rows):
        at = r * count + c % local
        line[pl.ds(HALO * rows + r, pairs, stride=rows), :] = flatten[pl.ds(at, pairs, stride=local), :]
    for m in range(tm):
        at = (tiles * m + skip) * rows
        stage[m, c] = line[at : at + size, :].astype(jnp.bfloat16)


def spread(packed, loose, wide, rows, first, count):
    loose[...] = packed.astype(jnp.float32)
    for n in range(loose.shape[0]):
        for p in range(count):
            wide[n, first + p, 0:rows, :] = loose[n, rows * p : rows * (p + 1), :]


def tile_kernel(
    sections, batches, tiles, acts, cot, ws_ref, wt_ref, out, spatial, temporal,
    x_stage, g_stage, x_buf, g_buf, r_buf, o_buf, home, fwd, back, time, acc, acc_t, ds,
    w_send, w_recv, w_piece, w_full,
    line, flatten, x_loose, g_loose, o_loose, x_wide, g_wide,
    x_sem, g_sem, z_sem, o_sem, w_sem, f_sem,
):
    tm = x_stage.shape[0]
    micro, frame_rows, count, _ = acts.shape
    chains = x_stage.shape[1]
    local = chains // micro
    width = count // local * LANES
    chans = ws_ref.shape[-1]
    pairs = x_wide.shape[1]
    tile_rows = o_buf.shape[2]
    group = tm * batches
    section, me, core = [lax.axis_index(a) for a in ("section", "tm", "batch")]
    rank = me * batches + core

    def member(e):
        other = lax.rem(rank + e, group)
        return other, (section, other // batches, lax.rem(other, batches))

    def peer(d):
        other = lax.rem(me + d, tm)
        return other, (section, other, core)

    barrier = pltpu.get_barrier_semaphore()
    for e in range(1, group):
        pl.semaphore_signal(barrier, inc=1, device_id=member(e)[1], device_id_type=MESH)

    @pl.when(section > 0)
    def _():
        pl.semaphore_signal(barrier, inc=1, device_id=(section - 1, me, core), device_id_type=MESH)

    @pl.when(section < sections - 1)
    def _():
        pl.semaphore_signal(barrier, inc=1, device_id=(section + 1, me, core), device_id_type=MESH)

    def copy(src, dst, sems, at, device):
        return pltpu.make_async_remote_copy(
            src_ref=src, dst_ref=dst, send_sem=sems.at[(0,) + at], recv_sem=sems.at[(1,) + at],
            device_id=device, device_id_type=MESH,
        )

    def x_copy(c, d):
        other, device = peer(d)
        return copy(x_stage.at[other, c], x_buf.at[c, me], x_sem, (c, d - 1), device)

    def g_copy(c, d):
        other, device = peer(d)
        return copy(g_stage.at[other, c], g_buf.at[c, me], g_sem, (c, d - 1), device)

    def z_copy(c):
        return copy(r_buf.at[c], g_buf.at[c], z_sem, (c,), (lax.max(section - 1, 0), me, core))

    def o_copy(c, d):
        other, device = peer(d)
        return copy(o_buf.at[c, other], home.at[c, me], o_sem, (c, d - 1), device)

    def w_copy(e):
        other, device = member(e)
        return copy(w_send.at[other], w_recv.at[rank], w_sem, (e - 1,), device)

    def f_copy(e):
        return copy(w_piece, w_full.at[rank], f_sem, (e - 1,), member(e)[1])

    line[...] = jnp.zeros_like(line)
    x_wide[...] = jnp.zeros_like(x_wide)
    g_wide[...] = jnp.zeros_like(g_wide)
    g_loose[...] = jnp.zeros_like(g_loose)
    pack(acts, x_stage, 0, tiles, line, flatten, 0)

    @pl.when(section == sections - 1)
    def _():
        pack(cot, g_stage, 0, tiles, line, flatten, 1)

    more = (section > 0).astype(jnp.int32) + (section < sections - 1).astype(jnp.int32)
    pl.semaphore_wait(barrier, group - 1 + more)

    def send(c):
        if c > 0:
            pack(acts, x_stage, c, tiles, line, flatten, 0)

            @pl.when(section == sections - 1)
            def _():
                pack(cot, g_stage, c, tiles, line, flatten, 1)

        for d in range(1, tm):
            x_copy(c, d).start()
        x_buf[c, me] = x_stage[me, c]

        @pl.when(section == sections - 1)
        def _():
            for d in range(1, tm):
                g_copy(c, d).start()
            g_buf[c, me] = g_stage[me, c]

    for c in range(chains):
        send(c)
    set_weights(ws_ref, wt_ref, fwd, back, time)
    acc[...] = jnp.zeros_like(acc)
    acc_t[...] = jnp.zeros_like(acc_t)

    shape = (tm, pairs, ROWS, LANES)
    blank = jnp.zeros((1, pairs, ROWS, LANES), jnp.float32)
    centre = slice(HALO, HALO + tiles)

    def turn(c, carry):
        for d in range(1, tm):
            x_copy(c, d).wait_recv()
        spread(x_buf[c], x_loose, x_wide, frame_rows, 0, pairs)
        x = x_wide[...]
        xx = jnp.concatenate([x, neighbours(x)], axis=3)
        y = mm(flat(xx).astype(jnp.bfloat16), fwd[...], ((1,), (0,)))
        part = [y[:, LANES * i : LANES * (i + 1)].reshape(-1, ROWS, LANES) for i in range(3)]
        z = part[1] + pltpu.roll(part[0], 1, 1) + pltpu.roll(part[2], ROWS - 1, 1)
        z = z.reshape(shape)
        sig = jax.nn.sigmoid(z)
        h = z * sig
        slope = sig * (1.0 + z * (1.0 - sig))

        @pl.when(section == sections - 1)
        def _():
            for d in range(1, tm):
                g_copy(c, d).wait_recv()

        @pl.when(section < sections - 1)
        def _():
            z_copy(c).wait_recv()

        spread(g_buf[c], g_loose, g_wide, frame_rows, 1, pairs - 2)
        g = g_wide[...]
        g3 = jnp.concatenate(
            [
                jnp.concatenate([g[1:], blank], axis=0),
                g,
                jnp.concatenate([blank, g[:-1]], axis=0),
            ],
            axis=3,
        )
        gh = mm(flat(g3).astype(jnp.bfloat16), time[...], ((1,), (1,))).astype(jnp.bfloat16)
        gz = (gh.astype(jnp.float32).reshape(shape) * slope).astype(jnp.bfloat16)
        gz = gz.astype(jnp.float32)
        flat_gz = gz.reshape(-1, ROWS, LANES)
        gg = [
            pltpu.roll(flat_gz, ROWS - 1, 1).reshape(shape),
            gz,
            pltpu.roll(flat_gz, 1, 1).reshape(shape),
        ]
        sides = []
        for v in gg:
            sides += [v, neighbours(v)]
        sides = jnp.concatenate(sides, axis=3).astype(jnp.bfloat16)
        inner = mm(flat(sides), back[...], ((1,), (1,))).reshape(shape)
        place = me * tiles - HALO + lax.broadcasted_iota(jnp.int32, shape, 1)
        row = lax.broadcasted_iota(jnp.int32, shape, 2)
        inside = (place >= 0) & (place < width // LANES) & (row < frame_rows)
        result = jnp.where(inside, g + inner, 0.0)
        for n in range(tm):
            for p in range(pairs - 2):
                at = frame_rows * p
                g_loose[n, at : at + frame_rows, :] = result[n, p + 1, 0:frame_rows]
        r_buf[c] = g_loose[...].astype(jnp.bfloat16)

        @pl.when(section > 0)
        def _():
            z_copy(c).start()

        at = (HALO - 1) * frame_rows
        o_buf[c] = g_loose[:, at : at + tile_rows, :].astype(jnp.bfloat16)
        for d in range(1, tm):
            o_copy(c, d).start()
        home[c, me] = o_buf[c, me]
        hc = flat(h[:, centre]).astype(jnp.bfloat16)
        acc_t[...] += mm(hc, flat(g3[:, centre]).astype(jnp.bfloat16), ((0,), (0,)))
        gc = jnp.concatenate([v[:, centre] for v in gg], axis=3).astype(jnp.bfloat16)
        acc[...] += mm(flat(xx[:, centre]).astype(jnp.bfloat16), flat(gc), ((0,), (0,)))
        return carry

    lax.fori_loop(0, chains, turn, 0)

    taps = taps_of(acc[...], acc_t[...], chans)
    for k in range(6):
        ds[k * chans : (k + 1) * chans, :] = jnp.concatenate([taps[2 * k], taps[2 * k + 1]], axis=1)
    rows = w_send.shape[1]
    for k in range(group):
        w_send[k] = ds[k * rows : (k + 1) * rows, :].astype(jnp.bfloat16)
    for e in range(1, group):
        w_copy(e).start()
    w_recv[rank] = w_send[rank]

    def unpack(c):
        for d in range(1, tm):
            o_copy(c, d).wait_recv()
        o_loose[...] = home[c].astype(jnp.float32)
        for m in range(tm):
            for r in range(frame_rows):
                at = r * count + m * tiles * local + c % local
                flatten[pl.ds(at, tiles, stride=local), :] = o_loose[m, pl.ds(r, tiles, stride=frame_rows), :]
        if c % local == local - 1:
            out[c // local] = flatten[...].astype(jnp.bfloat16).reshape(frame_rows, count, LANES)

    for c in range(chains - 1):
        unpack(c)
    for e in range(1, group):
        w_copy(e).wait_recv()
    w_piece[...] = jnp.sum(w_recv[...].astype(jnp.float32), axis=0)
    for e in range(1, group):
        f_copy(e).start()
    w_full[rank] = w_piece[...]
    unpack(chains - 1)

    for e in range(1, group):
        f_copy(e).wait_recv()
    for k in range(group):
        ds[k * rows : (k + 1) * rows, :] = w_full[k]
    for t in range(12):
        both = ds[(t // 2) * chans : (t // 2 + 1) * chans, :]
        half = both[:, (t % 2) * chans : (t % 2 + 1) * chans]
        if t < 9:
            spatial[t] = half
        else:
            temporal[t - 9] = half

    def finish(c, carry):
        for d in range(1, tm):
            x_copy(c, d).wait_send()
            o_copy(c, d).wait_send()

        @pl.when(section == sections - 1)
        def _():
            for d in range(1, tm):
                g_copy(c, d).wait_send()

        @pl.when(section > 0)
        def _():
            z_copy(c).wait_send()

        return carry

    lax.fori_loop(0, chains, finish, 0)
    for e in range(1, group):
        w_copy(e).wait_send()
        f_copy(e).wait_send()


def tiled(a):
    micro, local, rows, width = a.shape
    a = a.reshape(micro, local, rows, width // LANES, LANES)
    return a.transpose(0, 2, 3, 1, 4).reshape(micro, rows, width // LANES * local, LANES)


def untiled(a, local):
    micro, rows, count, _ = a.shape
    a = a.reshape(micro, rows, count // local, local, LANES)
    return a.transpose(0, 3, 1, 2, 4).reshape(micro, local, rows, count // local * LANES)


def tile_plan(acts, cot, spatial_weight, temporal_weight):
    sections, tm, batches = [lax.axis_size(a) for a in ("section", "tm", "batch")]
    micro, local, rows, width = cot.shape
    chans = spatial_weight.shape[-1]
    chains = micro * local
    group = tm * batches
    tiles = width // LANES // tm
    pairs = tiles + 2 * HALO
    pairs += pairs % 2
    x_rows, g_rows, tile_rows = [-(-n * rows // 16) * 16 for n in (pairs, pairs - 2, tiles)]
    piece = 6 * chans // group
    bf16, f32 = jnp.bfloat16, jnp.float32
    vmem, dma = pltpu.VMEM, pltpu.SemaphoreType.DMA
    grad, spatial, temporal = pl.pallas_call(
        functools.partial(tile_kernel, sections, batches, tiles),
        out_shape=[
            jax.ShapeDtypeStruct((micro, rows, width // LANES * local, LANES), bf16),
            jax.ShapeDtypeStruct((9, chans, chans), f32),
            jax.ShapeDtypeStruct((3, chans, chans), f32),
        ],
        in_specs=[pl.BlockSpec(memory_space=vmem)] * 4,
        out_specs=[pl.BlockSpec(memory_space=vmem)] * 3,
        scratch_shapes=[
            vmem((tm, chains, x_rows, LANES), bf16),
            vmem((tm, chains, g_rows, LANES), bf16),
            vmem((chains, tm, x_rows, LANES), bf16),
            vmem((chains, tm, g_rows, LANES), bf16),
            vmem((chains, tm, g_rows, LANES), bf16),
            vmem((chains, tm, tile_rows, LANES), bf16),
            vmem((chains, tm, tile_rows, LANES), bf16),
            vmem((2 * LANES, 3 * LANES), bf16),
            vmem((LANES, 6 * LANES), bf16),
            vmem((LANES, 3 * LANES), bf16),
            vmem((2 * LANES, 3 * LANES), f32),
            vmem((LANES, 3 * LANES), f32),
            vmem((6 * chans, LANES), f32),
            vmem((group, piece, LANES), bf16),
            vmem((group, piece, LANES), bf16),
            vmem((piece, LANES), f32),
            vmem((group, piece, LANES), f32),
            vmem(((width // LANES + HALO + pairs) * rows + 16, LANES), f32),
            vmem((rows * width // LANES * local, LANES), f32),
            vmem((tm, x_rows, LANES), f32),
            vmem((tm, g_rows, LANES), f32),
            vmem((tm, tile_rows, LANES), f32),
            vmem((tm, pairs, ROWS, LANES), f32),
            vmem((tm, pairs, ROWS, LANES), f32),
            dma((2, chains, tm - 1)),
            dma((2, chains, tm - 1)),
            dma((2, chains)),
            dma((2, chains, tm - 1)),
            dma((2, group - 1)),
            dma((2, group - 1)),
        ],
        compiler_params=pltpu.CompilerParams(
            collective_id=0, has_side_effects=True, vmem_limit_bytes=56 * 2**20
        ),
    )(tiled(acts[0]), tiled(cot), spatial_weight[0], temporal_weight[0])
    return grad, spatial, temporal

STEP = 6
TILE = 8
EARLY = 4


def row_before(v):
    sub = lax.broadcasted_iota(jnp.int32, v[:, :1].shape, 2)
    first = jnp.where(sub >= ROWS // 2, pltpu.roll(v[:, -1:], ROWS // 2, 2), 0.0)
    return jnp.concatenate([first, v[:, :-1]], axis=1)


def row_after(v):
    sub = lax.broadcasted_iota(jnp.int32, v[:, :1].shape, 2)
    last = jnp.where(sub < ROWS // 2, pltpu.roll(v[:, :1], ROWS // 2, 2), 0.0)
    return jnp.concatenate([v[:, 1:], last], axis=1)


def beside(v):
    count = v.shape[0] - 2
    lane = lax.broadcasted_iota(jnp.int32, (count,) + v.shape[1:], 3)
    return jnp.where(lane < LANES // 2, v[2:], v[:-2])


def lanes(parts):
    return jnp.concatenate([flat(v).astype(jnp.bfloat16) for v in parts], axis=1)


def wide_weights(ws_ref, wt_ref, fwd, back, time):
    chans = ws_ref.shape[-1]
    zero = jnp.zeros((chans, chans), jnp.bfloat16)

    def grid(rows):
        return jnp.concatenate([jnp.concatenate(v, axis=1) for v in rows], axis=0)

    for i in range(3):
        a, b, c = [ws_ref[3 * i + j] for j in range(3)]
        at = slice(i * LANES, (i + 1) * LANES)
        fwd[:, at] = grid([[b, a], [c, b], [zero, c], [a, zero]])
        back[at, :] = grid([[b, a, zero, c], [c, b, a, zero]])
        time[:, at] = grid([[wt_ref[i], zero], [zero, wt_ref[i]]])


def folded(d, dt, chans):
    low = lax.broadcasted_iota(jnp.int32, (chans, LANES), 1) < chans

    def both(ref, i, a, b):
        at = slice(i * LANES, (i + 1) * LANES)
        v = jnp.where(low, ref[a * chans : (a + 1) * chans, at], ref[b * chans : (b + 1) * chans, at])
        return v + pltpu.roll(v, chans, 1)

    taps = [both(d, i, *rows) for i in range(3) for rows in ((3, 0), (0, 1), (1, 2))]
    return taps + [both(dt, k, 0, 1) for k in range(3)]


def chain_kernel(
    sections, batches, acts_hbm, cot_hbm, ws_hbm, wt_hbm, out, spatial, temporal,
    acts, cot, ws, wt, x_stage, g_stage, x_in, g_in, xw, gw, res, xs, hs, slopes, gs, ggs, g_buf, r_buf, o_stage, o_in,
    loose, fwd, back, time, acc, acc_t, ds, w_send, w_recv, w_piece, w_full,
    l_sem, x_sem, g_sem, z_sem, o_sem, w_sem, f_sem,
):
    micro, rows, count, _ = acts.shape
    tiles, tm = x_in.shape[:2]
    local = tm // micro
    steps = g_buf.shape[0]
    chans = ws.shape[-1]
    pair = rows * tm
    size = STEP * pair
    group = tm * batches
    section, me, core = [lax.axis_index(a) for a in ("section", "tm", "batch")]
    last = section == sections - 1
    busy = section >= sections - 2
    early = jnp.where(last, 1, jnp.where(busy, min(EARLY, steps), steps))
    lag = sections - 1 - section
    rank = me * batches + core

    def member(e):
        other = lax.rem(rank + e, group)
        return other, (section, other // batches, lax.rem(other, batches))

    def peer(d):
        other = lax.rem(me + d, tm)
        return other, (section, other, core)

    barrier = pltpu.get_barrier_semaphore()
    for e in range(1, group):
        pl.semaphore_signal(barrier, inc=1, device_id=member(e)[1], device_id_type=MESH)

    @pl.when(section > 0)
    def _():
        pl.semaphore_signal(barrier, inc=1, device_id=(section - 1, me, core), device_id_type=MESH)

    @pl.when(section < sections - 1)
    def _():
        pl.semaphore_signal(barrier, inc=1, device_id=(section + 1, me, core), device_id_type=MESH)

    loads = [
        pltpu.make_async_copy(a, b, l_sem.at[i])
        for i, (a, b) in enumerate([(acts_hbm, acts), (cot_hbm, cot), (ws_hbm, ws), (wt_hbm, wt)])
    ]
    loads[0].start()

    @pl.when(last)
    def _():
        loads[1].start()

    loads[2].start()
    loads[3].start()

    def copy(src, dst, sems, at, device):
        return pltpu.make_async_remote_copy(
            src_ref=src, dst_ref=dst, send_sem=sems.at[(0,) + at], recv_sem=sems.at[(1,) + at],
            device_id=device, device_id_type=MESH,
        )

    def x_copy(j, d):
        other, device = peer(d)
        return copy(x_stage.at[j, other], x_in.at[j, me], x_sem, (j, d - 1), device)

    def g_copy(j, d):
        other = peer(d)[0]
        return copy(g_stage.at[j, other], g_in.at[j, me], g_sem, (j, d - 1), (section, other, core))

    def z_copy(k):
        return copy(r_buf.at[k], g_buf.at[k], z_sem, (k,), (lax.max(section - 1, 0), me, core))

    def o_copy(j, d):
        other, device = peer(d)
        return copy(o_stage.at[j, other], o_in.at[j, me], o_sem, (j, d - 1), device)

    def w_copy(e):
        other, device = member(e)
        return copy(w_send.at[other], w_recv.at[rank], w_sem, (e - 1,), device)

    def f_copy(e):
        return copy(w_piece, w_full.at[rank], f_sem, (e - 1,), member(e)[1])

    def sub_of(r):
        return r % (rows // 2) * ROWS + r // (rows // 2) * tm

    span = TILE * local

    def pack(frames, stage, j):
        at = pl.ds(pl.multiple_of(span * j, span), span)
        for n in range(micro):
            for r in range(rows):
                loose[(n * rows + r) * span : (n * rows + r + 1) * span, :] = frames[n, r, at, :].astype(jnp.float32)
        for n in range(micro):
            for t in range(local):
                cut = [loose[pl.ds((n * rows + r) * span + t, TILE, stride=local), :] for r in range(rows)]
                stage[j, n * local + t] = jnp.concatenate(cut, axis=0).astype(jnp.bfloat16)

    def send(j, carry):
        @pl.when(last)
        def _():
            pack(cot, g_stage, j)
            for d in range(1, tm):
                g_copy(j, d).start()
            g_in[j, me] = g_stage[j, me]

        pack(acts, x_stage, j)
        for d in range(1, tm):
            x_copy(j, d).start()
        x_in[j, me] = x_stage[j, me]
        return carry

    more = (section > 0).astype(jnp.int32) + (section < sections - 1).astype(jnp.int32)
    pl.semaphore_wait(barrier, group - 1 + more)

    @pl.when(last)
    def _():
        loads[1].wait()

    loads[0].wait()
    lax.fori_loop(0, tiles, send, 0)
    xw[...] = jnp.zeros_like(xw)
    gw[...] = jnp.zeros_like(gw)
    acc[...] = jnp.zeros_like(acc)
    acc_t[...] = jnp.zeros_like(acc_t)
    loads[2].wait()
    loads[3].wait()
    wide_weights(ws, wt, fwd, back, time)

    def spread(tile, wide, base):
        for m in range(tm):
            v = tile[m].astype(jnp.float32)
            for r in range(rows):
                at = base + (sub_of(r) + m)
                wide[pl.ds(at, TILE, stride=pair), :] = v[TILE * r : TILE * (r + 1)]

    def land(j, carry):
        for d in range(1, tm):
            x_copy(j, d).wait_recv()
        spread(x_in[j], xw, (j * TILE + 1 + lag) * pair)

        @pl.when(last)
        def _():
            for d in range(1, tm):
                g_copy(j, d).wait_recv()
            spread(g_in[j], gw, (j * TILE + 1) * pair)

        return carry

    def wanted(k):
        return jnp.where(k < 0, 0, lax.min((STEP * (k + 1) + TILE) // TILE, tiles))

    def ready(k):
        return lax.max((STEP * (k + 1) + TILE - sections) // TILE - 1, 0)

    shape = (STEP, rows // 2, ROWS, LANES)
    sub = lax.broadcasted_iota(jnp.int32, shape, 2)
    bin_at = sub % tm

    def window(ref, first, many):
        at = pl.multiple_of(first * pair, ROWS)
        return ref[pl.ds(at, many * pair), :].reshape((many,) + shape[1:])

    def give(j, carry):
        third = rows // 2 * TILE
        for m in range(tm):
            at = [pl.multiple_of((j + 1) * TILE * pair + (a * tm + m) * third, TILE) for a in range(2)]
            cut = [res[pl.ds(i, third), :] for i in at]
            o_stage[j, m] = jnp.concatenate(cut, axis=0).astype(jnp.bfloat16)
        for d in range(1, tm):
            o_copy(j, d).start()
        o_in[j, me] = o_stage[j, me]
        return carry

    def ahead(k, carry):
        lax.fori_loop(wanted(k - 1), wanted(k), land, 0)
        x = window(xw, STEP * k, STEP + 2)
        xx = lanes([x[1:-1], beside(x)])
        y = mm(xx, fwd[...], ((1,), (0,)))
        part = [y[:, LANES * i : LANES * (i + 1)].reshape(shape) for i in range(3)]
        z = part[1] + row_before(part[0]) + row_after(part[2])
        sig = jax.nn.sigmoid(z)
        h = z * sig
        xs[k] = xx
        hs[k] = flat(h).astype(jnp.bfloat16)
        slopes[k] = flat(sig * (1.0 + z * (1.0 - sig)))
        return carry

    def grads(i, carry):
        two = pl.ds(2 * i, 2)
        acc_t[...] += mm(flat(hs[two]), flat(gs[two]), ((0,), (0,)))
        acc[...] += mm(flat(xs[two]), flat(ggs[two]), ((0,), (0,)))
        return carry

    def turn(k, tail):
        @pl.when(section < sections - 1)
        def _():
            z_copy(k).wait_recv()
            at = pl.multiple_of((STEP * k + 1) * pair, ROWS)
            gw[pl.ds(at, size), :] = g_buf[k].astype(jnp.float32)

        held = window(gw, STEP * k, STEP + 1)
        g = held[1:]
        after = jnp.where(bin_at < tm - 1, pltpu.roll(g, ROWS - 1, 2), 0.0)
        before = jnp.where(bin_at > 0, pltpu.roll(g, 1, 2), 0.0)
        g3 = lanes([after, g, before])
        gh = mm(g3, time[...], ((1,), (1,))).astype(jnp.bfloat16)
        gz = (gh.astype(jnp.float32) * slopes[k]).reshape(shape).astype(jnp.bfloat16)
        gz = gz.astype(jnp.float32)
        sent = jnp.concatenate([tail, gz], axis=0)
        y = mm(lanes([sent[1:-1], beside(sent)]), back[...], ((1,), (1,)))
        part = [y[:, LANES * i : LANES * (i + 1)].reshape(shape) for i in range(3)]
        inner = part[1] + row_after(part[0]) + row_before(part[2])
        first = STEP * k - lag - 1
        place = first + lax.broadcasted_iota(jnp.int32, shape, 0)
        inside = (place >= 0) & (place < TILE * tiles)
        result = jnp.where(inside, held[:-1] + inner, 0.0)
        r_buf[k] = flat(result).astype(jnp.bfloat16)

        @pl.when(section > 0)
        def _():
            z_copy(k).start()

        for i in range(STEP):
            q = first + TILE + i
            at = q // TILE * (TILE * pair) + q % TILE
            for b in range(rows // 2):
                res[pl.ds(at + b * TILE, ROWS, stride=rows // 2 * TILE), :] = result[i, b]

        lax.fori_loop(ready(k - 1), ready(k), give, 0)
        gs[k] = g3
        ggs[k] = lanes([row_after(gz), gz, row_before(gz)])

        @pl.when(busy & (k + early < steps))
        def _():
            ahead(k + early, 0)

        @pl.when(~busy & (k % 2 == 1))
        def _():
            grads(k // 2, 0)

        return gz[-2:]

    lax.fori_loop(0, early, ahead, 0)
    lax.fori_loop(0, steps, turn, jnp.zeros((2,) + shape[1:], jnp.float32))

    @pl.when(busy)
    def _():
        lax.fori_loop(0, steps // 2, grads, 0)

    taps = folded(acc, acc_t, chans)
    low = lax.broadcasted_iota(jnp.int32, taps[0].shape, 1) < chans
    for k in range(6):
        ds[k * chans : (k + 1) * chans, :] = jnp.where(low, taps[2 * k], taps[2 * k + 1])
    share = w_send.shape[1]
    for k in range(group):
        w_send[k] = ds[k * share : (k + 1) * share, :].astype(jnp.bfloat16)
    for e in range(1, group):
        w_copy(e).start()
    w_recv[rank] = w_send[rank]

    def unpack(j, carry):
        for d in range(1, tm):
            o_copy(j, d).wait_recv()
        for c in range(tm):
            v = o_in[j, c].astype(jnp.float32)
            for r in range(rows):
                at = (c // local * rows + r) * span + c % local
                loose[pl.ds(at, TILE, stride=local), :] = v[TILE * r : TILE * (r + 1)]
        at = pl.ds(pl.multiple_of(span * j, span), span)
        for n in range(micro):
            for r in range(rows):
                v = loose[(n * rows + r) * span : (n * rows + r + 1) * span, :]
                out[n, r, at, :] = v.astype(jnp.bfloat16)
        return carry

    lax.fori_loop(0, tiles - 2, unpack, 0)
    for e in range(1, group):
        w_copy(e).wait_recv()
    w_piece[...] = jnp.sum(w_recv[...].astype(jnp.float32), axis=0).astype(jnp.bfloat16)
    for e in range(1, group):
        f_copy(e).start()
    w_full[rank] = w_piece[...]
    lax.fori_loop(tiles - 2, tiles, unpack, 0)

    def finish(j, carry):
        for d in range(1, tm):
            x_copy(j, d).wait_send()
            o_copy(j, d).wait_send()

        @pl.when(last)
        def _():
            for d in range(1, tm):
                g_copy(j, d).wait_send()

        return carry

    lax.fori_loop(0, tiles, finish, 0)

    @pl.when(section > 0)
    def _():
        def sent(k, carry):
            z_copy(k).wait_send()
            return carry

        lax.fori_loop(0, steps, sent, 0)

    for e in range(1, group):
        w_copy(e).wait_send()
    for e in range(1, group):
        f_copy(e).wait_recv()
    for k in range(group):
        ds[k * share : (k + 1) * share, :] = w_full[k].astype(jnp.float32)
    for t in range(12):
        half = ds[(t // 2) * chans : (t // 2 + 1) * chans, (t % 2) * chans : (t % 2 + 1) * chans]
        if t < 9:
            spatial[t] = half
        else:
            temporal[t - 9] = half
    for e in range(1, group):
        f_copy(e).wait_send()


def chain_plan(acts, cot, spatial_weight, temporal_weight):
    sections, tm, batches = [lax.axis_size(a) for a in ("section", "tm", "batch")]
    micro, local, rows, width = cot.shape
    chans = spatial_weight.shape[-1]
    group = tm * batches
    count = width // LANES
    tiles = count // TILE
    steps = -(-(count + sections) // (2 * STEP)) * 2
    pair = rows * tm
    piece = 6 * chans // group
    bf16, f32 = jnp.bfloat16, jnp.float32
    vmem, dma = pltpu.VMEM, pltpu.SemaphoreType.DMA
    return pl.pallas_call(
        functools.partial(chain_kernel, sections, batches),
        out_shape=[
            vmem((micro, rows, count * local, LANES), bf16),
            vmem((9, chans, chans), f32),
            vmem((3, chans, chans), f32),
        ],
        in_specs=[pl.BlockSpec(memory_space=pl.ANY)] * 4,
        out_specs=[pl.BlockSpec(memory_space=vmem)] * 3,
        scratch_shapes=[
            vmem((micro, rows, count * local, LANES), bf16),
            vmem((micro, rows, count * local, LANES), bf16),
            vmem((9, chans, chans), bf16),
            vmem((3, chans, chans), bf16),
        ]
        + [vmem((tiles, tm, TILE * rows, LANES), bf16)] * 4
        + [
            vmem(((max(steps * STEP, count + sections) + 2) * pair, LANES), f32),
            vmem(((steps * STEP + 1) * pair, LANES), f32),
            vmem(((tiles + 3) * TILE * pair, LANES), f32),
            vmem((steps, STEP * pair, 2 * LANES), bf16),
            vmem((steps, STEP * pair, LANES), bf16),
            vmem((steps, STEP * pair, LANES), f32),
            vmem((steps, STEP * pair, 3 * LANES), bf16),
            vmem((steps, STEP * pair, 3 * LANES), bf16),
            vmem((steps, STEP * pair, LANES), bf16),
            vmem((steps, STEP * pair, LANES), bf16),
            vmem((tiles, tm, TILE * rows, LANES), bf16),
            vmem((tiles, tm, TILE * rows, LANES), bf16),
            vmem((micro * rows * TILE * local + ROWS, LANES), f32),
            vmem((2 * LANES, 3 * LANES), bf16),
            vmem((3 * LANES, 2 * LANES), bf16),
            vmem((LANES, 3 * LANES), bf16),
            vmem((2 * LANES, 3 * LANES), f32),
            vmem((LANES, 3 * LANES), f32),
            vmem((6 * chans, LANES), f32),
            vmem((group, piece, LANES), bf16),
            vmem((group, piece, LANES), bf16),
            vmem((piece, LANES), bf16),
            vmem((group, piece, LANES), bf16),
            dma((4,)),
            dma((2, tiles, tm - 1)),
            dma((2, tiles, tm - 1)),
            dma((2, steps)),
            dma((2, tiles, tm - 1)),
            dma((2, group - 1)),
            dma((2, group - 1)),
        ],
        compiler_params=pltpu.CompilerParams(
            collective_id=0, has_side_effects=True, vmem_limit_bytes=56 * 2**20
        ),
    )(tiled(acts[0]), tiled(cot), spatial_weight[0], temporal_weight[0])


def hand_over(*refs):
    count = len(refs) // 2
    pieces = [(refs[0].at[n], refs[count].at[n]) for n in range(refs[0].shape[0])]
    pieces += [(refs[i], refs[count + i]) for i in range(1, count)]
    copies = [pltpu.make_async_copy(a, b, refs[-1].at[i]) for i, (a, b) in enumerate(pieces)]
    for c in copies:
        c.start()
    for c in copies:
        c.wait()


def settle(arrays):
    count = len(arrays)
    return pl.pallas_call(
        hand_over,
        out_shape=[jax.ShapeDtypeStruct(a.shape, a.dtype) for a in arrays],
        in_specs=[pl.BlockSpec(memory_space=pltpu.VMEM)] * count,
        out_specs=[pl.BlockSpec(memory_space=pl.ANY)] * count,
        scratch_shapes=[pltpu.SemaphoreType.DMA((arrays[0].shape[0] + count - 1,))],
    )(*[pltpu.with_memory_space_constraint(a, pltpu.VMEM) for a in arrays])


def body(acts, cot, spatial_weight, temporal_weight):
    tm, (micro, local, rows, width) = lax.axis_size("tm"), cot.shape
    one_chain_each = tm == micro * local and 2 * tm == ROWS
    whole = rows % 2 == 0 and width % (TILE * LANES) == 0 and TILE * local % 16 == 0 and TILE * rows % 16 == 0
    plan = chain_plan if one_chain_each and whole and local == DILATION else tile_plan
    grad, spatial, temporal = settle(plan(acts, cot, spatial_weight, temporal_weight))
    return untiled(grad, local)[None], spatial[None], temporal[None]


def solution(mesh):
    in_specs = (
        P("section", "batch", "tm", None, None),
        P("batch", "tm", None, None),
        P("section", None, None, None),
        P("section", None, None, None),
    )
    out_specs = (
        P("section", "batch", "tm", None, None),
        P("section", None, None, None),
        P("section", None, None, None),
    )
    return jax.shard_map(body, mesh=mesh, in_specs=in_specs, out_specs=out_specs, check_vma=False)
```

```python
import functools

import jax
import jax.numpy as jnp
from jax import lax
from jax.experimental import pallas as pl
from jax.experimental.pallas import tpu as pltpu
from jax.sharding import PartitionSpec as P

DILATION = 2
ROWS = 8
LANES = 128
HALO = 3
MESH = pl.DeviceIdType.MESH


def neighbours(x):
    none = jnp.zeros_like(x[:, :1])
    after = jnp.concatenate([x[:, 1:], none], axis=1)
    before = jnp.concatenate([none, x[:, :-1]], axis=1)
    lane = lax.broadcasted_iota(jnp.int32, x.shape, 3)
    return jnp.where(lane < LANES // 2, after, before)


def flat(x):
    return x.reshape(-1, x.shape[-1])


def mm(a, b, dims):
    return lax.dot_general(a, b, (dims, ((), ())), preferred_element_type=jnp.float32)


def taps_of(d, dt, chans):
    def block(a, r, i, b):
        at = i * LANES + b * chans
        return a[r * chans : (r + 1) * chans, at : at + chans]

    taps = []
    for i in range(3):
        taps.append(block(d, 0, i, 1) + block(d, 3, i, 0))
        taps.append(block(d, 0, i, 0) + block(d, 1, i, 1))
        taps.append(block(d, 1, i, 0) + block(d, 2, i, 1))
    for k in range(3):
        taps.append(block(dt, 0, k, 0) + block(dt, 1, k, 1))
    return taps


def set_weights(ws_ref, wt_ref, fwd, back, time):
    chans = ws_ref.shape[-1]
    zero = jnp.zeros((chans, chans), jnp.bfloat16)
    for i in range(3):
        a, b, c = [ws_ref[3 * i + j] for j in range(3)]
        at = slice(i * LANES, (i + 1) * LANES)
        rows = [[b, a], [c, b], [zero, c], [a, zero]]
        fwd[:, at] = jnp.concatenate([jnp.concatenate(v, axis=1) for v in rows], axis=0)
        at = slice(i * 2 * LANES, (i + 1) * 2 * LANES)
        rows = [[b, a, zero, c], [c, b, a, zero]]
        back[:, at] = jnp.concatenate([jnp.concatenate(v, axis=1) for v in rows], axis=0)
        at = slice(i * LANES, (i + 1) * LANES)
        rows = [[wt_ref[i], zero], [zero, wt_ref[i]]]
        time[:, at] = jnp.concatenate([jnp.concatenate(v, axis=1) for v in rows], axis=0)


def pack(frames, stage, c, tiles, line, flatten, skip):
    tm, size = stage.shape[0], stage.shape[2]
    rows, count = frames.shape[1], frames.shape[2]
    local = stage.shape[1] // frames.shape[0]
    pairs = count // local
    flatten[...] = frames[c // local].astype(jnp.float32).reshape(flatten.shape)
    for r in range(rows):
        at = r * count + c % local
        line[pl.ds(HALO * rows + r, pairs, stride=rows), :] = flatten[pl.ds(at, pairs, stride=local), :]
    for m in range(tm):
        at = (tiles * m + skip) * rows
        stage[m, c] = line[at : at + size, :].astype(jnp.bfloat16)


def spread(packed, loose, wide, rows, first, count):
    loose[...] = packed.astype(jnp.float32)
    for n in range(loose.shape[0]):
        for p in range(count):
            wide[n, first + p, 0:rows, :] = loose[n, rows * p : rows * (p + 1), :]


def tile_kernel(
    sections, batches, tiles, acts, cot, ws_ref, wt_ref, out, spatial, temporal,
    x_stage, g_stage, x_buf, g_buf, r_buf, o_buf, home, fwd, back, time, acc, acc_t, ds,
    w_send, w_recv, w_piece, w_full,
    line, flatten, x_loose, g_loose, o_loose, x_wide, g_wide,
    x_sem, g_sem, z_sem, o_sem, w_sem, f_sem,
):
    tm = x_stage.shape[0]
    micro, frame_rows, count, _ = acts.shape
    chains = x_stage.shape[1]
    local = chains // micro
    width = count // local * LANES
    chans = ws_ref.shape[-1]
    pairs = x_wide.shape[1]
    tile_rows = o_buf.shape[2]
    group = tm * batches
    section, me, core = [lax.axis_index(a) for a in ("section", "tm", "batch")]
    rank = me * batches + core

    def member(e):
        other = lax.rem(rank + e, group)
        return other, (section, other // batches, lax.rem(other, batches))

    def peer(d):
        other = lax.rem(me + d, tm)
        return other, (section, other, core)

    barrier = pltpu.get_barrier_semaphore()
    for e in range(1, group):
        pl.semaphore_signal(barrier, inc=1, device_id=member(e)[1], device_id_type=MESH)

    @pl.when(section > 0)
    def _():
        pl.semaphore_signal(barrier, inc=1, device_id=(section - 1, me, core), device_id_type=MESH)

    @pl.when(section < sections - 1)
    def _():
        pl.semaphore_signal(barrier, inc=1, device_id=(section + 1, me, core), device_id_type=MESH)

    def copy(src, dst, sems, at, device):
        return pltpu.make_async_remote_copy(
            src_ref=src, dst_ref=dst, send_sem=sems.at[(0,) + at], recv_sem=sems.at[(1,) + at],
            device_id=device, device_id_type=MESH,
        )

    def x_copy(c, d):
        other, device = peer(d)
        return copy(x_stage.at[other, c], x_buf.at[c, me], x_sem, (c, d - 1), device)

    def g_copy(c, d):
        other, device = peer(d)
        return copy(g_stage.at[other, c], g_buf.at[c, me], g_sem, (c, d - 1), device)

    def z_copy(c):
        return copy(r_buf.at[c], g_buf.at[c], z_sem, (c,), (lax.max(section - 1, 0), me, core))

    def o_copy(c, d):
        other, device = peer(d)
        return copy(o_buf.at[c, other], home.at[c, me], o_sem, (c, d - 1), device)

    def w_copy(e):
        other, device = member(e)
        return copy(w_send.at[other], w_recv.at[rank], w_sem, (e - 1,), device)

    def f_copy(e):
        return copy(w_piece, w_full.at[rank], f_sem, (e - 1,), member(e)[1])

    line[...] = jnp.zeros_like(line)
    x_wide[...] = jnp.zeros_like(x_wide)
    g_wide[...] = jnp.zeros_like(g_wide)
    g_loose[...] = jnp.zeros_like(g_loose)
    pack(acts, x_stage, 0, tiles, line, flatten, 0)

    @pl.when(section == sections - 1)
    def _():
        pack(cot, g_stage, 0, tiles, line, flatten, 1)

    more = (section > 0).astype(jnp.int32) + (section < sections - 1).astype(jnp.int32)
    pl.semaphore_wait(barrier, group - 1 + more)

    def send(c):
        if c > 0:
            pack(acts, x_stage, c, tiles, line, flatten, 0)

            @pl.when(section == sections - 1)
            def _():
                pack(cot, g_stage, c, tiles, line, flatten, 1)

        for d in range(1, tm):
            x_copy(c, d).start()
        x_buf[c, me] = x_stage[me, c]

        @pl.when(section == sections - 1)
        def _():
            for d in range(1, tm):
                g_copy(c, d).start()
            g_buf[c, me] = g_stage[me, c]

    for c in range(chains):
        send(c)
    set_weights(ws_ref, wt_ref, fwd, back, time)
    acc[...] = jnp.zeros_like(acc)
    acc_t[...] = jnp.zeros_like(acc_t)

    shape = (tm, pairs, ROWS, LANES)
    blank = jnp.zeros((1, pairs, ROWS, LANES), jnp.float32)
    centre = slice(HALO, HALO + tiles)

    def turn(c, carry):
        for d in range(1, tm):
            x_copy(c, d).wait_recv()
        spread(x_buf[c], x_loose, x_wide, frame_rows, 0, pairs)
        x = x_wide[...]
        xx = jnp.concatenate([x, neighbours(x)], axis=3)
        y = mm(flat(xx).astype(jnp.bfloat16), fwd[...], ((1,), (0,)))
        part = [y[:, LANES * i : LANES * (i + 1)].reshape(-1, ROWS, LANES) for i in range(3)]
        z = part[1] + pltpu.roll(part[0], 1, 1) + pltpu.roll(part[2], ROWS - 1, 1)
        z = z.reshape(shape)
        sig = jax.nn.sigmoid(z)
        h = z * sig
        slope = sig * (1.0 + z * (1.0 - sig))

        @pl.when(section == sections - 1)
        def _():
            for d in range(1, tm):
                g_copy(c, d).wait_recv()

        @pl.when(section < sections - 1)
        def _():
            z_copy(c).wait_recv()

        spread(g_buf[c], g_loose, g_wide, frame_rows, 1, pairs - 2)
        g = g_wide[...]
        g3 = jnp.concatenate(
            [
                jnp.concatenate([g[1:], blank], axis=0),
                g,
                jnp.concatenate([blank, g[:-1]], axis=0),
            ],
            axis=3,
        )
        gh = mm(flat(g3).astype(jnp.bfloat16), time[...], ((1,), (1,))).astype(jnp.bfloat16)
        gz = (gh.astype(jnp.float32).reshape(shape) * slope).astype(jnp.bfloat16)
        gz = gz.astype(jnp.float32)
        flat_gz = gz.reshape(-1, ROWS, LANES)
        gg = [
            pltpu.roll(flat_gz, ROWS - 1, 1).reshape(shape),
            gz,
            pltpu.roll(flat_gz, 1, 1).reshape(shape),
        ]
        sides = []
        for v in gg:
            sides += [v, neighbours(v)]
        sides = jnp.concatenate(sides, axis=3).astype(jnp.bfloat16)
        inner = mm(flat(sides), back[...], ((1,), (1,))).reshape(shape)
        place = me * tiles - HALO + lax.broadcasted_iota(jnp.int32, shape, 1)
        row = lax.broadcasted_iota(jnp.int32, shape, 2)
        inside = (place >= 0) & (place < width // LANES) & (row < frame_rows)
        result = jnp.where(inside, g + inner, 0.0)
        for n in range(tm):
            for p in range(pairs - 2):
                at = frame_rows * p
                g_loose[n, at : at + frame_rows, :] = result[n, p + 1, 0:frame_rows]
        r_buf[c] = g_loose[...].astype(jnp.bfloat16)

        @pl.when(section > 0)
        def _():
            z_copy(c).start()

        at = (HALO - 1) * frame_rows
        o_buf[c] = g_loose[:, at : at + tile_rows, :].astype(jnp.bfloat16)
        for d in range(1, tm):
            o_copy(c, d).start()
        home[c, me] = o_buf[c, me]
        hc = flat(h[:, centre]).astype(jnp.bfloat16)
        acc_t[...] += mm(hc, flat(g3[:, centre]).astype(jnp.bfloat16), ((0,), (0,)))
        gc = jnp.concatenate([v[:, centre] for v in gg], axis=3).astype(jnp.bfloat16)
        acc[...] += mm(flat(xx[:, centre]).astype(jnp.bfloat16), flat(gc), ((0,), (0,)))
        return carry

    lax.fori_loop(0, chains, turn, 0)

    taps = taps_of(acc[...], acc_t[...], chans)
    for k in range(6):
        ds[k * chans : (k + 1) * chans, :] = jnp.concatenate([taps[2 * k], taps[2 * k + 1]], axis=1)
    rows = w_send.shape[1]
    for k in range(group):
        w_send[k] = ds[k * rows : (k + 1) * rows, :].astype(jnp.bfloat16)
    for e in range(1, group):
        w_copy(e).start()
    w_recv[rank] = w_send[rank]

    def unpack(c):
        for d in range(1, tm):
            o_copy(c, d).wait_recv()
        o_loose[...] = home[c].astype(jnp.float32)
        for m in range(tm):
            for r in range(frame_rows):
                at = r * count + m * tiles * local + c % local
                flatten[pl.ds(at, tiles, stride=local), :] = o_loose[m, pl.ds(r, tiles, stride=frame_rows), :]
        if c % local == local - 1:
            out[c // local] = flatten[...].astype(jnp.bfloat16).reshape(frame_rows, count, LANES)

    for c in range(chains - 1):
        unpack(c)
    for e in range(1, group):
        w_copy(e).wait_recv()
    w_piece[...] = jnp.sum(w_recv[...].astype(jnp.float32), axis=0)
    for e in range(1, group):
        f_copy(e).start()
    w_full[rank] = w_piece[...]
    unpack(chains - 1)

    for e in range(1, group):
        f_copy(e).wait_recv()
    for k in range(group):
        ds[k * rows : (k + 1) * rows, :] = w_full[k]
    for t in range(12):
        both = ds[(t // 2) * chans : (t // 2 + 1) * chans, :]
        half = both[:, (t % 2) * chans : (t % 2 + 1) * chans]
        if t < 9:
            spatial[t] = half
        else:
            temporal[t - 9] = half

    def finish(c, carry):
        for d in range(1, tm):
            x_copy(c, d).wait_send()
            o_copy(c, d).wait_send()

        @pl.when(section == sections - 1)
        def _():
            for d in range(1, tm):
                g_copy(c, d).wait_send()

        @pl.when(section > 0)
        def _():
            z_copy(c).wait_send()

        return carry

    lax.fori_loop(0, chains, finish, 0)
    for e in range(1, group):
        w_copy(e).wait_send()
        f_copy(e).wait_send()


def tiled(a):
    micro, local, rows, width = a.shape
    a = a.reshape(micro, local, rows, width // LANES, LANES)
    return a.transpose(0, 2, 3, 1, 4).reshape(micro, rows, width // LANES * local, LANES)


def untiled(a, local):
    micro, rows, count, _ = a.shape
    a = a.reshape(micro, rows, count // local, local, LANES)
    return a.transpose(0, 3, 1, 2, 4).reshape(micro, local, rows, count // local * LANES)


def tile_plan(acts, cot, spatial_weight, temporal_weight):
    sections, tm, batches = [lax.axis_size(a) for a in ("section", "tm", "batch")]
    micro, local, rows, width = cot.shape
    chans = spatial_weight.shape[-1]
    chains = micro * local
    group = tm * batches
    tiles = width // LANES // tm
    pairs = tiles + 2 * HALO
    pairs += pairs % 2
    x_rows, g_rows, tile_rows = [-(-n * rows // 16) * 16 for n in (pairs, pairs - 2, tiles)]
    piece = 6 * chans // group
    bf16, f32 = jnp.bfloat16, jnp.float32
    vmem, dma = pltpu.VMEM, pltpu.SemaphoreType.DMA
    grad, spatial, temporal = pl.pallas_call(
        functools.partial(tile_kernel, sections, batches, tiles),
        out_shape=[
            jax.ShapeDtypeStruct((micro, rows, width // LANES * local, LANES), bf16),
            jax.ShapeDtypeStruct((9, chans, chans), f32),
            jax.ShapeDtypeStruct((3, chans, chans), f32),
        ],
        in_specs=[pl.BlockSpec(memory_space=vmem)] * 4,
        out_specs=[pl.BlockSpec(memory_space=vmem)] * 3,
        scratch_shapes=[
            vmem((tm, chains, x_rows, LANES), bf16),
            vmem((tm, chains, g_rows, LANES), bf16),
            vmem((chains, tm, x_rows, LANES), bf16),
            vmem((chains, tm, g_rows, LANES), bf16),
            vmem((chains, tm, g_rows, LANES), bf16),
            vmem((chains, tm, tile_rows, LANES), bf16),
            vmem((chains, tm, tile_rows, LANES), bf16),
            vmem((2 * LANES, 3 * LANES), bf16),
            vmem((LANES, 6 * LANES), bf16),
            vmem((LANES, 3 * LANES), bf16),
            vmem((2 * LANES, 3 * LANES), f32),
            vmem((LANES, 3 * LANES), f32),
            vmem((6 * chans, LANES), f32),
            vmem((group, piece, LANES), bf16),
            vmem((group, piece, LANES), bf16),
            vmem((piece, LANES), f32),
            vmem((group, piece, LANES), f32),
            vmem(((width // LANES + HALO + pairs) * rows + 16, LANES), f32),
            vmem((rows * width // LANES * local, LANES), f32),
            vmem((tm, x_rows, LANES), f32),
            vmem((tm, g_rows, LANES), f32),
            vmem((tm, tile_rows, LANES), f32),
            vmem((tm, pairs, ROWS, LANES), f32),
            vmem((tm, pairs, ROWS, LANES), f32),
            dma((2, chains, tm - 1)),
            dma((2, chains, tm - 1)),
            dma((2, chains)),
            dma((2, chains, tm - 1)),
            dma((2, group - 1)),
            dma((2, group - 1)),
        ],
        compiler_params=pltpu.CompilerParams(
            collective_id=0, has_side_effects=True, vmem_limit_bytes=56 * 2**20
        ),
    )(tiled(acts[0]), tiled(cot), spatial_weight[0], temporal_weight[0])
    return grad, spatial, temporal

STEP = 6
TILE = 8
EARLY = 4


def row_before(v):
    sub = lax.broadcasted_iota(jnp.int32, v[:, :1].shape, 2)
    first = jnp.where(sub >= ROWS // 2, pltpu.roll(v[:, -1:], ROWS // 2, 2), 0.0)
    return jnp.concatenate([first, v[:, :-1]], axis=1)


def row_after(v):
    sub = lax.broadcasted_iota(jnp.int32, v[:, :1].shape, 2)
    last = jnp.where(sub < ROWS // 2, pltpu.roll(v[:, :1], ROWS // 2, 2), 0.0)
    return jnp.concatenate([v[:, 1:], last], axis=1)


def beside(v):
    count = v.shape[0] - 2
    lane = lax.broadcasted_iota(jnp.int32, (count,) + v.shape[1:], 3)
    return jnp.where(lane < LANES // 2, v[2:], v[:-2])


def lanes(parts):
    return jnp.concatenate([flat(v).astype(jnp.bfloat16) for v in parts], axis=1)


def wide_weights(ws_ref, wt_ref, fwd, back, time):
    chans = ws_ref.shape[-1]
    zero = jnp.zeros((chans, chans), jnp.bfloat16)

    def grid(rows):
        return jnp.concatenate([jnp.concatenate(v, axis=1) for v in rows], axis=0)

    for i in range(3):
        a, b, c = [ws_ref[3 * i + j] for j in range(3)]
        at = slice(i * LANES, (i + 1) * LANES)
        fwd[:, at] = grid([[b, a], [c, b], [zero, c], [a, zero]])
        back[at, :] = grid([[b, a, zero, c], [c, b, a, zero]])
        time[:, at] = grid([[wt_ref[i], zero], [zero, wt_ref[i]]])


def folded(d, dt, chans):
    low = lax.broadcasted_iota(jnp.int32, (chans, LANES), 1) < chans

    def both(ref, i, a, b):
        at = slice(i * LANES, (i + 1) * LANES)
        v = jnp.where(low, ref[a * chans : (a + 1) * chans, at], ref[b * chans : (b + 1) * chans, at])
        return v + pltpu.roll(v, chans, 1)

    taps = [both(d, i, *rows) for i in range(3) for rows in ((3, 0), (0, 1), (1, 2))]
    return taps + [both(dt, k, 0, 1) for k in range(3)]


def chain_kernel(
    sections, batches, acts_hbm, cot_hbm, ws_hbm, wt_hbm, out, spatial, temporal,
    acts, cot, ws, wt, x_stage, g_stage, x_in, g_in, xw, gw, res, xs, hs, slopes, gs, ggs, g_buf, r_buf, o_stage, o_in,
    loose, fwd, back, time, acc, acc_t, ds, w_send, w_recv, w_piece, w_full,
    l_sem, x_sem, g_sem, z_sem, o_sem, w_sem, f_sem,
):
    micro, rows, count, _ = acts.shape
    tiles, tm = x_in.shape[:2]
    local = tm // micro
    steps = g_buf.shape[0]
    chans = ws.shape[-1]
    pair = rows * tm
    size = STEP * pair
    group = tm * batches
    section, me, core = [lax.axis_index(a) for a in ("section", "tm", "batch")]
    last = section == sections - 1
    busy = section >= sections - 2
    early = jnp.where(last, 1, jnp.where(busy, min(EARLY, steps), steps))
    lag = sections - 1 - section
    rank = me * batches + core

    def member(e):
        other = lax.rem(rank + e, group)
        return other, (section, other // batches, lax.rem(other, batches))

    def peer(d):
        other = lax.rem(me + d, tm)
        return other, (section, other, core)

    barrier = pltpu.get_barrier_semaphore()
    for e in range(1, group):
        pl.semaphore_signal(barrier, inc=1, device_id=member(e)[1], device_id_type=MESH)

    @pl.when(section > 0)
    def _():
        pl.semaphore_signal(barrier, inc=1, device_id=(section - 1, me, core), device_id_type=MESH)

    @pl.when(section < sections - 1)
    def _():
        pl.semaphore_signal(barrier, inc=1, device_id=(section + 1, me, core), device_id_type=MESH)

    loads = [
        pltpu.make_async_copy(a, b, l_sem.at[i])
        for i, (a, b) in enumerate([(acts_hbm, acts), (cot_hbm, cot), (ws_hbm, ws), (wt_hbm, wt)])
    ]
    loads[0].start()

    @pl.when(last)
    def _():
        loads[1].start()

    loads[2].start()
    loads[3].start()

    def copy(src, dst, sems, at, device):
        return pltpu.make_async_remote_copy(
            src_ref=src, dst_ref=dst, send_sem=sems.at[(0,) + at], recv_sem=sems.at[(1,) + at],
            device_id=device, device_id_type=MESH,
        )

    def x_copy(j, d):
        other, device = peer(d)
        return copy(x_stage.at[j, other], x_in.at[j, me], x_sem, (j, d - 1), device)

    def g_copy(j, d):
        other = peer(d)[0]
        return copy(g_stage.at[j, other], g_in.at[j, me], g_sem, (j, d - 1), (section, other, core))

    def z_copy(k):
        return copy(r_buf.at[k], g_buf.at[k], z_sem, (k,), (lax.max(section - 1, 0), me, core))

    def o_copy(j, d):
        other, device = peer(d)
        return copy(o_stage.at[j, other], o_in.at[j, me], o_sem, (j, d - 1), device)

    def w_copy(e):
        other, device = member(e)
        return copy(w_send.at[other], w_recv.at[rank], w_sem, (e - 1,), device)

    def f_copy(e):
        return copy(w_piece, w_full.at[rank], f_sem, (e - 1,), member(e)[1])

    def sub_of(r):
        return r % (rows // 2) * ROWS + r // (rows // 2) * tm

    span = TILE * local

    def pack(frames, stage, j):
        at = pl.ds(pl.multiple_of(span * j, span), span)
        for n in range(micro):
            for r in range(rows):
                loose[(n * rows + r) * span : (n * rows + r + 1) * span, :] = frames[n, r, at, :].astype(jnp.float32)
        for n in range(micro):
            for t in range(local):
                cut = [loose[pl.ds((n * rows + r) * span + t, TILE, stride=local), :] for r in range(rows)]
                stage[j, n * local + t] = jnp.concatenate(cut, axis=0).astype(jnp.bfloat16)

    def fill(j, carry):
        @pl.when(last)
        def _():
            pack(cot, g_stage, j)

        pack(acts, x_stage, j)
        return carry

    def send(j, carry):
        @pl.when(last)
        def _():
            for d in range(1, tm):
                g_copy(j, d).start()
            g_in[j, me] = g_stage[j, me]

        for d in range(1, tm):
            x_copy(j, d).start()
        x_in[j, me] = x_stage[j, me]
        return carry

    def fill_and_send(j, carry):
        return send(j, fill(j, carry))

    @pl.when(last)
    def _():
        loads[1].wait()

    loads[0].wait()
    first = min(4, tiles)
    lax.fori_loop(0, first, fill, 0)
    more = (section > 0).astype(jnp.int32) + (section < sections - 1).astype(jnp.int32)
    pl.semaphore_wait(barrier, group - 1 + more)
    lax.fori_loop(0, first, send, 0)
    lax.fori_loop(first, tiles, fill_and_send, 0)
    xw[...] = jnp.zeros_like(xw)
    gw[...] = jnp.zeros_like(gw)
    acc[...] = jnp.zeros_like(acc)
    acc_t[...] = jnp.zeros_like(acc_t)
    loads[2].wait()
    loads[3].wait()
    wide_weights(ws, wt, fwd, back, time)

    def spread(tile, wide, base):
        for m in range(tm):
            v = tile[m].astype(jnp.float32)
            for r in range(rows):
                at = base + (sub_of(r) + m)
                wide[pl.ds(at, TILE, stride=pair), :] = v[TILE * r : TILE * (r + 1)]

    def land(j, carry):
        for d in range(1, tm):
            x_copy(j, d).wait_recv()
        spread(x_in[j], xw, (j * TILE + 1 + lag) * pair)

        @pl.when(last)
        def _():
            for d in range(1, tm):
                g_copy(j, d).wait_recv()
            spread(g_in[j], gw, (j * TILE + 1) * pair)

        return carry

    def wanted(k):
        return jnp.where(k < 0, 0, lax.min((STEP * (k + 1) + TILE) // TILE, tiles))

    def ready(k):
        return lax.max((STEP * (k + 1) + TILE - sections) // TILE - 1, 0)

    shape = (STEP, rows // 2, ROWS, LANES)
    sub = lax.broadcasted_iota(jnp.int32, shape, 2)
    bin_at = sub % tm

    def window(ref, first, many):
        at = pl.multiple_of(first * pair, ROWS)
        return ref[pl.ds(at, many * pair), :].reshape((many,) + shape[1:])

    def give(j, carry):
        third = rows // 2 * TILE
        for m in range(tm):
            at = [pl.multiple_of((j + 1) * TILE * pair + (a * tm + m) * third, TILE) for a in range(2)]
            cut = [res[pl.ds(i, third), :] for i in at]
            o_stage[j, m] = jnp.concatenate(cut, axis=0).astype(jnp.bfloat16)
        for d in range(1, tm):
            o_copy(j, d).start()
        o_in[j, me] = o_stage[j, me]
        return carry

    def ahead(k, carry):
        lax.fori_loop(wanted(k - 1), wanted(k), land, 0)
        x = window(xw, STEP * k, STEP + 2)
        xx = lanes([x[1:-1], beside(x)])
        y = mm(xx, fwd[...], ((1,), (0,)))
        part = [y[:, LANES * i : LANES * (i + 1)].reshape(shape) for i in range(3)]
        z = part[1] + row_before(part[0]) + row_after(part[2])
        sig = jax.nn.sigmoid(z)
        h = z * sig
        xs[k] = xx
        hs[k] = flat(h).astype(jnp.bfloat16)
        slopes[k] = flat(sig * (1.0 + z * (1.0 - sig)))
        return carry

    def grads(i, carry):
        two = pl.ds(2 * i, 2)
        acc_t[...] += mm(flat(hs[two]), flat(gs[two]), ((0,), (0,)))
        acc[...] += mm(flat(xs[two]), flat(ggs[two]), ((0,), (0,)))
        return carry

    def turn(k, tail):
        @pl.when(section < sections - 1)
        def _():
            z_copy(k).wait_recv()
            at = pl.multiple_of((STEP * k + 1) * pair, ROWS)
            gw[pl.ds(at, size), :] = g_buf[k].astype(jnp.float32)

        held = window(gw, STEP * k, STEP + 1)
        g = held[1:]
        after = jnp.where(bin_at < tm - 1, pltpu.roll(g, ROWS - 1, 2), 0.0)
        before = jnp.where(bin_at > 0, pltpu.roll(g, 1, 2), 0.0)
        g3 = lanes([after, g, before])
        gh = mm(g3, time[...], ((1,), (1,))).astype(jnp.bfloat16)
        gz = (gh.astype(jnp.float32) * slopes[k]).reshape(shape).astype(jnp.bfloat16)
        gz = gz.astype(jnp.float32)
        sent = jnp.concatenate([tail, gz], axis=0)
        y = mm(lanes([sent[1:-1], beside(sent)]), back[...], ((1,), (1,)))
        part = [y[:, LANES * i : LANES * (i + 1)].reshape(shape) for i in range(3)]
        inner = part[1] + row_after(part[0]) + row_before(part[2])
        first = STEP * k - lag - 1
        place = first + lax.broadcasted_iota(jnp.int32, shape, 0)
        inside = (place >= 0) & (place < TILE * tiles)
        result = jnp.where(inside, held[:-1] + inner, 0.0)
        r_buf[k] = flat(result).astype(jnp.bfloat16)

        @pl.when(section > 0)
        def _():
            z_copy(k).start()

        for i in range(STEP):
            q = first + TILE + i
            at = q // TILE * (TILE * pair) + q % TILE
            for b in range(rows // 2):
                res[pl.ds(at + b * TILE, ROWS, stride=rows // 2 * TILE), :] = result[i, b]

        lax.fori_loop(ready(k - 1), ready(k), give, 0)
        gs[k] = g3
        ggs[k] = lanes([row_after(gz), gz, row_before(gz)])

        @pl.when(busy & (k + early < steps))
        def _():
            ahead(k + early, 0)

        @pl.when(~busy & (k % 2 == 1))
        def _():
            grads(k // 2, 0)

        return gz[-2:]

    lax.fori_loop(0, early, ahead, 0)
    lax.fori_loop(0, steps, turn, jnp.zeros((2,) + shape[1:], jnp.float32))

    @pl.when(busy)
    def _():
        lax.fori_loop(0, steps // 2, grads, 0)

    taps = folded(acc, acc_t, chans)
    low = lax.broadcasted_iota(jnp.int32, taps[0].shape, 1) < chans
    for k in range(6):
        ds[k * chans : (k + 1) * chans, :] = jnp.where(low, taps[2 * k], taps[2 * k + 1])
    share = w_send.shape[1]
    for k in range(group):
        w_send[k] = ds[k * share : (k + 1) * share, :].astype(jnp.bfloat16)
    for e in range(1, group):
        w_copy(e).start()
    w_recv[rank] = w_send[rank]

    def unpack(j, carry):
        for d in range(1, tm):
            o_copy(j, d).wait_recv()
        for c in range(tm):
            v = o_in[j, c].astype(jnp.float32)
            for r in range(rows):
                at = (c // local * rows + r) * span + c % local
                loose[pl.ds(at, TILE, stride=local), :] = v[TILE * r : TILE * (r + 1)]
        at = pl.ds(pl.multiple_of(span * j, span), span)
        for n in range(micro):
            for r in range(rows):
                v = loose[(n * rows + r) * span : (n * rows + r + 1) * span, :]
                out[n, r, at, :] = v.astype(jnp.bfloat16)
        return carry

    lax.fori_loop(0, tiles - 2, unpack, 0)
    for e in range(1, group):
        w_copy(e).wait_recv()
    w_piece[...] = jnp.sum(w_recv[...].astype(jnp.float32), axis=0).astype(jnp.bfloat16)
    for e in range(1, group):
        f_copy(e).start()
    w_full[rank] = w_piece[...]
    lax.fori_loop(tiles - 2, tiles, unpack, 0)

    def finish(j, carry):
        for d in range(1, tm):
            x_copy(j, d).wait_send()
            o_copy(j, d).wait_send()

        @pl.when(last)
        def _():
            for d in range(1, tm):
                g_copy(j, d).wait_send()

        return carry

    lax.fori_loop(0, tiles, finish, 0)

    @pl.when(section > 0)
    def _():
        def sent(k, carry):
            z_copy(k).wait_send()
            return carry

        lax.fori_loop(0, steps, sent, 0)

    for e in range(1, group):
        w_copy(e).wait_send()
    for e in range(1, group):
        f_copy(e).wait_recv()
    for k in range(group):
        ds[k * share : (k + 1) * share, :] = w_full[k].astype(jnp.float32)
    for t in range(12):
        half = ds[(t // 2) * chans : (t // 2 + 1) * chans, (t % 2) * chans : (t % 2 + 1) * chans]
        if t < 9:
            spatial[t] = half
        else:
            temporal[t - 9] = half
    for e in range(1, group):
        f_copy(e).wait_send()


def chain_plan(acts, cot, spatial_weight, temporal_weight):
    sections, tm, batches = [lax.axis_size(a) for a in ("section", "tm", "batch")]
    micro, local, rows, width = cot.shape
    chans = spatial_weight.shape[-1]
    group = tm * batches
    count = width // LANES
    tiles = count // TILE
    steps = -(-(count + sections) // (2 * STEP)) * 2
    pair = rows * tm
    piece = 6 * chans // group
    bf16, f32 = jnp.bfloat16, jnp.float32
    vmem, dma = pltpu.VMEM, pltpu.SemaphoreType.DMA
    return pl.pallas_call(
        functools.partial(chain_kernel, sections, batches),
        out_shape=[
            vmem((micro, rows, count * local, LANES), bf16),
            vmem((9, chans, chans), f32),
            vmem((3, chans, chans), f32),
        ],
        in_specs=[pl.BlockSpec(memory_space=pl.ANY)] * 4,
        out_specs=[pl.BlockSpec(memory_space=vmem)] * 3,
        scratch_shapes=[
            vmem((micro, rows, count * local, LANES), bf16),
            vmem((micro, rows, count * local, LANES), bf16),
            vmem((9, chans, chans), bf16),
            vmem((3, chans, chans), bf16),
        ]
        + [vmem((tiles, tm, TILE * rows, LANES), bf16)] * 4
        + [
            vmem(((max(steps * STEP, count + sections) + 2) * pair, LANES), f32),
            vmem(((steps * STEP + 1) * pair, LANES), f32),
            vmem(((tiles + 3) * TILE * pair, LANES), f32),
            vmem((steps, STEP * pair, 2 * LANES), bf16),
            vmem((steps, STEP * pair, LANES), bf16),
            vmem((steps, STEP * pair, LANES), f32),
            vmem((steps, STEP * pair, 3 * LANES), bf16),
            vmem((steps, STEP * pair, 3 * LANES), bf16),
            vmem((steps, STEP * pair, LANES), bf16),
            vmem((steps, STEP * pair, LANES), bf16),
            vmem((tiles, tm, TILE * rows, LANES), bf16),
            vmem((tiles, tm, TILE * rows, LANES), bf16),
            vmem((micro * rows * TILE * local + ROWS, LANES), f32),
            vmem((2 * LANES, 3 * LANES), bf16),
            vmem((3 * LANES, 2 * LANES), bf16),
            vmem((LANES, 3 * LANES), bf16),
            vmem((2 * LANES, 3 * LANES), f32),
            vmem((LANES, 3 * LANES), f32),
            vmem((6 * chans, LANES), f32),
            vmem((group, piece, LANES), bf16),
            vmem((group, piece, LANES), bf16),
            vmem((piece, LANES), bf16),
            vmem((group, piece, LANES), bf16),
            dma((4,)),
            dma((2, tiles, tm - 1)),
            dma((2, tiles, tm - 1)),
            dma((2, steps)),
            dma((2, tiles, tm - 1)),
            dma((2, group - 1)),
            dma((2, group - 1)),
        ],
        compiler_params=pltpu.CompilerParams(
            collective_id=0, has_side_effects=True, vmem_limit_bytes=56 * 2**20
        ),
    )(tiled(acts[0]), tiled(cot), spatial_weight[0], temporal_weight[0])


def hand_over(*refs):
    count = len(refs) // 2
    pieces = [(refs[0].at[n], refs[count].at[n]) for n in range(refs[0].shape[0])]
    pieces += [(refs[i], refs[count + i]) for i in range(1, count)]
    copies = [pltpu.make_async_copy(a, b, refs[-1].at[i]) for i, (a, b) in enumerate(pieces)]
    for c in copies:
        c.start()
    for c in copies:
        c.wait()


def settle(arrays):
    count = len(arrays)
    return pl.pallas_call(
        hand_over,
        out_shape=[jax.ShapeDtypeStruct(a.shape, a.dtype) for a in arrays],
        in_specs=[pl.BlockSpec(memory_space=pltpu.VMEM)] * count,
        out_specs=[pl.BlockSpec(memory_space=pl.ANY)] * count,
        scratch_shapes=[pltpu.SemaphoreType.DMA((arrays[0].shape[0] + count - 1,))],
    )(*[pltpu.with_memory_space_constraint(a, pltpu.VMEM) for a in arrays])


def body(acts, cot, spatial_weight, temporal_weight):
    tm, (micro, local, rows, width) = lax.axis_size("tm"), cot.shape
    one_chain_each = tm == micro * local and 2 * tm == ROWS
    whole = rows % 2 == 0 and width % (TILE * LANES) == 0 and TILE * local % 16 == 0 and TILE * rows % 16 == 0
    plan = chain_plan if one_chain_each and whole and local == DILATION else tile_plan
    grad, spatial, temporal = settle(plan(acts, cot, spatial_weight, temporal_weight))
    return untiled(grad, local)[None], spatial[None], temporal[None]


def solution(mesh):
    in_specs = (
        P("section", "batch", "tm", None, None),
        P("batch", "tm", None, None),
        P("section", None, None, None),
        P("section", None, None, None),
    )
    out_specs = (
        P("section", "batch", "tm", None, None),
        P("section", None, None, None),
        P("section", None, None, None),
    )
    return jax.shard_map(body, mesh=mesh, in_specs=in_specs, out_specs=out_specs, check_vma=False)
```

```python
import functools

import jax
import jax.numpy as jnp
from jax import lax
from jax.experimental import pallas as pl
from jax.experimental.pallas import tpu as pltpu
from jax.sharding import PartitionSpec as P

DILATION = 2
ROWS = 8
LANES = 128
HALO = 3
MESH = pl.DeviceIdType.MESH


def neighbours(x):
    none = jnp.zeros_like(x[:, :1])
    after = jnp.concatenate([x[:, 1:], none], axis=1)
    before = jnp.concatenate([none, x[:, :-1]], axis=1)
    lane = lax.broadcasted_iota(jnp.int32, x.shape, 3)
    return jnp.where(lane < LANES // 2, after, before)


def flat(x):
    return x.reshape(-1, x.shape[-1])


def mm(a, b, dims):
    return lax.dot_general(a, b, (dims, ((), ())), preferred_element_type=jnp.float32)


def taps_of(d, dt, chans):
    def block(a, r, i, b):
        at = i * LANES + b * chans
        return a[r * chans : (r + 1) * chans, at : at + chans]

    taps = []
    for i in range(3):
        taps.append(block(d, 0, i, 1) + block(d, 3, i, 0))
        taps.append(block(d, 0, i, 0) + block(d, 1, i, 1))
        taps.append(block(d, 1, i, 0) + block(d, 2, i, 1))
    for k in range(3):
        taps.append(block(dt, 0, k, 0) + block(dt, 1, k, 1))
    return taps


def set_weights(ws_ref, wt_ref, fwd, back, time):
    chans = ws_ref.shape[-1]
    zero = jnp.zeros((chans, chans), jnp.bfloat16)
    for i in range(3):
        a, b, c = [ws_ref[3 * i + j] for j in range(3)]
        at = slice(i * LANES, (i + 1) * LANES)
        rows = [[b, a], [c, b], [zero, c], [a, zero]]
        fwd[:, at] = jnp.concatenate([jnp.concatenate(v, axis=1) for v in rows], axis=0)
        at = slice(i * 2 * LANES, (i + 1) * 2 * LANES)
        rows = [[b, a, zero, c], [c, b, a, zero]]
        back[:, at] = jnp.concatenate([jnp.concatenate(v, axis=1) for v in rows], axis=0)
        at = slice(i * LANES, (i + 1) * LANES)
        rows = [[wt_ref[i], zero], [zero, wt_ref[i]]]
        time[:, at] = jnp.concatenate([jnp.concatenate(v, axis=1) for v in rows], axis=0)


def pack(frames, stage, c, tiles, line, flatten, skip):
    tm, size = stage.shape[0], stage.shape[2]
    rows, count = frames.shape[1], frames.shape[2]
    local = stage.shape[1] // frames.shape[0]
    pairs = count // local
    flatten[...] = frames[c // local].astype(jnp.float32).reshape(flatten.shape)
    for r in range(rows):
        at = r * count + c % local
        line[pl.ds(HALO * rows + r, pairs, stride=rows), :] = flatten[pl.ds(at, pairs, stride=local), :]
    for m in range(tm):
        at = (tiles * m + skip) * rows
        stage[m, c] = line[at : at + size, :].astype(jnp.bfloat16)


def spread(packed, loose, wide, rows, first, count):
    loose[...] = packed.astype(jnp.float32)
    for n in range(loose.shape[0]):
        for p in range(count):
            wide[n, first + p, 0:rows, :] = loose[n, rows * p : rows * (p + 1), :]


def tile_kernel(
    sections, batches, tiles, acts, cot, ws_ref, wt_ref, out, spatial, temporal,
    x_stage, g_stage, x_buf, g_buf, r_buf, o_buf, home, fwd, back, time, acc, acc_t, ds,
    w_send, w_recv, w_piece, w_full,
    line, flatten, x_loose, g_loose, o_loose, x_wide, g_wide,
    x_sem, g_sem, z_sem, o_sem, w_sem, f_sem,
):
    tm = x_stage.shape[0]
    micro, frame_rows, count, _ = acts.shape
    chains = x_stage.shape[1]
    local = chains // micro
    width = count // local * LANES
    chans = ws_ref.shape[-1]
    pairs = x_wide.shape[1]
    tile_rows = o_buf.shape[2]
    group = tm * batches
    section, me, core = [lax.axis_index(a) for a in ("section", "tm", "batch")]
    rank = me * batches + core

    def member(e):
        other = lax.rem(rank + e, group)
        return other, (section, other // batches, lax.rem(other, batches))

    def peer(d):
        other = lax.rem(me + d, tm)
        return other, (section, other, core)

    barrier = pltpu.get_barrier_semaphore()
    for e in range(1, group):
        pl.semaphore_signal(barrier, inc=1, device_id=member(e)[1], device_id_type=MESH)

    @pl.when(section > 0)
    def _():
        pl.semaphore_signal(barrier, inc=1, device_id=(section - 1, me, core), device_id_type=MESH)

    @pl.when(section < sections - 1)
    def _():
        pl.semaphore_signal(barrier, inc=1, device_id=(section + 1, me, core), device_id_type=MESH)

    def copy(src, dst, sems, at, device):
        return pltpu.make_async_remote_copy(
            src_ref=src, dst_ref=dst, send_sem=sems.at[(0,) + at], recv_sem=sems.at[(1,) + at],
            device_id=device, device_id_type=MESH,
        )

    def x_copy(c, d):
        other, device = peer(d)
        return copy(x_stage.at[other, c], x_buf.at[c, me], x_sem, (c, d - 1), device)

    def g_copy(c, d):
        other, device = peer(d)
        return copy(g_stage.at[other, c], g_buf.at[c, me], g_sem, (c, d - 1), device)

    def z_copy(c):
        return copy(r_buf.at[c], g_buf.at[c], z_sem, (c,), (lax.max(section - 1, 0), me, core))

    def o_copy(c, d):
        other, device = peer(d)
        return copy(o_buf.at[c, other], home.at[c, me], o_sem, (c, d - 1), device)

    def w_copy(e):
        other, device = member(e)
        return copy(w_send.at[other], w_recv.at[rank], w_sem, (e - 1,), device)

    def f_copy(e):
        return copy(w_piece, w_full.at[rank], f_sem, (e - 1,), member(e)[1])

    line[...] = jnp.zeros_like(line)
    x_wide[...] = jnp.zeros_like(x_wide)
    g_wide[...] = jnp.zeros_like(g_wide)
    g_loose[...] = jnp.zeros_like(g_loose)
    pack(acts, x_stage, 0, tiles, line, flatten, 0)

    @pl.when(section == sections - 1)
    def _():
        pack(cot, g_stage, 0, tiles, line, flatten, 1)

    more = (section > 0).astype(jnp.int32) + (section < sections - 1).astype(jnp.int32)
    pl.semaphore_wait(barrier, group - 1 + more)

    def send(c):
        if c > 0:
            pack(acts, x_stage, c, tiles, line, flatten, 0)

            @pl.when(section == sections - 1)
            def _():
                pack(cot, g_stage, c, tiles, line, flatten, 1)

        for d in range(1, tm):
            x_copy(c, d).start()
        x_buf[c, me] = x_stage[me, c]

        @pl.when(section == sections - 1)
        def _():
            for d in range(1, tm):
                g_copy(c, d).start()
            g_buf[c, me] = g_stage[me, c]

    for c in range(chains):
        send(c)
    set_weights(ws_ref, wt_ref, fwd, back, time)
    acc[...] = jnp.zeros_like(acc)
    acc_t[...] = jnp.zeros_like(acc_t)

    shape = (tm, pairs, ROWS, LANES)
    blank = jnp.zeros((1, pairs, ROWS, LANES), jnp.float32)
    centre = slice(HALO, HALO + tiles)

    def turn(c, carry):
        for d in range(1, tm):
            x_copy(c, d).wait_recv()
        spread(x_buf[c], x_loose, x_wide, frame_rows, 0, pairs)
        x = x_wide[...]
        xx = jnp.concatenate([x, neighbours(x)], axis=3)
        y = mm(flat(xx).astype(jnp.bfloat16), fwd[...], ((1,), (0,)))
        part = [y[:, LANES * i : LANES * (i + 1)].reshape(-1, ROWS, LANES) for i in range(3)]
        z = part[1] + pltpu.roll(part[0], 1, 1) + pltpu.roll(part[2], ROWS - 1, 1)
        z = z.reshape(shape)
        sig = jax.nn.sigmoid(z)
        h = z * sig
        slope = sig * (1.0 + z * (1.0 - sig))

        @pl.when(section == sections - 1)
        def _():
            for d in range(1, tm):
                g_copy(c, d).wait_recv()

        @pl.when(section < sections - 1)
        def _():
            z_copy(c).wait_recv()

        spread(g_buf[c], g_loose, g_wide, frame_rows, 1, pairs - 2)
        g = g_wide[...]
        g3 = jnp.concatenate(
            [
                jnp.concatenate([g[1:], blank], axis=0),
                g,
                jnp.concatenate([blank, g[:-1]], axis=0),
            ],
            axis=3,
        )
        gh = mm(flat(g3).astype(jnp.bfloat16), time[...], ((1,), (1,))).astype(jnp.bfloat16)
        gz = (gh.astype(jnp.float32).reshape(shape) * slope).astype(jnp.bfloat16)
        gz = gz.astype(jnp.float32)
        flat_gz = gz.reshape(-1, ROWS, LANES)
        gg = [
            pltpu.roll(flat_gz, ROWS - 1, 1).reshape(shape),
            gz,
            pltpu.roll(flat_gz, 1, 1).reshape(shape),
        ]
        sides = []
        for v in gg:
            sides += [v, neighbours(v)]
        sides = jnp.concatenate(sides, axis=3).astype(jnp.bfloat16)
        inner = mm(flat(sides), back[...], ((1,), (1,))).reshape(shape)
        place = me * tiles - HALO + lax.broadcasted_iota(jnp.int32, shape, 1)
        row = lax.broadcasted_iota(jnp.int32, shape, 2)
        inside = (place >= 0) & (place < width // LANES) & (row < frame_rows)
        result = jnp.where(inside, g + inner, 0.0)
        for n in range(tm):
            for p in range(pairs - 2):
                at = frame_rows * p
                g_loose[n, at : at + frame_rows, :] = result[n, p + 1, 0:frame_rows]
        r_buf[c] = g_loose[...].astype(jnp.bfloat16)

        @pl.when(section > 0)
        def _():
            z_copy(c).start()

        at = (HALO - 1) * frame_rows
        o_buf[c] = g_loose[:, at : at + tile_rows, :].astype(jnp.bfloat16)
        for d in range(1, tm):
            o_copy(c, d).start()
        home[c, me] = o_buf[c, me]
        hc = flat(h[:, centre]).astype(jnp.bfloat16)
        acc_t[...] += mm(hc, flat(g3[:, centre]).astype(jnp.bfloat16), ((0,), (0,)))
        gc = jnp.concatenate([v[:, centre] for v in gg], axis=3).astype(jnp.bfloat16)
        acc[...] += mm(flat(xx[:, centre]).astype(jnp.bfloat16), flat(gc), ((0,), (0,)))
        return carry

    lax.fori_loop(0, chains, turn, 0)

    taps = taps_of(acc[...], acc_t[...], chans)
    for k in range(6):
        ds[k * chans : (k + 1) * chans, :] = jnp.concatenate([taps[2 * k], taps[2 * k + 1]], axis=1)
    rows = w_send.shape[1]
    for k in range(group):
        w_send[k] = ds[k * rows : (k + 1) * rows, :].astype(jnp.bfloat16)
    for e in range(1, group):
        w_copy(e).start()
    w_recv[rank] = w_send[rank]

    def unpack(c):
        for d in range(1, tm):
            o_copy(c, d).wait_recv()
        o_loose[...] = home[c].astype(jnp.float32)
        for m in range(tm):
            for r in range(frame_rows):
                at = r * count + m * tiles * local + c % local
                flatten[pl.ds(at, tiles, stride=local), :] = o_loose[m, pl.ds(r, tiles, stride=frame_rows), :]
        if c % local == local - 1:
            out[c // local] = flatten[...].astype(jnp.bfloat16).reshape(frame_rows, count, LANES)

    for c in range(chains - 1):
        unpack(c)
    for e in range(1, group):
        w_copy(e).wait_recv()
    w_piece[...] = jnp.sum(w_recv[...].astype(jnp.float32), axis=0)
    for e in range(1, group):
        f_copy(e).start()
    w_full[rank] = w_piece[...]
    unpack(chains - 1)

    for e in range(1, group):
        f_copy(e).wait_recv()
    for k in range(group):
        ds[k * rows : (k + 1) * rows, :] = w_full[k]
    for t in range(12):
        both = ds[(t // 2) * chans : (t // 2 + 1) * chans, :]
        half = both[:, (t % 2) * chans : (t % 2 + 1) * chans]
        if t < 9:
            spatial[t] = half
        else:
            temporal[t - 9] = half

    def finish(c, carry):
        for d in range(1, tm):
            x_copy(c, d).wait_send()
            o_copy(c, d).wait_send()

        @pl.when(section == sections - 1)
        def _():
            for d in range(1, tm):
                g_copy(c, d).wait_send()

        @pl.when(section > 0)
        def _():
            z_copy(c).wait_send()

        return carry

    lax.fori_loop(0, chains, finish, 0)
    for e in range(1, group):
        w_copy(e).wait_send()
        f_copy(e).wait_send()


def tiled(a):
    micro, local, rows, width = a.shape
    a = a.reshape(micro, local, rows, width // LANES, LANES)
    return a.transpose(0, 2, 3, 1, 4).reshape(micro, rows, width // LANES * local, LANES)


def untiled(a, local):
    micro, rows, count, _ = a.shape
    a = a.reshape(micro, rows, count // local, local, LANES)
    return a.transpose(0, 3, 1, 2, 4).reshape(micro, local, rows, count // local * LANES)


def tile_plan(acts, cot, spatial_weight, temporal_weight):
    sections, tm, batches = [lax.axis_size(a) for a in ("section", "tm", "batch")]
    micro, local, rows, width = cot.shape
    chans = spatial_weight.shape[-1]
    chains = micro * local
    group = tm * batches
    tiles = width // LANES // tm
    pairs = tiles + 2 * HALO
    pairs += pairs % 2
    x_rows, g_rows, tile_rows = [-(-n * rows // 16) * 16 for n in (pairs, pairs - 2, tiles)]
    piece = 6 * chans // group
    bf16, f32 = jnp.bfloat16, jnp.float32
    vmem, dma = pltpu.VMEM, pltpu.SemaphoreType.DMA
    grad, spatial, temporal = pl.pallas_call(
        functools.partial(tile_kernel, sections, batches, tiles),
        out_shape=[
            jax.ShapeDtypeStruct((micro, rows, width // LANES * local, LANES), bf16),
            jax.ShapeDtypeStruct((9, chans, chans), f32),
            jax.ShapeDtypeStruct((3, chans, chans), f32),
        ],
        in_specs=[pl.BlockSpec(memory_space=vmem)] * 4,
        out_specs=[pl.BlockSpec(memory_space=vmem)] * 3,
        scratch_shapes=[
            vmem((tm, chains, x_rows, LANES), bf16),
            vmem((tm, chains, g_rows, LANES), bf16),
            vmem((chains, tm, x_rows, LANES), bf16),
            vmem((chains, tm, g_rows, LANES), bf16),
            vmem((chains, tm, g_rows, LANES), bf16),
            vmem((chains, tm, tile_rows, LANES), bf16),
            vmem((chains, tm, tile_rows, LANES), bf16),
            vmem((2 * LANES, 3 * LANES), bf16),
            vmem((LANES, 6 * LANES), bf16),
            vmem((LANES, 3 * LANES), bf16),
            vmem((2 * LANES, 3 * LANES), f32),
            vmem((LANES, 3 * LANES), f32),
            vmem((6 * chans, LANES), f32),
            vmem((group, piece, LANES), bf16),
            vmem((group, piece, LANES), bf16),
            vmem((piece, LANES), f32),
            vmem((group, piece, LANES), f32),
            vmem(((width // LANES + HALO + pairs) * rows + 16, LANES), f32),
            vmem((rows * width // LANES * local, LANES), f32),
            vmem((tm, x_rows, LANES), f32),
            vmem((tm, g_rows, LANES), f32),
            vmem((tm, tile_rows, LANES), f32),
            vmem((tm, pairs, ROWS, LANES), f32),
            vmem((tm, pairs, ROWS, LANES), f32),
            dma((2, chains, tm - 1)),
            dma((2, chains, tm - 1)),
            dma((2, chains)),
            dma((2, chains, tm - 1)),
            dma((2, group - 1)),
            dma((2, group - 1)),
        ],
        compiler_params=pltpu.CompilerParams(
            collective_id=0, has_side_effects=True, vmem_limit_bytes=56 * 2**20
        ),
    )(tiled(acts[0]), tiled(cot), spatial_weight[0], temporal_weight[0])
    return grad, spatial, temporal

STEP = 6
TILE = 8
EARLY = 4


def row_before(v):
    sub = lax.broadcasted_iota(jnp.int32, v[:, :1].shape, 2)
    first = jnp.where(sub >= ROWS // 2, pltpu.roll(v[:, -1:], ROWS // 2, 2), 0.0)
    return jnp.concatenate([first, v[:, :-1]], axis=1)


def row_after(v):
    sub = lax.broadcasted_iota(jnp.int32, v[:, :1].shape, 2)
    last = jnp.where(sub < ROWS // 2, pltpu.roll(v[:, :1], ROWS // 2, 2), 0.0)
    return jnp.concatenate([v[:, 1:], last], axis=1)


def beside(v):
    count = v.shape[0] - 2
    lane = lax.broadcasted_iota(jnp.int32, (count,) + v.shape[1:], 3)
    return jnp.where(lane < LANES // 2, v[2:], v[:-2])


def lanes(parts):
    return jnp.concatenate([flat(v).astype(jnp.bfloat16) for v in parts], axis=1)


def wide_weights(ws_ref, wt_ref, fwd, back, time):
    chans = ws_ref.shape[-1]
    zero = jnp.zeros((chans, chans), jnp.bfloat16)

    def grid(rows):
        return jnp.concatenate([jnp.concatenate(v, axis=1) for v in rows], axis=0)

    for i in range(3):
        a, b, c = [ws_ref[3 * i + j] for j in range(3)]
        at = slice(i * LANES, (i + 1) * LANES)
        fwd[:, at] = grid([[b, a], [c, b], [zero, c], [a, zero]])
        back[at, :] = grid([[b, a, zero, c], [c, b, a, zero]])
        time[:, at] = grid([[wt_ref[i], zero], [zero, wt_ref[i]]])


def folded(d, dt, chans):
    low = lax.broadcasted_iota(jnp.int32, (chans, LANES), 1) < chans

    def both(ref, i, a, b):
        at = slice(i * LANES, (i + 1) * LANES)
        v = jnp.where(low, ref[a * chans : (a + 1) * chans, at], ref[b * chans : (b + 1) * chans, at])
        return v + pltpu.roll(v, chans, 1)

    taps = [both(d, i, *rows) for i in range(3) for rows in ((3, 0), (0, 1), (1, 2))]
    return taps + [both(dt, k, 0, 1) for k in range(3)]


def chain_kernel(
    sections, batches, acts_hbm, cot_hbm, ws_hbm, wt_hbm, out, spatial, temporal,
    acts, cot, ws, wt, x_stage, g_stage, x_in, g_in, xw, gw, res, xs, hs, slopes, gs, ggs, g_buf, r_buf, o_stage, o_in,
    loose, fwd, back, time, acc, acc_t, ds, w_send, w_recv, w_piece, w_full,
    l_sem, x_sem, g_sem, z_sem, o_sem, w_sem, f_sem,
):
    micro, rows, count, _ = acts.shape
    tiles, tm = x_in.shape[:2]
    local = tm // micro
    steps = g_buf.shape[0]
    chans = ws.shape[-1]
    pair = rows * tm
    size = STEP * pair
    group = tm * batches
    section, me, core = [lax.axis_index(a) for a in ("section", "tm", "batch")]
    last = section == sections - 1
    busy = section >= sections - 2
    early = jnp.where(last, 1, jnp.where(busy, min(EARLY, steps), steps))
    lag = sections - 1 - section
    rank = me * batches + core

    def member(e):
        other = lax.rem(rank + e, group)
        return other, (section, other // batches, lax.rem(other, batches))

    def peer(d):
        other = tm - 1 - me if d == 1 else lax.rem(me + tm // 2, tm) if d == 2 else me + 1 - 2 * lax.rem(me, 2)
        return other, (section, other, core)

    barrier = pltpu.get_barrier_semaphore()
    for e in range(1, group):
        pl.semaphore_signal(barrier, inc=1, device_id=member(e)[1], device_id_type=MESH)

    @pl.when(section > 0)
    def _():
        pl.semaphore_signal(barrier, inc=1, device_id=(section - 1, me, core), device_id_type=MESH)

    @pl.when(section < sections - 1)
    def _():
        pl.semaphore_signal(barrier, inc=1, device_id=(section + 1, me, core), device_id_type=MESH)

    loads = [
        pltpu.make_async_copy(a, b, l_sem.at[i])
        for i, (a, b) in enumerate([(acts_hbm, acts), (cot_hbm, cot), (ws_hbm, ws), (wt_hbm, wt)])
    ]
    loads[0].start()

    @pl.when(last)
    def _():
        loads[1].start()

    loads[2].start()
    loads[3].start()

    def copy(src, dst, sems, at, device):
        return pltpu.make_async_remote_copy(
            src_ref=src, dst_ref=dst, send_sem=sems.at[(0,) + at], recv_sem=sems.at[(1,) + at],
            device_id=device, device_id_type=MESH,
        )

    def x_copy(j, d):
        other, device = peer(d)
        return copy(x_stage.at[j, other], x_in.at[j, me], x_sem, (j, d - 1), device)

    def g_copy(j, d):
        other = peer(d)[0]
        return copy(g_stage.at[j, other], g_in.at[j, me], g_sem, (j, d - 1), (section, other, core))

    def z_copy(k):
        return copy(r_buf.at[k], g_buf.at[k], z_sem, (k,), (lax.max(section - 1, 0), me, core))

    def o_copy(j, d):
        other, device = peer(d)
        return copy(o_stage.at[j, other], o_in.at[j, me], o_sem, (j, d - 1), device)

    def w_copy(e):
        other, device = member(e)
        return copy(w_send.at[other], w_recv.at[rank], w_sem, (e - 1,), device)

    def f_copy(e):
        return copy(w_piece, w_full.at[rank], f_sem, (e - 1,), member(e)[1])

    def sub_of(r):
        return r % (rows // 2) * ROWS + r // (rows // 2) * tm

    span = TILE * local

    def pack(frames, stage, j):
        at = pl.ds(pl.multiple_of(span * j, span), span)
        for n in range(micro):
            for r in range(rows):
                loose[(n * rows + r) * span : (n * rows + r + 1) * span, :] = frames[n, r, at, :].astype(jnp.float32)
        for n in range(micro):
            for t in range(local):
                cut = [loose[pl.ds((n * rows + r) * span + t, TILE, stride=local), :] for r in range(rows)]
                stage[j, n * local + t] = jnp.concatenate(cut, axis=0).astype(jnp.bfloat16)

    def send(j, carry):
        @pl.when(last)
        def _():
            pack(cot, g_stage, j)
            for d in range(1, tm):
                g_copy(j, d).start()
            g_in[j, me] = g_stage[j, me]

        pack(acts, x_stage, j)
        for d in range(1, tm):
            x_copy(j, d).start()
        x_in[j, me] = x_stage[j, me]
        return carry

    more = (section > 0).astype(jnp.int32) + (section < sections - 1).astype(jnp.int32)
    pl.semaphore_wait(barrier, group - 1 + more)

    @pl.when(last)
    def _():
        loads[1].wait()

    loads[0].wait()
    lax.fori_loop(0, tiles, send, 0)
    xw[...] = jnp.zeros_like(xw)
    gw[...] = jnp.zeros_like(gw)
    acc[...] = jnp.zeros_like(acc)
    acc_t[...] = jnp.zeros_like(acc_t)
    loads[2].wait()
    loads[3].wait()
    wide_weights(ws, wt, fwd, back, time)

    def spread(tile, wide, base):
        for m in range(tm):
            v = tile[m].astype(jnp.float32)
            for r in range(rows):
                at = base + (sub_of(r) + m)
                wide[pl.ds(at, TILE, stride=pair), :] = v[TILE * r : TILE * (r + 1)]

    def land(j, carry):
        for d in range(1, tm):
            x_copy(j, d).wait_recv()
        spread(x_in[j], xw, (j * TILE + 1 + lag) * pair)

        @pl.when(last)
        def _():
            for d in range(1, tm):
                g_copy(j, d).wait_recv()
            spread(g_in[j], gw, (j * TILE + 1) * pair)

        return carry

    def wanted(k):
        return jnp.where(k < 0, 0, lax.min((STEP * (k + 1) + TILE) // TILE, tiles))

    def ready(k):
        return lax.max((STEP * (k + 1) + TILE - sections) // TILE - 1, 0)

    shape = (STEP, rows // 2, ROWS, LANES)
    sub = lax.broadcasted_iota(jnp.int32, shape, 2)
    bin_at = sub % tm

    def window(ref, first, many):
        at = pl.multiple_of(first * pair, ROWS)
        return ref[pl.ds(at, many * pair), :].reshape((many,) + shape[1:])

    def give(j, carry):
        third = rows // 2 * TILE
        for m in range(tm):
            at = [pl.multiple_of((j + 1) * TILE * pair + (a * tm + m) * third, TILE) for a in range(2)]
            cut = [res[pl.ds(i, third), :] for i in at]
            o_stage[j, m] = jnp.concatenate(cut, axis=0).astype(jnp.bfloat16)
        for d in range(1, tm):
            o_copy(j, d).start()
        o_in[j, me] = o_stage[j, me]
        return carry

    def ahead(k, carry):
        lax.fori_loop(wanted(k - 1), wanted(k), land, 0)
        x = window(xw, STEP * k, STEP + 2)
        xx = lanes([x[1:-1], beside(x)])
        y = mm(xx, fwd[...], ((1,), (0,)))
        part = [y[:, LANES * i : LANES * (i + 1)].reshape(shape) for i in range(3)]
        z = part[1] + row_before(part[0]) + row_after(part[2])
        sig = jax.nn.sigmoid(z)
        h = z * sig
        xs[k] = xx
        hs[k] = flat(h).astype(jnp.bfloat16)
        slopes[k] = flat(sig * (1.0 + z * (1.0 - sig)))
        return carry

    def grads(i, carry):
        two = pl.ds(2 * i, 2)
        acc_t[...] += mm(flat(hs[two]), flat(gs[two]), ((0,), (0,)))
        acc[...] += mm(flat(xs[two]), flat(ggs[two]), ((0,), (0,)))
        return carry

    def turn(k, tail):
        @pl.when(section < sections - 1)
        def _():
            z_copy(k).wait_recv()
            at = pl.multiple_of((STEP * k + 1) * pair, ROWS)
            gw[pl.ds(at, size), :] = g_buf[k].astype(jnp.float32)

        held = window(gw, STEP * k, STEP + 1)
        g = held[1:]
        after = jnp.where(bin_at < tm - 1, pltpu.roll(g, ROWS - 1, 2), 0.0)
        before = jnp.where(bin_at > 0, pltpu.roll(g, 1, 2), 0.0)
        g3 = lanes([after, g, before])
        gh = mm(g3, time[...], ((1,), (1,))).astype(jnp.bfloat16)
        gz = (gh.astype(jnp.float32) * slopes[k]).reshape(shape).astype(jnp.bfloat16)
        gz = gz.astype(jnp.float32)
        sent = jnp.concatenate([tail, gz], axis=0)
        y = mm(lanes([sent[1:-1], beside(sent)]), back[...], ((1,), (1,)))
        part = [y[:, LANES * i : LANES * (i + 1)].reshape(shape) for i in range(3)]
        inner = part[1] + row_after(part[0]) + row_before(part[2])
        first = STEP * k - lag - 1
        place = first + lax.broadcasted_iota(jnp.int32, shape, 0)
        inside = (place >= 0) & (place < TILE * tiles)
        result = jnp.where(inside, held[:-1] + inner, 0.0)
        r_buf[k] = flat(result).astype(jnp.bfloat16)

        @pl.when(section > 0)
        def _():
            z_copy(k).start()

        for i in range(STEP):
            q = first + TILE + i
            at = q // TILE * (TILE * pair) + q % TILE
            for b in range(rows // 2):
                res[pl.ds(at + b * TILE, ROWS, stride=rows // 2 * TILE), :] = result[i, b]

        lax.fori_loop(ready(k - 1), ready(k), give, 0)
        gs[k] = g3
        ggs[k] = lanes([row_after(gz), gz, row_before(gz)])

        @pl.when(busy & (k + early < steps))
        def _():
            ahead(k + early, 0)

        @pl.when(~busy & (k % 2 == 1))
        def _():
            grads(k // 2, 0)

        return gz[-2:]

    lax.fori_loop(0, early, ahead, 0)
    lax.fori_loop(0, steps, turn, jnp.zeros((2,) + shape[1:], jnp.float32))

    @pl.when(busy)
    def _():
        lax.fori_loop(0, steps // 2, grads, 0)

    taps = folded(acc, acc_t, chans)
    low = lax.broadcasted_iota(jnp.int32, taps[0].shape, 1) < chans
    for k in range(6):
        ds[k * chans : (k + 1) * chans, :] = jnp.where(low, taps[2 * k], taps[2 * k + 1])
    share = w_send.shape[1]
    for k in range(group):
        w_send[k] = ds[k * share : (k + 1) * share, :].astype(jnp.bfloat16)
    for e in range(1, group):
        w_copy(e).start()
    w_recv[rank] = w_send[rank]

    def unpack(j, carry):
        for d in range(1, tm):
            o_copy(j, d).wait_recv()
        for c in range(tm):
            v = o_in[j, c].astype(jnp.float32)
            for r in range(rows):
                at = (c // local * rows + r) * span + c % local
                loose[pl.ds(at, TILE, stride=local), :] = v[TILE * r : TILE * (r + 1)]
        at = pl.ds(pl.multiple_of(span * j, span), span)
        for n in range(micro):
            for r in range(rows):
                v = loose[(n * rows + r) * span : (n * rows + r + 1) * span, :]
                out[n, r, at, :] = v.astype(jnp.bfloat16)
        return carry

    lax.fori_loop(0, tiles - 2, unpack, 0)
    for e in range(1, group):
        w_copy(e).wait_recv()
    w_piece[...] = jnp.sum(w_recv[...].astype(jnp.float32), axis=0).astype(jnp.bfloat16)
    for e in range(1, group):
        f_copy(e).start()
    w_full[rank] = w_piece[...]
    lax.fori_loop(tiles - 2, tiles, unpack, 0)

    def finish(j, carry):
        for d in range(1, tm):
            x_copy(j, d).wait_send()
            o_copy(j, d).wait_send()

        @pl.when(last)
        def _():
            for d in range(1, tm):
                g_copy(j, d).wait_send()

        return carry

    lax.fori_loop(0, tiles, finish, 0)

    @pl.when(section > 0)
    def _():
        def sent(k, carry):
            z_copy(k).wait_send()
            return carry

        lax.fori_loop(0, steps, sent, 0)

    for e in range(1, group):
        w_copy(e).wait_send()
    for e in range(1, group):
        f_copy(e).wait_recv()
    for k in range(group):
        ds[k * share : (k + 1) * share, :] = w_full[k].astype(jnp.float32)
    for t in range(12):
        half = ds[(t // 2) * chans : (t // 2 + 1) * chans, (t % 2) * chans : (t % 2 + 1) * chans]
        if t < 9:
            spatial[t] = half
        else:
            temporal[t - 9] = half
    for e in range(1, group):
        f_copy(e).wait_send()


def chain_plan(acts, cot, spatial_weight, temporal_weight):
    sections, tm, batches = [lax.axis_size(a) for a in ("section", "tm", "batch")]
    micro, local, rows, width = cot.shape
    chans = spatial_weight.shape[-1]
    group = tm * batches
    count = width // LANES
    tiles = count // TILE
    steps = -(-(count + sections) // (2 * STEP)) * 2
    pair = rows * tm
    piece = 6 * chans // group
    bf16, f32 = jnp.bfloat16, jnp.float32
    vmem, dma = pltpu.VMEM, pltpu.SemaphoreType.DMA
    return pl.pallas_call(
        functools.partial(chain_kernel, sections, batches),
        out_shape=[
            vmem((micro, rows, count * local, LANES), bf16),
            vmem((9, chans, chans), f32),
            vmem((3, chans, chans), f32),
        ],
        in_specs=[pl.BlockSpec(memory_space=pl.ANY)] * 4,
        out_specs=[pl.BlockSpec(memory_space=vmem)] * 3,
        scratch_shapes=[
            vmem((micro, rows, count * local, LANES), bf16),
            vmem((micro, rows, count * local, LANES), bf16),
            vmem((9, chans, chans), bf16),
            vmem((3, chans, chans), bf16),
        ]
        + [vmem((tiles, tm, TILE * rows, LANES), bf16)] * 4
        + [
            vmem(((max(steps * STEP, count + sections) + 2) * pair, LANES), f32),
            vmem(((steps * STEP + 1) * pair, LANES), f32),
            vmem(((tiles + 3) * TILE * pair, LANES), f32),
            vmem((steps, STEP * pair, 2 * LANES), bf16),
            vmem((steps, STEP * pair, LANES), bf16),
            vmem((steps, STEP * pair, LANES), f32),
            vmem((steps, STEP * pair, 3 * LANES), bf16),
            vmem((steps, STEP * pair, 3 * LANES), bf16),
            vmem((steps, STEP * pair, LANES), bf16),
            vmem((steps, STEP * pair, LANES), bf16),
            vmem((tiles, tm, TILE * rows, LANES), bf16),
            vmem((tiles, tm, TILE * rows, LANES), bf16),
            vmem((micro * rows * TILE * local + ROWS, LANES), f32),
            vmem((2 * LANES, 3 * LANES), bf16),
            vmem((3 * LANES, 2 * LANES), bf16),
            vmem((LANES, 3 * LANES), bf16),
            vmem((2 * LANES, 3 * LANES), f32),
            vmem((LANES, 3 * LANES), f32),
            vmem((6 * chans, LANES), f32),
            vmem((group, piece, LANES), bf16),
            vmem((group, piece, LANES), bf16),
            vmem((piece, LANES), bf16),
            vmem((group, piece, LANES), bf16),
            dma((4,)),
            dma((2, tiles, tm - 1)),
            dma((2, tiles, tm - 1)),
            dma((2, steps)),
            dma((2, tiles, tm - 1)),
            dma((2, group - 1)),
            dma((2, group - 1)),
        ],
        compiler_params=pltpu.CompilerParams(
            collective_id=0, has_side_effects=True, vmem_limit_bytes=56 * 2**20
        ),
    )(tiled(acts[0]), tiled(cot), spatial_weight[0], temporal_weight[0])


def hand_over(*refs):
    count = len(refs) // 2
    pieces = [(refs[0].at[n], refs[count].at[n]) for n in range(refs[0].shape[0])]
    pieces += [(refs[i], refs[count + i]) for i in range(1, count)]
    copies = [pltpu.make_async_copy(a, b, refs[-1].at[i]) for i, (a, b) in enumerate(pieces)]
    for c in copies:
        c.start()
    for c in copies:
        c.wait()


def settle(arrays):
    count = len(arrays)
    return pl.pallas_call(
        hand_over,
        out_shape=[jax.ShapeDtypeStruct(a.shape, a.dtype) for a in arrays],
        in_specs=[pl.BlockSpec(memory_space=pltpu.VMEM)] * count,
        out_specs=[pl.BlockSpec(memory_space=pl.ANY)] * count,
        scratch_shapes=[pltpu.SemaphoreType.DMA((arrays[0].shape[0] + count - 1,))],
    )(*[pltpu.with_memory_space_constraint(a, pltpu.VMEM) for a in arrays])


def body(acts, cot, spatial_weight, temporal_weight):
    tm, (micro, local, rows, width) = lax.axis_size("tm"), cot.shape
    one_chain_each = tm == micro * local and 2 * tm == ROWS
    whole = rows % 2 == 0 and width % (TILE * LANES) == 0 and TILE * local % 16 == 0 and TILE * rows % 16 == 0
    plan = chain_plan if one_chain_each and whole and local == DILATION else tile_plan
    grad, spatial, temporal = settle(plan(acts, cot, spatial_weight, temporal_weight))
    return untiled(grad, local)[None], spatial[None], temporal[None]


def solution(mesh):
    in_specs = (
        P("section", "batch", "tm", None, None),
        P("batch", "tm", None, None),
        P("section", None, None, None),
        P("section", None, None, None),
    )
    out_specs = (
        P("section", "batch", "tm", None, None),
        P("section", None, None, None),
        P("section", None, None, None),
    )
    return jax.shard_map(body, mesh=mesh, in_specs=in_specs, out_specs=out_specs, check_vma=False)
```
